128 devices in a mesh: row: 32 (over z, x, core), col: 4 (over y).
Axes of the slice: x: 4, y: 4, z: 4, core: 2. Of those that a mesh axis runs over, the one named last changes fastest.
Arguments:
- front: float32 [8192, 8192], P('row', 'col'), as said below
- ancestor_front: float32 [8192, 8192], P('row', 'col'), may hold values from -6 to 6
- tile_map: int32 [32], replicated, may hold values from 0 to 31, as said below
Outputs:
- panel_factor: float32 [8192, 512], P('row')
- updated: float32 [8192, 8192], P('row', 'col')
The draws below stay inside these ranges and needn't reach their ends.
Inputs may be any that keep to these rules, and one draw needn't show every extreme that they name: front is symmetric and positive definite. Each tile column is named once; of the 8 tile columns j of one index of col, the numbers whose tile_map[j] lies in the block of each index of col differ from one another by at most one, so none exceeds 2.
All inputs are finite; a program needn't handle non-finite values.
Results may differ from the reference program's by a relative error of at most 0.0001.
Values sent between devices are 32-bit elements; how exact they have to be, the bound alone decides.
No kernel may reach another device: no remote copies, remote signals or barrier semaphores. Data moves between devices by JAX's collectives and lax.ppermute only.
A program may use at most 64 MiB of HBM per device.

```python
import jax
import jax.numpy as jnp
from jax import lax

PW = 256
PANELS = 2
NF = 8192
NT = 32
TILES_COL = 8


def draw_front(key, part):
    key = jax.random.fold_in(key, 11)
    first, second, third = jax.random.split(key, 3)
    across = jax.random.uniform(first, (NF,), jnp.float32)
    downward = jax.random.uniform(second, (NF,), jnp.float32)
    distance = jnp.abs(across[:, None] - across[None, :]) + jnp.abs(downward[:, None] - downward[None, :])
    coupling = jnp.exp(distance * jnp.float32(-10.0))
    nugget = jax.random.uniform(third, (NF,), jnp.float32, 0.5, 1.5)
    positions = jnp.arange(NF, dtype=jnp.int32)
    matrix = coupling + jnp.where(positions[:, None] == positions[None, :], nugget[None, :], jnp.float32(0.0))
    return matrix


def draw_tile_map(key, part):
    key = jax.random.fold_in(key, 23)
    first, second, third = jax.random.split(key, 3)
    columns = NT // TILES_COL
    tile_ids = jnp.arange(NT, dtype=jnp.int32)
    sources = tile_ids // TILES_COL
    within = jax.random.permutation(first, NT).astype(jnp.int32)
    before = (sources[None, :] == sources[:, None]) & (within[None, :] < within[:, None])
    shuffled = jnp.sum(before.astype(jnp.int32), axis=1).astype(jnp.int32)
    offsets = jax.random.permutation(second, columns).astype(jnp.int32)
    owners = (jnp.take(offsets, sources) + shuffled) % columns
    order_keys = owners * NT + jax.random.permutation(third, NT).astype(jnp.int32)
    lesser = order_keys[None, :] < order_keys[:, None]
    return jnp.sum(lesser.astype(jnp.int32), axis=1).astype(jnp.int32)


def level_of(own_key, extent, cuts, smallest, top_value):
    gain, own = 1.0, jax.random.fold_in(own_key, 6)
    for dim, parts in cuts:
        heights = jnp.exp(jax.random.uniform(jax.random.fold_in(own, dim), (parts,), jnp.float32, smallest / len(cuts), top_value / len(cuts)))
        gain = gain * jnp.repeat(heights, extent[dim] // parts).reshape([-1 if axis == dim else 1 for axis in range(len(extent))])
    return gain


def centred(rng, extent, scale, bound, cuts=(), kind=jnp.bfloat16):
    array = scale * jax.random.normal(rng, extent, jnp.float32)
    if cuts:
        array = array * level_of(rng, extent, cuts, -0.22, 0.18)
    return jnp.clip(array, -bound, bound).astype(kind)


def setup_inputs(seed: int = 0) -> dict:
    arg_keys = jax.random.split(jax.random.key(seed), 4)
    return {
        "front": draw_front(jax.random.fold_in(arg_keys[3], 71), 0),
        "ancestor_front": centred(arg_keys[1], (NF, NF), 1.0, 6.0, ((0, 32), (1, 4)), jnp.float32),
        "tile_map": draw_tile_map(jax.random.fold_in(arg_keys[3], 71), 0),
    }


def reference(front, ancestor_front, tile_map):
    current = front
    rows = jnp.arange(NF, dtype=jnp.int32)
    panels = []
    for panel in range(PANELS):
        lower = panel * PW
        upper = lower + PW
        factor = jnp.linalg.cholesky(current[lower:upper, lower:upper])
        inverse = jax.scipy.linalg.solve_triangular(factor, jnp.eye(PW, dtype=jnp.float32), lower=True)
        solved = lax.dot_general(current[:, lower:upper], inverse, (((1,), (1,)), ((), ())), precision=lax.Precision.HIGHEST)
        solved = jnp.where((rows >= lower)[:, None], solved, jnp.float32(0.0))
        panels.append(solved)
        trailing = jnp.where((rows >= upper)[:, None], solved, jnp.float32(0.0))
        current = current - lax.dot_general(trailing, trailing, (((1,), (1,)), ((), ())), precision=lax.Precision.HIGHEST)
    limit = PANELS * PW
    keep = (rows >= limit)[:, None] & (rows >= limit)[None, :]
    schur = jnp.where(keep, current, jnp.float32(0.0))
    targets = jnp.arange(NT, dtype=jnp.int32)
    match = tile_map[None, :] == targets[:, None]
    source = jnp.sum(jnp.where(match, targets[None, :], 0), axis=1).astype(jnp.int32)
    tiles = schur.reshape(NF, NT, PW)
    picked = jnp.take(tiles, source, axis=1).reshape(NF, NF)
    return (jnp.concatenate(panels, axis=1), ancestor_front + picked)
```

```python
import jax
import jax.numpy as jnp
from jax import lax
from jax.experimental import pallas as pl
from jax.experimental.pallas import tpu as pltpu
from jax.sharding import PartitionSpec as P

PW = 256
LEAD = 512
HALF = 128
STEP = 8
HIGHEST = lax.Precision.HIGHEST


def dot(a, b, ca, cb):
    return lax.dot_general(
        a, b, (((ca,), (cb,)), ((), ())), precision=HIGHEST, preferred_element_type=jnp.float32
    )


def inverse_factor_128(block):
    n = HALF
    lane = lax.broadcasted_iota(jnp.int32, (STEP, n), 1)
    sub = lax.broadcasted_iota(jnp.int32, (STEP, n), 0)
    lane_all = lax.broadcasted_iota(jnp.int32, (n, n), 1)
    work = block
    for start in range(0, n, STEP):
        end = start + STEP
        top = work[start:end, :]
        columns = [jnp.broadcast_to(top[:, start + i : start + i + 1], (STEP, n)) for i in range(STEP)]
        entry = [
            [jnp.broadcast_to(columns[i][j : j + 1, :], (STEP, n)) if i <= j else None for i in range(STEP)]
            for j in range(STEP)
        ]
        inside = (lane >= start) & (lane < end)
        top = jnp.where(inside, jnp.where(lane - start == sub, 1.0, 0.0), top)
        rows = [jnp.broadcast_to(top[j : j + 1, :], (STEP, n)) for j in range(STEP)]
        done = [None] * STEP
        for i in range(STEP):
            scale = lax.rsqrt(entry[i][i])
            done[i] = rows[i] * scale
            below = [None] * STEP
            for j in range(i + 1, STEP):
                below[j] = entry[j][i] * scale
                for k in range(i + 1, j + 1):
                    entry[j][k] = entry[j][k] - below[j] * below[k]
            for j in range(i + 1, STEP):
                rows[j] = rows[j] - below[j] * done[i]
        solved = done[0]
        for i in range(1, STEP):
            solved = jnp.where(sub == i, done[i], solved)
        work = jnp.where((lane_all >= start) & (lane_all < end), 0.0, work)
        pieces = [work[:start]] if start else []
        pieces.append(solved)
        if end < n:
            ahead = jnp.where(lane >= end, solved, 0.0)
            pieces.append(work[end:] - dot(ahead, solved, 0, 0)[end:])
        work = jnp.concatenate(pieces, 0)
    return work


def inverse_factor_256(block):
    first = inverse_factor_128(block[:HALF, :HALF])
    across = dot(block[HALF:, :HALF], first, 1, 1)
    second = inverse_factor_128(block[HALF:, HALF:] - dot(across, across, 1, 1))
    lower = -dot(second, dot(across, first, 1, 0), 1, 0)
    return jnp.concatenate(
        [
            jnp.concatenate([first, jnp.zeros_like(first)], 1),
            jnp.concatenate([lower, second], 1),
        ],
        0,
    )


def factor_kernel(where_ref, own_ref, other_ref, rows_ref, panel_ref, weight_ref):
    row_index, core = where_ref[0], where_ref[1]
    even = core == 0
    own, other = own_ref[...], other_ref[...]
    zero = jnp.where(even, own, other)
    one = jnp.where(even, other, own)
    corner = zero[:, :PW]
    below = one[:, :PW]
    last = jnp.concatenate([zero[:, PW:], one[:, PW:]], 1)
    inv_a = inverse_factor_256(corner)
    across = dot(below, inv_a, 1, 1)
    inv_b = inverse_factor_256(last - dot(across, across, 1, 1))
    rows = rows_ref[...]
    panel_a = dot(rows[:, :PW], inv_a, 1, 1)
    panel_b = dot(rows[:, PW:] - dot(panel_a, across, 1, 1), inv_b, 1, 1)
    weight_b = dot(panel_b, inv_b, 1, 0)
    weight_a = dot(panel_a - dot(weight_b, across, 1, 0), inv_a, 1, 0)
    panel_ref[:, :PW] = panel_a
    panel_ref[:, PW:] = jnp.where(row_index == 0, 0.0, panel_b)
    weight_ref[:, :PW] = weight_a
    weight_ref[:, PW:] = weight_b


def factor(where, own, other, rows):
    whole = pl.BlockSpec(memory_space=pltpu.VMEM)
    return pl.pallas_call(
        factor_kernel,
        out_shape=[jax.ShapeDtypeStruct((PW, LEAD), jnp.float32)] * 2,
        in_specs=[pl.BlockSpec(memory_space=pltpu.SMEM), whole, whole, whole],
        out_specs=[whole, whole],
        compiler_params=pltpu.CompilerParams(vmem_limit_bytes=40 << 20),
        name="factor",
    )(where, own, other, rows)


def pick_kernel(index_ref, front_ref, *refs):
    outs, sem = refs[:-1], refs[-1]
    copies = []
    for place in range(2 * len(outs)):
        start = pl.multiple_of(index_ref[place] * PW, PW)
        half = (place % 2) * PW
        copies.append(
            pltpu.make_async_copy(
                front_ref.at[:, pl.ds(start, PW)],
                outs[place // 2].at[:, pl.ds(half, PW)],
                sem.at[place],
            )
        )
    for copy in copies:
        copy.start()
    for copy in copies:
        copy.wait()


def pick(index, front):
    anywhere = pl.BlockSpec(memory_space=pl.ANY)
    return pl.pallas_call(
        pick_kernel,
        out_shape=[jax.ShapeDtypeStruct((front.shape[0], 2 * PW), jnp.float32)] * 4,
        in_specs=[pl.BlockSpec(memory_space=pltpu.SMEM), anywhere],
        out_specs=[anywhere] * 4,
        scratch_shapes=[pltpu.SemaphoreType.DMA((8,))],
        name="pick",
    )(index, front)


def update_kernel(shift, group, place, live, weight_ref, p0, p1, p2, p3, ahead_ref, base_ref, out_ref):
    slot = pl.program_id(0)
    ahead = ahead_ref[...].reshape(PW, LEAD)
    product = dot(weight_ref[...], ahead, 1, 1)
    column = pl.multiple_of(place[slot] * PW, PW)
    base = base_ref[...]
    out_ref[...] = base
    for index, ref in enumerate((p0, p1, p2, p3)):

        @pl.when((shift[slot] == index) & (live[slot] == 1))
        def _():
            out_ref[...] = base + (ref[:, pl.ds(column, PW)] - product)


def update(shift, group, place, live, weight, pieces, ahead, base):
    rows, cols = base.shape
    full = pl.BlockSpec((rows, 2 * PW), lambda u, *s: (0, 0))
    tile = pl.BlockSpec((rows, PW), lambda u, *s: (0, u))
    return pl.pallas_call(
        update_kernel,
        out_shape=jax.ShapeDtypeStruct(base.shape, jnp.float32),
        grid_spec=pltpu.PrefetchScalarGridSpec(
            num_scalar_prefetch=4,
            grid=(cols // PW,),
            in_specs=[
                full,
                full,
                full,
                full,
                full,
                pl.BlockSpec((8, 1, 32, LEAD), lambda u, shift, group, place, live: (group[u], place[u], 0, 0)),
                tile,
            ],
            out_specs=tile,
        ),
        compiler_params=pltpu.CompilerParams(vmem_limit_bytes=40 << 20),
        name="update",
    )(shift, group, place, live, weight, *pieces, ahead, base)


def device(z, x, core, y):
    return ((z * 4 + x) * 2 + core) * 4 + y


def spread_steps():
    orders = ("yxz", "xzy")
    have = [{(0, 0, 0)}, {(0, 0, 0)}]
    steps = []
    for step in range(6):
        pairs = []
        for core in range(2):
            axis = "zxy".index(orders[core][step // 2])
            new = set()
            for at in sorted(have[core]):
                to = list(at)
                if step % 2 == 0:
                    to[axis] = 1
                else:
                    to[axis] = 3 if at[axis] == 0 else 2
                new.add(tuple(to))
                pairs.append((device(at[0], at[1], core, at[2]), device(to[0], to[1], core, to[2])))
            have[core] |= new
        steps.append(pairs)
    return steps


def shards(front, ancestor, tile_map):
    row = lax.axis_index("row")
    col = lax.axis_index("col")
    core = row % 2
    line = (row // 2) % 4
    plane = row // 8
    swap = [(i, i ^ 1) for i in range(32)]

    owner = (tile_map // 8).reshape(4, 8)
    ids = jnp.arange(8, dtype=jnp.int32)
    same = owner[:, :, None] == owner[:, None, :]
    rank = jnp.sum(jnp.where(same & (ids[None, None, :] < ids[None, :, None]), 1, 0), axis=2)
    cols4 = jnp.arange(4, dtype=jnp.int32)
    hit = (owner[:, None, None, :] == cols4[None, :, None, None]) & (
        rank[:, None, None, :] == jnp.arange(2, dtype=jnp.int32)[None, None, :, None]
    )
    chosen = jnp.sum(jnp.where(hit, ids, 0), axis=3)
    slots = col * 8 + ids
    found = tile_map[None, :] == slots[:, None]
    all_ids = jnp.arange(32, dtype=jnp.int32)
    source = jnp.sum(jnp.where(found, all_ids, 0), axis=1)
    place = jnp.sum(jnp.where(found, rank.reshape(32), 0), axis=1)
    group = source // 8
    shift = (col - group) % 4
    live = jnp.where((source >= 2) & (row >= 2), 1, 0).astype(jnp.int32)

    lead = front[:, :LEAD]
    mate = lax.ppermute(lead, "row", swap)

    tail = jnp.where(core == 0, mate[:, PW : PW + HALF], lead[:, PW + HALF :])
    block = jnp.concatenate([lead[:, :PW], tail], axis=1)
    block = jnp.where((row < 2) & (col == 0), block, 0.0)
    for pairs in spread_steps():
        block = block + lax.ppermute(block, ("row", "col"), pairs)
    other = lax.ppermute(block, "row", swap)

    even = jnp.where(core == 0, lead, mate)
    odd = jnp.where(core == 0, mate, lead)
    both = jnp.stack([even, odd])
    parts = []
    for hop in range(4):
        at = 32 * (2 * ((line + hop) % 4) + core)
        part = lax.dynamic_slice(both, (0, at, 0), (2, 32, LEAD))
        if hop:
            pairs = [(z * 8 + x * 2 + k, z * 8 + (x + hop) % 4 * 2 + k) for z in range(4) for x in range(4) for k in range(2)]
            part = lax.ppermute(part, "row", pairs)
        parts.append(part)
    parts = jnp.concatenate(parts, 0)
    mine = lax.dynamic_index_in_dim(chosen, plane, 0, keepdims=False)
    index = ((line - mine // 2) % 4) * 2 + mine % 2
    sent = jnp.take(parts, index, axis=0)
    kept = jnp.where(col == 0, sent[0], 0.0)
    for to in range(1, 4):
        kept = kept + lax.ppermute(sent[to], "col", [(0, to)])
    ahead = lax.all_gather(kept, "row", axis=0, tiled=False)

    rows = jnp.where(col == 0, lead, 0.0)
    rows = rows + lax.ppermute(rows, "col", [(0, 1)])
    rows = rows + lax.ppermute(rows, "col", [(0, 3), (1, 2)])

    own = lax.dynamic_index_in_dim(chosen, col, 0, keepdims=False)
    order = jnp.take(own, (col + cols4) % 4, axis=0).reshape(8)
    pieces = list(pick(order, front))
    for hop in range(1, 4):
        pieces[hop] = lax.ppermute(pieces[hop], "col", [(i, (i + hop) % 4) for i in range(4)])

    panel, weight = factor(jnp.stack([row, core]), block, other, rows)
    updated = update(shift, group, place, live, weight, pieces, ahead, ancestor)
    return panel, updated


def solution(mesh):
    return jax.shard_map(
        shards,
        mesh=mesh,
        in_specs=(P("row", "col"), P("row", "col"), P()),
        out_specs=(P("row", None), P("row", "col")),
        check_vma=False,
    )
```

```python
import jax
import jax.numpy as jnp
from jax import lax
from jax.experimental import pallas as pl
from jax.experimental.pallas import tpu as pltpu
from jax.sharding import PartitionSpec as P

PW = 256
LEAD = 512
HALF = 128
STEP = 8
HIGHEST = lax.Precision.HIGHEST


def dot(a, b, ca, cb):
    return lax.dot_general(
        a, b, (((ca,), (cb,)), ((), ())), precision=HIGHEST, preferred_element_type=jnp.float32
    )


def inverse_factor_128(block):
    n = HALF
    lane = lax.broadcasted_iota(jnp.int32, (STEP, n), 1)
    sub = lax.broadcasted_iota(jnp.int32, (STEP, n), 0)
    lane_all = lax.broadcasted_iota(jnp.int32, (n, n), 1)
    work = block
    for start in range(0, n, STEP):
        end = start + STEP
        top = work[start:end, :]
        columns = [jnp.broadcast_to(top[:, start + i : start + i + 1], (STEP, n)) for i in range(STEP)]
        entry = [
            [jnp.broadcast_to(columns[i][j : j + 1, :], (STEP, n)) if i <= j else None for i in range(STEP)]
            for j in range(STEP)
        ]
        inside = (lane >= start) & (lane < end)
        top = jnp.where(inside, jnp.where(lane - start == sub, 1.0, 0.0), top)
        rows = [jnp.broadcast_to(top[j : j + 1, :], (STEP, n)) for j in range(STEP)]
        done = [None] * STEP
        for i in range(STEP):
            scale = lax.rsqrt(entry[i][i])
            done[i] = rows[i] * scale
            below = [None] * STEP
            for j in range(i + 1, STEP):
                below[j] = entry[j][i] * scale
                for k in range(i + 1, j + 1):
                    entry[j][k] = entry[j][k] - below[j] * below[k]
            for j in range(i + 1, STEP):
                rows[j] = rows[j] - below[j] * done[i]
        solved = done[0]
        for i in range(1, STEP):
            solved = jnp.where(sub == i, done[i], solved)
        work = jnp.where((lane_all >= start) & (lane_all < end), 0.0, work)
        pieces = [work[:start]] if start else []
        pieces.append(solved)
        if end < n:
            ahead = jnp.where(lane >= end, solved, 0.0)
            pieces.append(work[end:] - dot(ahead, solved, 0, 0)[end:])
        work = jnp.concatenate(pieces, 0)
    return work


def inverse_factor_256(top, left, bottom):
    first = inverse_factor_128(top)
    across = dot(left, first, 1, 1)
    second = inverse_factor_128(bottom - dot(across, across, 1, 1))
    lower = -dot(second, dot(across, first, 1, 0), 1, 0)
    return jnp.concatenate(
        [
            jnp.concatenate([first, jnp.zeros_like(first)], 1),
            jnp.concatenate([lower, second], 1),
        ],
        0,
    )


def factor_kernel(core_ref, own_ref, other_ref, inv_a_ref, across_ref, inv_b_ref):
    even = core_ref[0] == 0
    own, other = own_ref[...], other_ref[...]
    zero = jnp.where(even, own, other)
    one = jnp.where(even, other, own)

    def piece(blocks, index):
        return blocks[index * HALF : (index + 1) * HALF]

    inv_a = inverse_factor_256(piece(zero, 0), piece(zero, 1), piece(zero, 2))
    across = jnp.concatenate(
        [
            dot(jnp.concatenate([piece(zero, 3), piece(zero, 4)], 0), inv_a, 0, 1),
            dot(jnp.concatenate([piece(one, 3), piece(one, 4)], 1), inv_a, 1, 1),
        ],
        0,
    )
    square = dot(across, across, 1, 1)
    inv_b = inverse_factor_256(
        piece(one, 0) - square[:HALF, :HALF],
        piece(one, 1) - square[HALF:, :HALF],
        piece(one, 2) - square[HALF:, HALF:],
    )
    inv_a_ref[...] = inv_a
    across_ref[...] = across
    inv_b_ref[...] = inv_b


def factor(core, own, other):
    whole = pl.BlockSpec(memory_space=pltpu.VMEM)
    return pl.pallas_call(
        factor_kernel,
        out_shape=[jax.ShapeDtypeStruct((PW, PW), jnp.float32)] * 3,
        in_specs=[pl.BlockSpec(memory_space=pltpu.SMEM), whole, whole],
        out_specs=[whole] * 3,
        compiler_params=pltpu.CompilerParams(vmem_limit_bytes=24 << 20),
        name="factor",
    )(core, own, other)


def pick_kernel(index_ref, front_ref, *outs):
    for place in range(2 * len(outs)):
        start = pl.multiple_of(index_ref[place] * PW, PW)
        half = (place % 2) * PW
        outs[place // 2][:, half : half + PW] = front_ref[:, pl.ds(start, PW)]


def pick(index, front):
    whole = pl.BlockSpec(memory_space=pltpu.VMEM)
    return pl.pallas_call(
        pick_kernel,
        out_shape=[jax.ShapeDtypeStruct((front.shape[0], 2 * PW), jnp.float32)] * 4,
        in_specs=[pl.BlockSpec(memory_space=pltpu.SMEM), whole],
        out_specs=[whole] * 4,
        compiler_params=pltpu.CompilerParams(vmem_limit_bytes=16 << 20),
        name="pick",
    )(index, front)


def update_kernel(
    shift, group, place, live, at, r0, r1, r2, r3, inv_a_ref, across_ref, inv_b_ref, p0, p1, p2, p3, ahead_ref, base_ref,
    panel_ref, out_ref, weight_ref,
):
    slot = pl.program_id(0)

    @pl.when(slot == 0)
    def _():
        inv_a, across, inv_b = inv_a_ref[...], across_ref[...], inv_b_ref[...]
        rows_ref = jnp.where(at[1] == 0, r0[...], r1[...] + r2[...] + r3[...])
        panel_a = dot(rows_ref[:, :PW], inv_a, 1, 1)
        panel_b = dot(rows_ref[:, PW:] - dot(panel_a, across, 1, 1), inv_b, 1, 1)
        weight_b = dot(panel_b, inv_b, 1, 0)
        panel_ref[:, :PW] = panel_a
        panel_ref[:, PW:] = jnp.where(at[0] == 0, 0.0, panel_b)
        weight_ref[:, :PW] = dot(panel_a - dot(weight_b, across, 1, 0), inv_a, 1, 0)
        weight_ref[:, PW:] = weight_b

    product = dot(weight_ref[...], ahead_ref[...].reshape(PW, LEAD), 1, 1)
    column = pl.multiple_of(place[slot] * PW, PW)
    base = base_ref[...]
    out_ref[...] = base
    for index, ref in enumerate((p0, p1, p2, p3)):

        @pl.when((shift[slot] == index) & (live[slot] == 1))
        def _():
            out_ref[...] = base + (ref[:, pl.ds(column, PW)] - product)


def update(scalars, rows, inverse, pieces, ahead, base):
    height, width = base.shape
    full = pl.BlockSpec((height, LEAD), lambda u, *s: (0, 0))
    square = pl.BlockSpec((PW, PW), lambda u, *s: (0, 0))
    tile = pl.BlockSpec((height, PW), lambda u, *s: (0, u))
    return pl.pallas_call(
        update_kernel,
        out_shape=[
            jax.ShapeDtypeStruct((height, LEAD), jnp.float32),
            jax.ShapeDtypeStruct(base.shape, jnp.float32),
        ],
        grid_spec=pltpu.PrefetchScalarGridSpec(
            num_scalar_prefetch=5,
            grid=(width // PW,),
            in_specs=[
                *[full] * 4,
                *[square] * 3,
                *[full] * 4,
                pl.BlockSpec((8, 1, 32, LEAD), lambda u, shift, group, place, live, at: (group[u], place[u], 0, 0)),
                tile,
            ],
            out_specs=[full, tile],
            scratch_shapes=[pltpu.VMEM((height, LEAD), jnp.float32)],
        ),
        compiler_params=pltpu.CompilerParams(vmem_limit_bytes=56 << 20),
        name="update",
    )(*scalars, *rows, *inverse, *pieces, ahead, base)


def spread_steps():
    have = [{(0, 0)}, {(0, 0)}]
    steps = []
    for step in range(4):
        pairs = []
        for core in range(2):
            axis = (step // 2 + 1 - core) % 2
            new = set()
            for at in sorted(have[core]):
                to = list(at)
                if step % 2 == 0:
                    to[axis] = 1
                else:
                    to[axis] = 3 if at[axis] == 0 else 2
                new.add(tuple(to))
                pairs.append(((at[0] * 4 + at[1]) * 2 + core, (to[0] * 4 + to[1]) * 2 + core))
            have[core] |= new
        steps.append(pairs)
    return steps


def corner_blocks(rows, core):
    first = [rows[:HALF, :HALF], rows[HALF:, :HALF], rows[HALF:, HALF:PW], rows[:HALF, PW : PW + HALF], rows[HALF:, PW : PW + HALF]]
    second = [rows[:HALF, PW : PW + HALF], rows[HALF:, PW : PW + HALF], rows[HALF:, PW + HALF :], rows[HALF:, :HALF], rows[HALF:, HALF:PW]]
    return jnp.where(core == 0, jnp.concatenate(first, 0), jnp.concatenate(second, 0))


def shards(front, ancestor, tile_map):
    row = lax.axis_index("row")
    col = lax.axis_index("col")
    core = row % 2
    line = (row // 2) % 4
    plane = row // 8
    swap = [(i, i ^ 1) for i in range(32)]

    owner = (tile_map // 8).reshape(4, 8)
    ids = jnp.arange(8, dtype=jnp.int32)
    same = owner[:, :, None] == owner[:, None, :]
    rank = jnp.sum(jnp.where(same & (ids[None, None, :] < ids[None, :, None]), 1, 0), axis=2)
    cols4 = jnp.arange(4, dtype=jnp.int32)
    hit = (owner[:, None, None, :] == cols4[None, :, None, None]) & (
        rank[:, None, None, :] == jnp.arange(2, dtype=jnp.int32)[None, None, :, None]
    )
    chosen = jnp.sum(jnp.where(hit, ids, 0), axis=3)
    slots = col * 8 + ids
    found = tile_map[None, :] == slots[:, None]
    all_ids = jnp.arange(32, dtype=jnp.int32)
    source = jnp.sum(jnp.where(found, all_ids, 0), axis=1)
    place = jnp.sum(jnp.where(found, rank.reshape(32), 0), axis=1)
    group = source // 8
    shift = (col - group) % 4
    live = jnp.where((source >= 2) & (row >= 2), 1, 0).astype(jnp.int32)

    lead = front[:, :LEAD]
    copies = [lax.ppermute(lead, "col", [(0, to)]) for to in (1, 3, 2)]
    mate = lax.ppermute(lead, "row", swap)

    even = jnp.where(core == 0, lead, mate)
    odd = jnp.where(core == 0, mate, lead)
    both = jnp.stack([even, odd])
    parts = []
    for hop in range(4):
        at = 32 * (2 * ((line + hop) % 4) + core)
        parts.append(lax.dynamic_slice(both, (0, at, 0), (2, 32, LEAD)))
    parts = list(lax.optimization_barrier(tuple(parts)))
    for hop in range(1, 4):
        pairs = [(z * 8 + x * 2 + k, z * 8 + (x + hop) % 4 * 2 + k) for z in range(4) for x in range(4) for k in range(2)]
        parts[hop] = lax.ppermute(parts[hop], "row", pairs)

    own = lax.dynamic_index_in_dim(chosen, col, 0, keepdims=False)
    order = jnp.take(own, (col + cols4) % 4, axis=0).reshape(8)
    order, mate = lax.optimization_barrier((order, mate))
    pieces = list(pick(order, front))

    parts = jnp.concatenate(parts, 0)
    mine = lax.dynamic_index_in_dim(chosen, plane, 0, keepdims=False)
    index = ((line - mine // 2) % 4) * 2 + mine % 2
    sent = jnp.take(parts, index, axis=0)
    kept = jnp.where(col == 0, sent[0], 0.0)
    for to in range(1, 4):
        kept = kept + lax.ppermute(sent[to], "col", [(0, to)])
    copies[0], kept, *pieces = lax.optimization_barrier((copies[0], kept, *pieces))
    ahead = lax.all_gather(kept, "row", axis=0, tiled=False)

    rows = jnp.where(col == 0, lead, copies[0] + copies[1] + copies[2])
    block = jnp.where(row < 2, corner_blocks(rows, core), 0.0)
    for hop, pairs in enumerate(spread_steps()):
        if hop:
            pieces[hop] = lax.ppermute(pieces[hop], "col", [(i, (i + hop) % 4) for i in range(4)])
        block = block + lax.ppermute(block, "row", pairs)
        if hop < 3:
            block, pieces[hop + 1] = lax.optimization_barrier((block, pieces[hop + 1]))
    other = lax.ppermute(block, "row", swap)

    inverse = factor(core[None], block, other)
    panel, updated = update(
        (shift, group, place, live, jnp.stack([row, col])), [lead, *copies], inverse, pieces, ahead, ancestor
    )
    return panel, updated


def solution(mesh):
    return jax.shard_map(
        shards,
        mesh=mesh,
        in_specs=(P("row", "col"), P("row", "col"), P()),
        out_specs=(P("row", None), P("row", "col")),
        check_vma=False,
    )
```

```python
import jax
import jax.numpy as jnp
from jax import lax
from jax.experimental import pallas as pl
from jax.experimental.pallas import tpu as pltpu
from jax.sharding import PartitionSpec as P

PW = 256
LEAD = 512
HALF = 128
STEP = 8
HIGHEST = lax.Precision.HIGHEST


def dot(a, b, ca, cb):
    return lax.dot_general(
        a, b, (((ca,), (cb,)), ((), ())), precision=HIGHEST, preferred_element_type=jnp.float32
    )


def inverse_factor_128(block):
    n = HALF
    lane = lax.broadcasted_iota(jnp.int32, (STEP, n), 1)
    sub = lax.broadcasted_iota(jnp.int32, (STEP, n), 0)
    lane_all = lax.broadcasted_iota(jnp.int32, (n, n), 1)
    work = block
    for start in range(0, n, STEP):
        end = start + STEP
        top = work[start:end, :]
        columns = [jnp.broadcast_to(top[:, start + i : start + i + 1], (STEP, n)) for i in range(STEP)]
        entry = [
            [jnp.broadcast_to(columns[i][j : j + 1, :], (STEP, n)) if i <= j else None for i in range(STEP)]
            for j in range(STEP)
        ]
        inside = (lane >= start) & (lane < end)
        top = jnp.where(inside, jnp.where(lane - start == sub, 1.0, 0.0), top)
        rows = [jnp.broadcast_to(top[j : j + 1, :], (STEP, n)) for j in range(STEP)]
        done = [None] * STEP
        for i in range(STEP):
            scale = lax.rsqrt(entry[i][i])
            done[i] = rows[i] * scale
            below = [None] * STEP
            for j in range(i + 1, STEP):
                below[j] = entry[j][i] * scale
                for k in range(i + 1, j + 1):
                    entry[j][k] = entry[j][k] - below[j] * below[k]
            for j in range(i + 1, STEP):
                rows[j] = rows[j] - below[j] * done[i]
        solved = done[0]
        for i in range(1, STEP):
            solved = jnp.where(sub == i, done[i], solved)
        work = jnp.where((lane_all >= start) & (lane_all < end), 0.0, work)
        pieces = [work[:start]] if start else []
        pieces.append(solved)
        if end < n:
            ahead = jnp.where(lane >= end, solved, 0.0)
            pieces.append(work[end:] - dot(ahead, solved, 0, 0)[end:])
        work = jnp.concatenate(pieces, 0)
    return work


def inverse_factor_256(top, left, bottom):
    first = inverse_factor_128(top)
    across = dot(left, first, 1, 1)
    second = inverse_factor_128(bottom - dot(across, across, 1, 1))
    lower = -dot(second, dot(across, first, 1, 0), 1, 0)
    return jnp.concatenate(
        [
            jnp.concatenate([first, jnp.zeros_like(first)], 1),
            jnp.concatenate([lower, second], 1),
        ],
        0,
    )


def factor_kernel(core_ref, own_ref, other_ref, inv_a_ref, across_ref, inv_b_ref):
    even = core_ref[0] == 0
    own, other = own_ref[...], other_ref[...]
    zero = jnp.where(even, own, other)
    one = jnp.where(even, other, own)

    def piece(blocks, index):
        return blocks[index * HALF : (index + 1) * HALF]

    inv_a = inverse_factor_256(piece(zero, 0), piece(zero, 1), piece(zero, 2))
    across = jnp.concatenate(
        [
            dot(jnp.concatenate([piece(zero, 3), piece(zero, 4)], 0), inv_a, 0, 1),
            dot(jnp.concatenate([piece(one, 3), piece(one, 4)], 1), inv_a, 1, 1),
        ],
        0,
    )
    square = dot(across, across, 1, 1)
    inv_b = inverse_factor_256(
        piece(one, 0) - square[:HALF, :HALF],
        piece(one, 1) - square[HALF:, :HALF],
        piece(one, 2) - square[HALF:, HALF:],
    )
    inv_a_ref[...] = inv_a
    across_ref[...] = across
    inv_b_ref[...] = inv_b


def factor(core, own, other):
    whole = pl.BlockSpec(memory_space=pltpu.VMEM)
    return pl.pallas_call(
        factor_kernel,
        out_shape=[jax.ShapeDtypeStruct((PW, PW), jnp.float32)] * 3,
        in_specs=[pl.BlockSpec(memory_space=pltpu.SMEM), whole, whole],
        out_specs=[whole] * 3,
        compiler_params=pltpu.CompilerParams(vmem_limit_bytes=24 << 20),
        name="factor",
    )(core, own, other)


def pick_kernel(index_ref, front_ref, *outs):
    for place in range(2 * len(outs)):
        start = pl.multiple_of(index_ref[place] * PW, PW)
        half = (place % 2) * PW
        outs[place // 2][:, half : half + PW] = front_ref[:, pl.ds(start, PW)]


def pick(index, front):
    whole = pl.BlockSpec(memory_space=pltpu.VMEM)
    return pl.pallas_call(
        pick_kernel,
        out_shape=[jax.ShapeDtypeStruct((front.shape[0], 2 * PW), jnp.float32)] * 4,
        in_specs=[pl.BlockSpec(memory_space=pltpu.SMEM), whole],
        out_specs=[whole] * 4,
        compiler_params=pltpu.CompilerParams(vmem_limit_bytes=16 << 20),
        name="pick",
    )(index, front)


def update_kernel(
    shift, group, place, live, at, r0, r1, r2, r3, inv_a_ref, across_ref, inv_b_ref, p0, p1, p2, p3, ahead_ref, base_ref,
    panel_ref, out_ref, weight_ref,
):
    slot = pl.program_id(0)

    @pl.when(slot == 0)
    def _():
        inv_a, across, inv_b = inv_a_ref[...], across_ref[...], inv_b_ref[...]
        rows_ref = jnp.where(at[1] == 0, r0[...], r1[...] + r2[...] + r3[...])
        panel_a = dot(rows_ref[:, :PW], inv_a, 1, 1)
        panel_b = dot(rows_ref[:, PW:] - dot(panel_a, across, 1, 1), inv_b, 1, 1)
        weight_b = dot(panel_b, inv_b, 1, 0)
        panel_ref[:, :PW] = panel_a
        panel_ref[:, PW:] = jnp.where(at[0] == 0, 0.0, panel_b)
        weight_ref[:, :PW] = dot(panel_a - dot(weight_b, across, 1, 0), inv_a, 1, 0)
        weight_ref[:, PW:] = weight_b

    product = dot(weight_ref[...], ahead_ref[...].reshape(PW, LEAD), 1, 1)
    column = pl.multiple_of(place[slot] * PW, PW)
    base = base_ref[...]
    out_ref[...] = base
    for index, ref in enumerate((p0, p1, p2, p3)):

        @pl.when((shift[slot] == index) & (live[slot] == 1))
        def _():
            out_ref[...] = base + (ref[:, pl.ds(column, PW)] - product)


def update(scalars, rows, inverse, pieces, ahead, base):
    height, width = base.shape
    full = pl.BlockSpec((height, LEAD), lambda u, *s: (0, 0))
    square = pl.BlockSpec((PW, PW), lambda u, *s: (0, 0))
    tile = pl.BlockSpec((height, PW), lambda u, *s: (0, u))
    return pl.pallas_call(
        update_kernel,
        out_shape=[
            jax.ShapeDtypeStruct((height, LEAD), jnp.float32),
            jax.ShapeDtypeStruct(base.shape, jnp.float32),
        ],
        grid_spec=pltpu.PrefetchScalarGridSpec(
            num_scalar_prefetch=5,
            grid=(width // PW,),
            in_specs=[
                *[full] * 4,
                *[square] * 3,
                *[full] * 4,
                pl.BlockSpec((8, 1, 32, LEAD), lambda u, shift, group, place, live, at: (group[u], place[u], 0, 0)),
                tile,
            ],
            out_specs=[full, tile],
            scratch_shapes=[pltpu.VMEM((height, LEAD), jnp.float32)],
        ),
        compiler_params=pltpu.CompilerParams(vmem_limit_bytes=56 << 20),
        name="update",
    )(*scalars, *rows, *inverse, *pieces, ahead, base)


def spread_steps():
    have = [{(0, 0)}, {(0, 0)}]
    steps = []
    for step in range(4):
        pairs = []
        for core in range(2):
            axis = (step // 2 + 1 - core) % 2
            new = set()
            for at in sorted(have[core]):
                to = list(at)
                if step % 2 == 0:
                    to[axis] = 1
                else:
                    to[axis] = 3 if at[axis] == 0 else 2
                new.add(tuple(to))
                pairs.append(((at[0] * 4 + at[1]) * 2 + core, (to[0] * 4 + to[1]) * 2 + core))
            have[core] |= new
        steps.append(pairs)
    return steps


def corner_blocks(rows, core):
    first = [rows[:HALF, :HALF], rows[HALF:, :HALF], rows[HALF:, HALF:PW], rows[:HALF, PW : PW + HALF], rows[HALF:, PW : PW + HALF]]
    second = [rows[:HALF, PW : PW + HALF], rows[HALF:, PW : PW + HALF], rows[HALF:, PW + HALF :], rows[HALF:, :HALF], rows[HALF:, HALF:PW]]
    return jnp.where(core == 0, jnp.concatenate(first, 0), jnp.concatenate(second, 0))


def shards(front, ancestor, tile_map):
    row = lax.axis_index("row")
    col = lax.axis_index("col")
    core = row % 2
    line = (row // 2) % 4
    plane = row // 8
    swap = [(i, i ^ 1) for i in range(32)]

    owner = (tile_map // 8).reshape(4, 8)
    ids = jnp.arange(8, dtype=jnp.int32)
    same = owner[:, :, None] == owner[:, None, :]
    rank = jnp.sum(jnp.where(same & (ids[None, None, :] < ids[None, :, None]), 1, 0), axis=2)
    cols4 = jnp.arange(4, dtype=jnp.int32)
    hit = (owner[:, None, None, :] == cols4[None, :, None, None]) & (
        rank[:, None, None, :] == jnp.arange(2, dtype=jnp.int32)[None, None, :, None]
    )
    chosen = jnp.sum(jnp.where(hit, ids, 0), axis=3)
    slots = col * 8 + ids
    found = tile_map[None, :] == slots[:, None]
    all_ids = jnp.arange(32, dtype=jnp.int32)
    source = jnp.sum(jnp.where(found, all_ids, 0), axis=1)
    place = jnp.sum(jnp.where(found, rank.reshape(32), 0), axis=1)
    group = source // 8
    shift = (col - group) % 4
    live = jnp.where((source >= 2) & (row >= 2), 1, 0).astype(jnp.int32)

    lead = front[:, :LEAD]
    copies = [lax.ppermute(lead, "col", [(0, to)]) for to in (1, 3, 2)]
    mate = lax.ppermute(lead, "row", swap)

    even = jnp.where(core == 0, lead, mate)
    odd = jnp.where(core == 0, mate, lead)
    both = jnp.stack([even, odd])
    parts = []
    for hop in range(4):
        at = 32 * (2 * ((line + hop) % 4) + core)
        parts.append(lax.dynamic_slice(both, (0, at, 0), (2, 32, LEAD)))
    parts = list(lax.optimization_barrier(tuple(parts)))
    for hop in range(1, 4):
        pairs = [(z * 8 + x * 2 + k, z * 8 + (x + hop) % 4 * 2 + k) for z in range(4) for x in range(4) for k in range(2)]
        parts[hop] = lax.ppermute(parts[hop], "row", pairs)

    own = lax.dynamic_index_in_dim(chosen, col, 0, keepdims=False)
    order = jnp.take(own, (col + cols4) % 4, axis=0).reshape(8)
    order, mate = lax.optimization_barrier((order, mate))
    pieces = list(pick(order, front))

    parts = jnp.concatenate(parts, 0)
    mine = lax.dynamic_index_in_dim(chosen, plane, 0, keepdims=False)
    index = ((line - mine // 2) % 4) * 2 + mine % 2
    sent = jnp.take(parts, index, axis=0)
    sent, *copies = lax.optimization_barrier((sent, *copies))

    spread = spread_steps()
    rows = jnp.where(col == 0, lead, copies[0] + copies[1] + copies[2])
    block = jnp.where(row < 2, corner_blocks(rows, core), 0.0)
    block = block + lax.ppermute(block, "row", spread[0])
    kept = jnp.where(col == 0, sent[0], 0.0)
    for to in range(1, 4):
        kept = kept + lax.ppermute(sent[to], "col", [(0, to)])
    block, kept, *pieces = lax.optimization_barrier((block, kept, *pieces))
    ahead = lax.all_gather(kept, "row", axis=0, tiled=False)

    for hop in (1, 3, 2):
        pieces[hop] = lax.ppermute(pieces[hop], "col", [(i, (i + hop) % 4) for i in range(4)])
    block = block + lax.ppermute(block, "row", spread[1])
    block = block + lax.ppermute(block, "row", spread[2])
    block, pieces[1] = lax.optimization_barrier((block, pieces[1]))
    block = block + lax.ppermute(block, "row", spread[3])
    block, pieces[3] = lax.optimization_barrier((block, pieces[3]))
    other = lax.ppermute(block, "row", swap)

    inverse = factor(core[None], block, other)
    panel, updated = update(
        (shift, group, place, live, jnp.stack([row, col])), [lead, *copies], inverse, pieces, ahead, ancestor
    )
    return panel, updated


def solution(mesh):
    return jax.shard_map(
        shards,
        mesh=mesh,
        in_specs=(P("row", "col"), P("row", "col"), P()),
        out_specs=(P("row", None), P("row", "col")),
        check_vma=False,
    )
```

```python
import jax
import jax.numpy as jnp
from jax import lax
from jax.experimental import pallas as pl
from jax.experimental.pallas import tpu as pltpu
from jax.sharding import PartitionSpec as P

PW = 256
LEAD = 512
HALF = 128
STEP = 8
TURN = 2
HIGHEST = lax.Precision.HIGHEST


def dot(a, b, ca, cb):
    return lax.dot_general(
        a, b, (((ca,), (cb,)), ((), ())), precision=HIGHEST, preferred_element_type=jnp.float32
    )


def spread_lane(rows, index):
    return jnp.broadcast_to(rows[:, index : index + 1], rows.shape)


def spread_row(rows, index):
    return jnp.broadcast_to(rows[index : index + 1, :], rows.shape)


def inverse_factor_128(square):
    n = HALF
    lane = lax.broadcasted_iota(jnp.int32, (STEP, n), 1)
    sub = lax.broadcasted_iota(jnp.int32, (STEP, n), 0)
    lane_turn = lax.broadcasted_iota(jnp.int32, (TURN * STEP, n), 1)
    count = n // STEP
    groups = [square[STEP * t : STEP * (t + 1), :] for t in range(count)]
    for turn in range(0, count, TURN):
        for step in range(turn, turn + TURN):
            start = STEP * step
            inside = (lane >= start) & (lane < start + STEP)
            top = groups[step]
            columns = [spread_lane(top, start + i) for i in range(STEP)]
            entry = [[spread_row(columns[i], j) if i <= j else None for i in range(STEP)] for j in range(STEP)]
            top = jnp.where(inside, jnp.where(lane - start == sub, 1.0, 0.0), top)
            rows = [spread_row(top, j) for j in range(STEP)]
            near = range(step + 1, min(turn + 2 * TURN, count))
            beside = {t: [spread_lane(groups[t], start + i) for i in range(STEP)] for t in near}
            for t in near:
                groups[t] = jnp.where(inside, 0.0, groups[t])
            done = [None] * STEP
            for i in range(STEP):
                scale = lax.rsqrt(entry[i][i])
                below = [None] * STEP
                for j in range(i + 1, STEP):
                    below[j] = entry[j][i] * scale
                    for k in range(i + 1, j + 1):
                        entry[j][k] = entry[j][k] - below[j] * below[k]
                done[i] = rows[i] * scale
                for j in range(i + 1, STEP):
                    rows[j] = rows[j] - below[j] * done[i]
                for t in near:
                    column = beside[t][i] * scale
                    for k in range(i + 1, STEP):
                        beside[t][k] = beside[t][k] - column * below[k]
                    groups[t] = groups[t] - column * done[i]
            solved = done[0]
            for i in range(1, STEP):
                solved = jnp.where(sub == i, done[i], solved)
            for t in range(step):
                groups[t] = jnp.where(inside, 0.0, groups[t])
            groups[step] = solved
        far = range(turn + 2 * TURN, count)
        if far:
            start, end = STEP * turn, STEP * (turn + TURN)
            solved = jnp.concatenate(groups[turn : turn + TURN], 0)
            ahead = jnp.where(lane_turn >= end + STEP * TURN, solved, 0.0)
            product = dot(ahead, solved, 0, 0)
            inside = (lane >= start) & (lane < end)
            for t in far:
                groups[t] = jnp.where(inside, 0.0, groups[t]) - product[STEP * t : STEP * (t + 1), :]
    return jnp.concatenate(groups, 0)


def inverse_factor_256(top, left, bottom):
    first = inverse_factor_128(top)
    across = dot(left, first, 1, 1)
    second = inverse_factor_128(bottom - dot(across, across, 1, 1))
    lower = -dot(second, dot(across, first, 1, 0), 1, 0)
    return jnp.concatenate(
        [
            jnp.concatenate([first, jnp.zeros_like(first)], 1),
            jnp.concatenate([lower, second], 1),
        ],
        0,
    )


def local_call(kernel, name, shapes, scalars=0, plan=()):
    whole = pl.BlockSpec(memory_space=pltpu.VMEM)
    small = pl.BlockSpec(memory_space=pltpu.SMEM)

    def call(*args):
        return pl.pallas_call(
            kernel,
            out_shape=[jax.ShapeDtypeStruct(shape, jnp.float32) for shape in shapes]
            + [jax.ShapeDtypeStruct(shape, jnp.int32) for shape in plan],
            in_specs=[small] * scalars + [whole] * (len(args) - scalars),
            out_specs=[whole] * len(shapes) + [small] * len(plan),
            compiler_params=pltpu.CompilerParams(vmem_limit_bytes=16 << 20),
            name=name,
        )(*args)

    return call


def position():
    row = lax.axis_index("row")
    return row // 8, (row // 2) % 4, row % 2, lax.axis_index("col")


def factor_kernel(own_ref, other_ref, inv_a_ref, across_ref, inv_b_ref):
    even = lax.axis_index("row") % 2 == 0
    own, other = own_ref[...], other_ref[...]
    zero = jnp.where(even, own, other)
    one = jnp.where(even, other, own)

    def piece(blocks, index):
        return blocks[index * HALF : (index + 1) * HALF]

    inv_a = inverse_factor_256(piece(zero, 0), piece(zero, 1), piece(zero, 2))
    across = jnp.concatenate(
        [
            dot(jnp.concatenate([piece(zero, 3), piece(zero, 4)], 0), inv_a, 0, 1),
            dot(jnp.concatenate([piece(one, 3), piece(one, 4)], 1), inv_a, 1, 1),
        ],
        0,
    )
    square = dot(across, across, 1, 1)
    inv_b = inverse_factor_256(
        piece(one, 0) - square[:HALF, :HALF],
        piece(one, 1) - square[HALF:, :HALF],
        piece(one, 2) - square[HALF:, HALF:],
    )
    inv_a_ref[...] = inv_a
    across_ref[...] = across
    inv_b_ref[...] = inv_b


def factor(own, other):
    return local_call(factor_kernel, "factor", [(PW, PW)] * 3)(own, other)


def share_kernel(lead_ref, mate_ref, *outs):
    _, line, core, _ = position()
    for hop in range(4):
        rows = pl.ds(pl.multiple_of(32 * (2 * ((line + hop) % 4) + core), 32), 32)
        for parity in range(2):

            @pl.when(core == parity)
            def _():
                outs[hop][parity] = lead_ref[rows, :]
                outs[hop][1 - parity] = mate_ref[rows, :]


def owners_and_ranks(map_ref, group):
    owners = [map_ref[8 * group + t] // 8 for t in range(8)]
    ranks = [sum((owners[p] == owners[t]).astype(jnp.int32) for p in range(t)) + jnp.int32(0) for t in range(8)]
    return owners, ranks


def sort_kernel(map_ref, *refs):
    ins, outs = refs[:4], refs[4:]
    plane, line, _, _ = position()
    owners, ranks = owners_and_ranks(map_ref, plane)
    for tile in range(8):
        for hop in range(4):

            @pl.when((line - tile // 2) % 4 == hop)
            def _():
                piece = ins[hop][tile % 2]
                for owner in range(4):

                    @pl.when(owners[tile] == owner)
                    def _():
                        outs[owner][pl.ds(ranks[tile], 1)] = piece[None]


def merge_kernel(*refs):
    for index, ref in enumerate(refs[:4]):

        @pl.when(lax.axis_index("col") == index)
        def _():
            refs[4][...] = ref[...]


def corner_kernel(*refs):
    plane, line, core, col = position()
    out = refs[4]
    out[...] = jnp.zeros_like(out)
    for index, ref in enumerate(refs[:4]):

        @pl.when((col == index) & (plane == 0) & (line == 0))
        def _():
            @pl.when(core == 0)
            def _():
                out[0 : 2 * HALF] = ref[:, :HALF]
                out[2 * HALF : 3 * HALF] = ref[HALF:, HALF:PW]
                out[3 * HALF :] = ref[:, PW : PW + HALF]

            @pl.when(core == 1)
            def _():
                out[0 : 2 * HALF] = ref[:, PW : PW + HALF]
                out[2 * HALF : 3 * HALF] = ref[HALF:, PW + HALF :]
                out[3 * HALF : 4 * HALF] = ref[HALF:, :HALF]
                out[4 * HALF :] = ref[HALF:, HALF:PW]


def pick_kernel(map_ref, front_ref, *refs):
    outs, plan_ref = refs[:4], refs[4]
    col = lax.axis_index("col")
    row = lax.axis_index("row")
    for group in range(4):
        owners, ranks = owners_and_ranks(map_ref, group)

        @pl.when(col == group)
        def _():
            for tile in range(8):
                for hop in range(4):

                    @pl.when((owners[tile] - col) % 4 == hop)
                    def _():
                        column = pl.multiple_of(ranks[tile] * PW, PW)
                        outs[hop][:, pl.ds(column, PW)] = front_ref[:, tile * PW : (tile + 1) * PW]

        for tile in range(8):
            slot = map_ref[8 * group + tile] % 8

            @pl.when(owners[tile] == col)
            def _():
                plan_ref[0, slot] = (col - group) % 4
                plan_ref[1, slot] = jnp.int32(group)
                plan_ref[2, slot] = ranks[tile]
                plan_ref[3, slot] = ((row >= 2) & (8 * group + tile >= 2)).astype(jnp.int32)


def update_kernel(plan, *refs):
    rows, inverse, pieces = refs[:4], refs[4:7], refs[7:11]
    ahead_ref, base_ref, panel_ref, out_ref, rows_ref, weight_ref = refs[11:]
    slot = pl.program_id(0)

    @pl.when(slot == 0)
    def _():
        for index, ref in enumerate(rows):

            @pl.when(lax.axis_index("col") == index)
            def _():
                rows_ref[...] = ref[...]

        inv_a, across, inv_b = [ref[...] for ref in inverse]
        panel_a = dot(rows_ref[:, :PW], inv_a, 1, 1)
        panel_b = dot(rows_ref[:, PW:] - dot(panel_a, across, 1, 1), inv_b, 1, 1)
        weight_b = dot(panel_b, inv_b, 1, 0)
        panel_ref[:, :PW] = panel_a
        panel_ref[:, PW:] = jnp.where(lax.axis_index("row") == 0, 0.0, panel_b)
        weight_ref[:, :PW] = dot(panel_a - dot(weight_b, across, 1, 0), inv_a, 1, 0)
        weight_ref[:, PW:] = weight_b

    product = dot(weight_ref[...], ahead_ref[...].reshape(PW, LEAD), 1, 1)
    column = pl.multiple_of(plan[2, slot] * PW, PW)
    base = base_ref[...]
    out_ref[...] = base
    for index, ref in enumerate(pieces):

        @pl.when((plan[0, slot] == index) & (plan[3, slot] == 1))
        def _():
            out_ref[...] = base + (ref[:, pl.ds(column, PW)] - product)


def update(plan, rows, inverse, pieces, ahead, base):
    height, width = base.shape
    whole = pl.BlockSpec(memory_space=pltpu.VMEM)
    tile = pl.BlockSpec((height, PW), lambda u, plan: (0, u))
    return pl.pallas_call(
        update_kernel,
        out_shape=[
            jax.ShapeDtypeStruct((height, LEAD), jnp.float32),
            jax.ShapeDtypeStruct(base.shape, jnp.float32),
        ],
        grid_spec=pltpu.PrefetchScalarGridSpec(
            num_scalar_prefetch=1,
            grid=(width // PW,),
            in_specs=[whole] * 11
            + [pl.BlockSpec((8, 1, 32, LEAD), lambda u, plan: (plan[1, u], plan[2, u], 0, 0)), tile],
            out_specs=[pl.BlockSpec((height, LEAD), lambda u, plan: (0, 0)), tile],
            scratch_shapes=[pltpu.VMEM((height, LEAD), jnp.float32)] * 2,
        ),
        compiler_params=pltpu.CompilerParams(vmem_limit_bytes=16 << 20),
        name="update",
    )(plan, *rows, *inverse, *pieces, ahead, base)


def spread_steps():
    have = [{(0, 0)}, {(0, 0)}]
    steps = []
    for step in range(4):
        pairs = []
        for core in range(2):
            axis = (step // 2 + 1 - core) % 2
            new = set()
            for at in sorted(have[core]):
                to = list(at)
                if step % 2 == 0:
                    to[axis] = 1
                else:
                    to[axis] = 3 if at[axis] == 0 else 2
                new.add(tuple(to))
                pairs.append(((at[0] * 4 + at[1]) * 2 + core, (to[0] * 4 + to[1]) * 2 + core))
            have[core] |= new
        steps.append(pairs)
    return steps


def shards(front, ancestor, tile_map):
    height = front.shape[0]
    swap = [(i, i ^ 1) for i in range(32)]
    part = (2, 32, LEAD)
    lead = front[:, :LEAD]

    copies = [lax.ppermute(lead, "col", [(0, to)]) for to in (1, 2, 3)]

    mate = lax.ppermute(lead, "row", swap)
    parts = list(local_call(share_kernel, "share", [part] * 4)(lead, mate))
    for hop in range(1, 4):
        pairs = [(z * 8 + x * 2 + k, z * 8 + (x + hop) % 4 * 2 + k) for z in range(4) for x in range(4) for k in range(2)]
        parts[hop] = lax.ppermute(parts[hop], "row", pairs)
    parts = list(local_call(sort_kernel, "sort", [part] * 4, 1)(tile_map, *parts))
    for to in range(1, 4):
        parts[to] = lax.ppermute(parts[to], "col", [(0, to)])
    copies, parts = lax.optimization_barrier((copies, parts))
    ahead = lax.all_gather(local_call(merge_kernel, "merge", [part])(*parts)[0], "row", axis=0, tiled=False)

    *pieces, plan = local_call(pick_kernel, "pick", [(height, 2 * PW)] * 4, 1, [(4, 8)])(tile_map, front)

    block = local_call(corner_kernel, "corner", [(5 * HALF, HALF)])(lead, *copies)[0]
    spread = spread_steps()
    block = block + lax.ppermute(block, "row", spread[0])
    block, *pieces = lax.optimization_barrier((block, *pieces))
    for hop in (1, 3, 2):
        pieces[hop] = lax.ppermute(pieces[hop], "col", [(i, (i + hop) % 4) for i in range(4)])
    block = block + lax.ppermute(block, "row", spread[1])
    block = block + lax.ppermute(block, "row", spread[2])
    block = block + lax.ppermute(block, "row", spread[3])
    block, pieces[1], pieces[3] = lax.optimization_barrier((block, pieces[1], pieces[3]))
    other = lax.ppermute(block, "row", swap)

    inverse = factor(block, other)
    panel, updated = update(plan, [lead, *copies], inverse, pieces, ahead, ancestor)
    return panel, updated


def solution(mesh):
    return jax.shard_map(
        shards,
        mesh=mesh,
        in_specs=(P("row", "col"), P("row", "col"), P()),
        out_specs=(P("row", None), P("row", "col")),
        check_vma=False,
    )
```

```python
import jax
import jax.numpy as jnp
from jax import lax
from jax.experimental import pallas as pl
from jax.experimental.pallas import tpu as pltpu
from jax.sharding import PartitionSpec as P

PW = 256
LEAD = 512
HALF = 128
STEP = 8
TURN = 2
HIGHEST = lax.Precision.HIGHEST


def dot(a, b, ca, cb):
    return lax.dot_general(
        a, b, (((ca,), (cb,)), ((), ())), precision=HIGHEST, preferred_element_type=jnp.float32
    )


def spread_lane(rows, index):
    return jnp.broadcast_to(rows[:, index : index + 1], rows.shape)


def spread_row(rows, index):
    return jnp.broadcast_to(rows[index : index + 1, :], rows.shape)


def inverse_factor_128(square):
    n = HALF
    lane = lax.broadcasted_iota(jnp.int32, (STEP, n), 1)
    sub = lax.broadcasted_iota(jnp.int32, (STEP, n), 0)
    lane_turn = lax.broadcasted_iota(jnp.int32, (TURN * STEP, n), 1)
    count = n // STEP
    groups = [square[STEP * t : STEP * (t + 1), :] for t in range(count)]
    for turn in range(0, count, TURN):
        for step in range(turn, turn + TURN):
            start = STEP * step
            inside = (lane >= start) & (lane < start + STEP)
            top = groups[step]
            columns = [spread_lane(top, start + i) for i in range(STEP)]
            entry = [[spread_row(columns[i], j) if i <= j else None for i in range(STEP)] for j in range(STEP)]
            top = jnp.where(inside, jnp.where(lane - start == sub, 1.0, 0.0), top)
            rows = [spread_row(top, j) for j in range(STEP)]
            near = range(step + 1, min(turn + 2 * TURN, count))
            beside = {t: [spread_lane(groups[t], start + i) for i in range(STEP)] for t in near}
            for t in near:
                groups[t] = jnp.where(inside, 0.0, groups[t])
            done = [None] * STEP
            for i in range(STEP):
                scale = lax.rsqrt(entry[i][i])
                below = [None] * STEP
                for j in range(i + 1, STEP):
                    below[j] = entry[j][i] * scale
                    for k in range(i + 1, j + 1):
                        entry[j][k] = entry[j][k] - below[j] * below[k]
                done[i] = rows[i] * scale
                for j in range(i + 1, STEP):
                    rows[j] = rows[j] - below[j] * done[i]
                for t in near:
                    column = beside[t][i] * scale
                    for k in range(i + 1, STEP):
                        beside[t][k] = beside[t][k] - column * below[k]
                    groups[t] = groups[t] - column * done[i]
            solved = done[0]
            for i in range(1, STEP):
                solved = jnp.where(sub == i, done[i], solved)
            for t in range(step):
                groups[t] = jnp.where(inside, 0.0, groups[t])
            groups[step] = solved
        far = range(turn + 2 * TURN, count)
        if far:
            start, end = STEP * turn, STEP * (turn + TURN)
            solved = jnp.concatenate(groups[turn : turn + TURN], 0)
            ahead = jnp.where(lane_turn >= end + STEP * TURN, solved, 0.0)
            product = dot(ahead, solved, 0, 0)
            inside = (lane >= start) & (lane < end)
            for t in far:
                groups[t] = jnp.where(inside, 0.0, groups[t]) - product[STEP * t : STEP * (t + 1), :]
    return jnp.concatenate(groups, 0)


def inverse_factor_256(top, left, bottom):
    first = inverse_factor_128(top)
    across = dot(left, first, 1, 1)
    second = inverse_factor_128(bottom - dot(across, across, 1, 1))
    lower = -dot(second, dot(across, first, 1, 0), 1, 0)
    return jnp.concatenate(
        [
            jnp.concatenate([first, jnp.zeros_like(first)], 1),
            jnp.concatenate([lower, second], 1),
        ],
        0,
    )


def local_call(kernel, name, shapes, scalars=0, plan=()):
    whole = pl.BlockSpec(memory_space=pltpu.VMEM)
    small = pl.BlockSpec(memory_space=pltpu.SMEM)

    def call(*args):
        return pl.pallas_call(
            kernel,
            out_shape=[jax.ShapeDtypeStruct(shape, jnp.float32) for shape in shapes]
            + [jax.ShapeDtypeStruct(shape, jnp.int32) for shape in plan],
            in_specs=[small] * scalars + [whole] * (len(args) - scalars),
            out_specs=[whole] * len(shapes) + [small] * len(plan),
            compiler_params=pltpu.CompilerParams(vmem_limit_bytes=16 << 20),
            name=name,
        )(*args)

    return call


def position():
    row = lax.axis_index("row")
    return row // 8, (row // 2) % 4, row % 2, lax.axis_index("col")


def factor_kernel(own_ref, other_ref, inv_a_ref, across_ref, inv_b_ref):
    even = lax.axis_index("row") % 2 == 0
    own, other = own_ref[...], other_ref[...]
    zero = jnp.where(even, own, other)
    one = jnp.where(even, other, own)

    def piece(blocks, index):
        return blocks[index * HALF : (index + 1) * HALF]

    inv_a = inverse_factor_256(piece(zero, 0), piece(zero, 1), piece(zero, 2))
    across = jnp.concatenate(
        [
            dot(jnp.concatenate([piece(zero, 3), piece(zero, 4)], 0), inv_a, 0, 1),
            dot(jnp.concatenate([piece(one, 3), piece(one, 4)], 1), inv_a, 1, 1),
        ],
        0,
    )
    square = dot(across, across, 1, 1)
    inv_b = inverse_factor_256(
        piece(one, 0) - square[:HALF, :HALF],
        piece(one, 1) - square[HALF:, :HALF],
        piece(one, 2) - square[HALF:, HALF:],
    )
    inv_a_ref[...] = inv_a
    across_ref[...] = across
    inv_b_ref[...] = inv_b


def factor(own, other):
    return local_call(factor_kernel, "factor", [(PW, PW)] * 3)(own, other)


def share_kernel(lead_ref, mate_ref, *outs):
    _, line, core, _ = position()
    for hop in range(4):
        rows = pl.ds(pl.multiple_of(32 * (2 * ((line + hop) % 4) + core), 32), 32)
        for parity in range(2):

            @pl.when(core == parity)
            def _():
                outs[hop][parity] = lead_ref[rows, :]
                outs[hop][1 - parity] = mate_ref[rows, :]


def owners_and_ranks(map_ref, group):
    owners = [map_ref[8 * group + t] // 8 for t in range(8)]
    ranks = [sum((owners[p] == owners[t]).astype(jnp.int32) for p in range(t)) + jnp.int32(0) for t in range(8)]
    return owners, ranks


def sort_kernel(map_ref, *refs):
    ins, outs = refs[:4], refs[4:]
    plane, line, _, _ = position()
    owners, ranks = owners_and_ranks(map_ref, plane)
    for tile in range(8):
        for hop in range(4):

            @pl.when((line - tile // 2) % 4 == hop)
            def _():
                piece = ins[hop][tile % 2]
                for owner in range(4):

                    @pl.when(owners[tile] == owner)
                    def _():
                        outs[owner][pl.ds(ranks[tile], 1)] = piece[None]


def merge_kernel(*refs):
    for index, ref in enumerate(refs[:4]):

        @pl.when(lax.axis_index("col") == index)
        def _():
            refs[4][...] = ref[...]


def corner_kernel(*refs):
    plane, line, core, col = position()
    out = refs[4]
    out[...] = jnp.zeros_like(out)
    for index, ref in enumerate(refs[:4]):

        @pl.when((col == index) & (plane == 0) & (line == 0))
        def _():
            @pl.when(core == 0)
            def _():
                out[0 : 2 * HALF] = ref[:, :HALF]
                out[2 * HALF : 3 * HALF] = ref[HALF:, HALF:PW]
                out[3 * HALF :] = ref[:, PW : PW + HALF]

            @pl.when(core == 1)
            def _():
                out[0 : 2 * HALF] = ref[:, PW : PW + HALF]
                out[2 * HALF : 3 * HALF] = ref[HALF:, PW + HALF :]
                out[3 * HALF : 4 * HALF] = ref[HALF:, :HALF]
                out[4 * HALF :] = ref[HALF:, HALF:PW]


def pick_kernel(map_ref, front_ref, *refs):
    outs, plan_ref = refs[:4], refs[4]
    col = lax.axis_index("col")
    row = lax.axis_index("row")
    for group in range(4):
        owners, ranks = owners_and_ranks(map_ref, group)

        @pl.when(col == group)
        def _():
            for tile in range(8):
                for hop in range(4):

                    @pl.when((owners[tile] - col) % 4 == hop)
                    def _():
                        column = pl.multiple_of(ranks[tile] * PW, PW)
                        outs[hop][:, pl.ds(column, PW)] = front_ref[:, tile * PW : (tile + 1) * PW]

        for tile in range(8):
            slot = map_ref[8 * group + tile] % 8

            @pl.when(owners[tile] == col)
            def _():
                plan_ref[0, slot] = (col - group) % 4
                plan_ref[1, slot] = jnp.int32(group)
                plan_ref[2, slot] = ranks[tile]
                plan_ref[3, slot] = ((row >= 2) & (8 * group + tile >= 2)).astype(jnp.int32)


def weight_kernel(*refs):
    rows, inverse = refs[:4], refs[4:7]
    panel_ref, weight_ref, rows_ref = refs[7:]
    for index, ref in enumerate(rows):

        @pl.when(lax.axis_index("col") == index)
        def _():
            rows_ref[...] = ref[...]

    inv_a, across, inv_b = [ref[...] for ref in inverse]
    panel_a = dot(rows_ref[:, :PW], inv_a, 1, 1)
    panel_b = dot(rows_ref[:, PW:] - dot(panel_a, across, 1, 1), inv_b, 1, 1)
    weight_b = dot(panel_b, inv_b, 1, 0)
    panel_ref[:, :PW] = panel_a
    panel_ref[:, PW:] = jnp.where(lax.axis_index("row") == 0, 0.0, panel_b)
    weight_ref[:, :PW] = dot(panel_a - dot(weight_b, across, 1, 0), inv_a, 1, 0)
    weight_ref[:, PW:] = weight_b


def weigh(rows, inverse):
    whole = pl.BlockSpec(memory_space=pltpu.VMEM)
    shape = (rows[0].shape[0], LEAD)
    return pl.pallas_call(
        weight_kernel,
        out_shape=[jax.ShapeDtypeStruct(shape, jnp.float32)] * 2,
        in_specs=[whole] * 7,
        out_specs=[whole] * 2,
        scratch_shapes=[pltpu.VMEM(shape, jnp.float32)],
        compiler_params=pltpu.CompilerParams(vmem_limit_bytes=16 << 20),
        name="weigh",
    )(*rows, *inverse)


def update_kernel(plan, *refs):
    weight_ref, pieces, gathered = refs[0], refs[1:5], refs[5:9]
    base_ref, out_ref, ahead_ref = refs[9:]
    slot = pl.program_id(0)
    plane, line, core, _ = position()
    group, place = plan[1, slot], plan[2, slot]
    for parity in range(2):
        holder = core if parity == 0 else 1 - core
        for x in range(4):
            off_z, off_x = plane ^ group, line ^ x
            first = jnp.where(holder == 0, off_x, off_z)
            second = jnp.where(holder == 0, off_z, off_x)
            index = ((first & 1) ^ (first >> 1)) + 2 * (first >> 1) + 4 * ((second & 1) ^ (second >> 1))
            rows = pl.ds(pl.multiple_of(index * 64 + place * 32, 32), 32)
            into = pl.ds(pl.multiple_of((2 * x + holder) * 32, 32), 32)
            for late in range(2):

                @pl.when((second >> 1) == late)
                def _():
                    ahead_ref[into, :] = gathered[2 * parity + late][rows, :]

    product = dot(weight_ref[...], ahead_ref[...], 1, 1)
    column = pl.multiple_of(place * PW, PW)
    base = base_ref[...]
    out_ref[...] = base
    for index, ref in enumerate(pieces):

        @pl.when((plan[0, slot] == index) & (plan[3, slot] == 1))
        def _():
            out_ref[...] = base + (ref[:, pl.ds(column, PW)] - product)


def update(plan, weight, pieces, gathered, base):
    height, width = base.shape
    whole = pl.BlockSpec(memory_space=pltpu.VMEM)
    tile = pl.BlockSpec((height, PW), lambda u, plan: (0, u))
    return pl.pallas_call(
        update_kernel,
        out_shape=jax.ShapeDtypeStruct(base.shape, jnp.float32),
        grid_spec=pltpu.PrefetchScalarGridSpec(
            num_scalar_prefetch=1,
            grid=(width // PW,),
            in_specs=[whole] * 9 + [tile],
            out_specs=tile,
            scratch_shapes=[pltpu.VMEM((PW, LEAD), jnp.float32)],
        ),
        compiler_params=pltpu.CompilerParams(vmem_limit_bytes=16 << 20),
        name="update",
    )(plan, weight, *pieces, *gathered, base)


def doubling_steps():
    every, spread = [], []
    have = [{(0, 0)}, {(0, 0)}]
    for step in range(4):
        flip = 1 if step % 2 == 0 else 3
        pairs = []
        for z in range(4):
            for x in range(4):
                for core in range(2):
                    to = (z, x ^ flip) if step // 2 == core else (z ^ flip, x)
                    pairs.append(((z * 4 + x) * 2 + core, (to[0] * 4 + to[1]) * 2 + core, (z, x), to, core))
        every.append([pair[:2] for pair in pairs])
        spread.append([pair[:2] for pair in pairs if pair[2] in have[pair[4]]])
        for core in range(2):
            have[core] |= {pair[3] for pair in pairs if pair[4] == core and pair[2] in have[core]}
    return every, spread


def shards(front, ancestor, tile_map):
    height = front.shape[0]
    swap = [(i, i ^ 1) for i in range(32)]
    part = (2, 32, LEAD)
    lead = front[:, :LEAD]

    copies = [lax.ppermute(lead, "col", [(0, to)]) for to in (1, 2, 3)]

    mate = lax.ppermute(lead, "row", swap)
    parts = list(local_call(share_kernel, "share", [part] * 4)(lead, mate))
    for hop in range(1, 4):
        pairs = [(z * 8 + x * 2 + k, z * 8 + (x + hop) % 4 * 2 + k) for z in range(4) for x in range(4) for k in range(2)]
        parts[hop] = lax.ppermute(parts[hop], "row", pairs)
    parts = list(local_call(sort_kernel, "sort", [part] * 4, 1)(tile_map, *parts))
    for to in range(1, 4):
        parts[to] = lax.ppermute(parts[to], "col", [(0, to)])
    copies, parts = lax.optimization_barrier((copies, parts))
    gathered = local_call(merge_kernel, "merge", [part])(*parts)[0].reshape(64, LEAD)

    *pieces, plan = local_call(pick_kernel, "pick", [(height, 2 * PW)] * 4, 1, [(4, 8)])(tile_map, front)

    block = local_call(corner_kernel, "corner", [(5 * HALF, HALF)])(lead, *copies)[0]
    every, spread = doubling_steps()
    ring = [[(i, (i + hop) % 4) for i in range(4)] for hop in range(4)]
    for step in range(3):
        block = block + lax.ppermute(block, "row", spread[step])
        gathered = jnp.concatenate([gathered, lax.ppermute(gathered, "row", every[step])], 0)
        if step == 1:
            pieces[1], pieces[3] = [lax.ppermute(pieces[hop], "col", ring[hop]) for hop in (1, 3)]
        if step != 1:
            block, gathered, *pieces = lax.optimization_barrier((block, gathered, *pieces))
        else:
            block, gathered = lax.optimization_barrier((block, gathered))
    pieces[2] = lax.ppermute(pieces[2], "col", ring[2])
    late = lax.ppermute(gathered, "row", every[3])
    block = block + lax.ppermute(block, "row", spread[3])
    other = lax.ppermute(block, "row", swap)
    other_gathered = lax.ppermute(gathered, "row", swap)

    inverse = factor(block, other)
    late, inverse = lax.optimization_barrier((late, inverse))
    other_late = lax.ppermute(late, "row", swap)
    panel, weight = weigh([lead, *copies], inverse)
    updated = update(plan, weight, pieces, [gathered, late, other_gathered, other_late], ancestor)
    return panel, updated


def solution(mesh):
    return jax.shard_map(
        shards,
        mesh=mesh,
        in_specs=(P("row", "col"), P("row", "col"), P()),
        out_specs=(P("row", None), P("row", "col")),
        check_vma=False,
    )
```

```python
import jax
import jax.numpy as jnp
from jax import lax
from jax.experimental import pallas as pl
from jax.experimental.pallas import tpu as pltpu
from jax.sharding import PartitionSpec as P

PW = 256
LEAD = 512
HALF = 128
STEP = 8
TURN = 2
BLOCK = 160
LARGE = pl.CostEstimate(flops=20 << 30, bytes_accessed=1 << 20, transcendentals=0)
SMALL = pl.CostEstimate(flops=1 << 10, bytes_accessed=1 << 10, transcendentals=0)
HIGHEST = lax.Precision.HIGHEST


def dot(a, b, ca, cb):
    return lax.dot_general(
        a, b, (((ca,), (cb,)), ((), ())), precision=HIGHEST, preferred_element_type=jnp.float32
    )


def spread_lane(rows, index):
    return jnp.broadcast_to(rows[:, index : index + 1], rows.shape)


def spread_row(rows, index):
    return jnp.broadcast_to(rows[index : index + 1, :], rows.shape)


def inverse_factor_128(square):
    n = HALF
    lane = lax.broadcasted_iota(jnp.int32, (STEP, n), 1)
    sub = lax.broadcasted_iota(jnp.int32, (STEP, n), 0)
    lane_turn = lax.broadcasted_iota(jnp.int32, (TURN * STEP, n), 1)
    count = n // STEP
    groups = [square[STEP * t : STEP * (t + 1), :] for t in range(count)]
    for turn in range(0, count, TURN):
        for step in range(turn, turn + TURN):
            start = STEP * step
            inside = (lane >= start) & (lane < start + STEP)
            top = groups[step]
            columns = [spread_lane(top, start + i) for i in range(STEP)]
            entry = [[spread_row(columns[i], j) if i <= j else None for i in range(STEP)] for j in range(STEP)]
            top = jnp.where(inside, jnp.where(lane - start == sub, 1.0, 0.0), top)
            rows = [spread_row(top, j) for j in range(STEP)]
            near = range(step + 1, min(turn + 2 * TURN, count))
            beside = {t: [spread_lane(groups[t], start + i) for i in range(STEP)] for t in near}
            for t in near:
                groups[t] = jnp.where(inside, 0.0, groups[t])
            done = [None] * STEP
            for i in range(STEP):
                scale = lax.rsqrt(entry[i][i])
                below = [None] * STEP
                for j in range(i + 1, STEP):
                    below[j] = entry[j][i] * scale
                    for k in range(i + 1, j + 1):
                        entry[j][k] = entry[j][k] - below[j] * below[k]
                done[i] = rows[i] * scale
                for j in range(i + 1, STEP):
                    rows[j] = rows[j] - below[j] * done[i]
                for t in near:
                    column = beside[t][i] * scale
                    for k in range(i + 1, STEP):
                        beside[t][k] = beside[t][k] - column * below[k]
                    groups[t] = groups[t] - column * done[i]
            solved = done[0]
            for i in range(1, STEP):
                solved = jnp.where(sub == i, done[i], solved)
            for t in range(step):
                groups[t] = jnp.where(inside, 0.0, groups[t])
            groups[step] = solved
        far = range(turn + 2 * TURN, count)
        if far:
            start, end = STEP * turn, STEP * (turn + TURN)
            solved = jnp.concatenate(groups[turn : turn + TURN], 0)
            ahead = jnp.where(lane_turn >= end + STEP * TURN, solved, 0.0)
            product = dot(ahead, solved, 0, 0)
            inside = (lane >= start) & (lane < end)
            for t in far:
                groups[t] = jnp.where(inside, 0.0, groups[t]) - product[STEP * t : STEP * (t + 1), :]
    return jnp.concatenate(groups, 0)


def inverse_factor_256(top, left, bottom):
    first = inverse_factor_128(top)
    across = dot(left, first, 1, 1)
    second = inverse_factor_128(bottom - dot(across, across, 1, 1))
    lower = -dot(second, dot(across, first, 1, 0), 1, 0)
    return jnp.concatenate(
        [
            jnp.concatenate([first, jnp.zeros_like(first)], 1),
            jnp.concatenate([lower, second], 1),
        ],
        0,
    )


def local_call(kernel, name, shapes, scalars=0, plan=(), cost=SMALL):
    whole = pl.BlockSpec(memory_space=pltpu.VMEM)
    small = pl.BlockSpec(memory_space=pltpu.SMEM)

    def call(*args):
        return pl.pallas_call(
            kernel,
            out_shape=[jax.ShapeDtypeStruct(shape, jnp.float32) for shape in shapes]
            + [jax.ShapeDtypeStruct(shape, jnp.int32) for shape in plan],
            in_specs=[small] * scalars + [whole] * (len(args) - scalars),
            out_specs=[whole] * len(shapes) + [small] * len(plan),
            compiler_params=pltpu.CompilerParams(vmem_limit_bytes=16 << 20),
            cost_estimate=cost,
            name=name,
        )(*args)

    return call


def position():
    row = lax.axis_index("row")
    return row // 8, (row // 2) % 4, row % 2, lax.axis_index("col")


def factor_kernel(own_ref, other_ref, inv_a_ref, across_ref, inv_b_ref):
    even = lax.axis_index("row") % 2 == 0
    own, other = own_ref[...], other_ref[...]
    zero = jnp.where(even, own, other)
    one = jnp.where(even, other, own)

    def piece(blocks, index):
        rows = blocks[index * 32 : (index + 1) * 32]
        return jnp.concatenate([rows[:, part * HALF : (part + 1) * HALF] for part in range(4)], 0)

    inv_a = inverse_factor_256(piece(zero, 0), piece(zero, 1), piece(zero, 2))
    across = jnp.concatenate(
        [
            dot(jnp.concatenate([piece(zero, 3), piece(zero, 4)], 0), inv_a, 0, 1),
            dot(jnp.concatenate([piece(one, 3), piece(one, 4)], 1), inv_a, 1, 1),
        ],
        0,
    )
    square = dot(across, across, 1, 1)
    inv_b = inverse_factor_256(
        piece(one, 0) - square[:HALF, :HALF],
        piece(one, 1) - square[HALF:, :HALF],
        piece(one, 2) - square[HALF:, HALF:],
    )
    inv_a_ref[...] = inv_a
    across_ref[...] = across
    inv_b_ref[...] = inv_b


def factor(own, other):
    return local_call(factor_kernel, "factor", [(PW, PW)] * 3, cost=LARGE)(own, other)


def share_kernel(lead_ref, mate_ref, *outs):
    _, line, core, _ = position()
    for hop in range(4):
        rows = pl.ds(pl.multiple_of(32 * (2 * ((line + hop) % 4) + core), 32), 32)
        for parity in range(2):

            @pl.when(core == parity)
            def _():
                outs[hop][parity] = lead_ref[rows, :]
                outs[hop][1 - parity] = mate_ref[rows, :]


def owners_and_ranks(map_ref, group):
    owners = [map_ref[8 * group + t] // 8 for t in range(8)]
    ranks = [sum((owners[p] == owners[t]).astype(jnp.int32) for p in range(t)) + jnp.int32(0) for t in range(8)]
    return owners, ranks


def sort_kernel(map_ref, *refs):
    ins, outs = refs[:4], refs[4:]
    plane, line, _, _ = position()
    owners, ranks = owners_and_ranks(map_ref, plane)
    for tile in range(8):
        for hop in range(4):

            @pl.when((line - tile // 2) % 4 == hop)
            def _():
                piece = ins[hop][tile % 2]
                for owner in range(4):

                    @pl.when(owners[tile] == owner)
                    def _():
                        outs[owner][pl.ds(ranks[tile], 1)] = piece[None]


def corner_kernel(lead_ref, out_ref):
    plane, line, core, col = position()
    out_ref[...] = jnp.zeros_like(out_ref)
    places = [[(0, 0), (1, 0), (1, 1), (0, 2), (1, 2)], [(0, 2), (1, 2), (1, 3), (1, 0), (1, 1)]]
    for holder in range(2):

        @pl.when((col == 0) & (plane == 0) & (line == 0) & (core == holder))
        def _():
            for index, (down, right) in enumerate(places[holder]):
                for part in range(4):
                    rows = slice(down * HALF + part * 32, down * HALF + part * 32 + 32)
                    out_ref[index * 32 : index * 32 + 32, part * HALF : part * HALF + HALF] = lead_ref[
                        rows, right * HALF : right * HALF + HALF
                    ]


def merge_kernel(*refs):
    parts, blocks, out_ref = refs[:4], refs[4:8], refs[8]
    for index, ref in enumerate(parts):

        @pl.when(lax.axis_index("col") == index)
        def _():
            out_ref[:32] = ref[0]
            out_ref[32:64] = ref[1]

    out_ref[64:] = (blocks[0][...] + blocks[1][...]) + (blocks[2][...] + blocks[3][...])


def join_kernel(own_ref, got_ref, *outs):
    rows = own_ref.shape[0] - BLOCK
    outs[0][:rows] = own_ref[:rows]
    outs[0][rows : 2 * rows] = got_ref[:rows]
    block = own_ref[rows:] + got_ref[rows:]
    if len(outs) == 1:
        outs[0][2 * rows :] = block
    else:
        outs[1][...] = block


def pick_kernel(map_ref, front_ref, *refs):
    outs, plan_ref = refs[:4], refs[4]
    col = lax.axis_index("col")
    row = lax.axis_index("row")
    for group in range(4):
        owners, ranks = owners_and_ranks(map_ref, group)

        @pl.when(col == group)
        def _():
            for tile in range(8):
                for hop in range(4):

                    @pl.when((owners[tile] - col) % 4 == hop)
                    def _():
                        column = pl.multiple_of(ranks[tile] * PW, PW)
                        outs[hop][:, pl.ds(column, PW)] = front_ref[:, tile * PW : (tile + 1) * PW]

        for tile in range(8):
            slot = map_ref[8 * group + tile] % 8

            @pl.when(owners[tile] == col)
            def _():
                plan_ref[0, slot] = (col - group) % 4
                plan_ref[1, slot] = jnp.int32(group)
                plan_ref[2, slot] = ranks[tile]
                plan_ref[3, slot] = ((row >= 2) & (8 * group + tile >= 2)).astype(jnp.int32)


def weight_kernel(*refs):
    rows, inverse = refs[:4], refs[4:7]
    panel_ref, weight_ref, rows_ref = refs[7:]
    for index, ref in enumerate(rows):

        @pl.when(lax.axis_index("col") == index)
        def _():
            rows_ref[...] = ref[...]

    inv_a, across, inv_b = [ref[...] for ref in inverse]
    panel_a = dot(rows_ref[:, :PW], inv_a, 1, 1)
    panel_b = dot(rows_ref[:, PW:] - dot(panel_a, across, 1, 1), inv_b, 1, 1)
    weight_b = dot(panel_b, inv_b, 1, 0)
    panel_ref[:, :PW] = panel_a
    panel_ref[:, PW:] = jnp.where(lax.axis_index("row") == 0, 0.0, panel_b)
    weight_ref[:, :PW] = dot(panel_a - dot(weight_b, across, 1, 0), inv_a, 1, 0)
    weight_ref[:, PW:] = weight_b


def weigh(rows, inverse):
    whole = pl.BlockSpec(memory_space=pltpu.VMEM)
    shape = (rows[0].shape[0], LEAD)
    return pl.pallas_call(
        weight_kernel,
        out_shape=[jax.ShapeDtypeStruct(shape, jnp.float32)] * 2,
        in_specs=[whole] * 7,
        out_specs=[whole] * 2,
        scratch_shapes=[pltpu.VMEM(shape, jnp.float32)],
        compiler_params=pltpu.CompilerParams(vmem_limit_bytes=16 << 20),
        cost_estimate=SMALL,
        name="weigh",
    )(*rows, *inverse)


def update_kernel(plan, *refs):
    weight_ref, pieces, gathered = refs[0], refs[1:5], refs[5:9]
    base_ref, out_ref, ahead_ref = refs[9:]
    slot = pl.program_id(0)
    plane, line, core, _ = position()
    group, place = plan[1, slot], plan[2, slot]
    for parity in range(2):
        holder = core if parity == 0 else 1 - core
        for x in range(4):
            off_z, off_x = plane ^ group, line ^ x
            first = jnp.where(holder == 0, off_x, off_z)
            second = jnp.where(holder == 0, off_z, off_x)
            index = ((first & 1) ^ (first >> 1)) + 2 * (first >> 1) + 4 * ((second & 1) ^ (second >> 1))
            rows = pl.ds(pl.multiple_of(index * 64 + place * 32, 32), 32)
            into = pl.ds(pl.multiple_of((2 * x + holder) * 32, 32), 32)
            for late in range(2):

                @pl.when((second >> 1) == late)
                def _():
                    ahead_ref[into, :] = gathered[2 * parity + late][rows, :]

    product = dot(weight_ref[...], ahead_ref[...], 1, 1)
    column = pl.multiple_of(place * PW, PW)
    base = base_ref[...]
    out_ref[...] = base
    for index, ref in enumerate(pieces):

        @pl.when((plan[0, slot] == index) & (plan[3, slot] == 1))
        def _():
            out_ref[...] = base + (ref[:, pl.ds(column, PW)] - product)


def update(plan, weight, pieces, gathered, base):
    height, width = base.shape
    whole = pl.BlockSpec(memory_space=pltpu.VMEM)
    tile = pl.BlockSpec((height, PW), lambda u, plan: (0, u))
    return pl.pallas_call(
        update_kernel,
        out_shape=jax.ShapeDtypeStruct(base.shape, jnp.float32),
        grid_spec=pltpu.PrefetchScalarGridSpec(
            num_scalar_prefetch=1,
            grid=(width // PW,),
            in_specs=[whole] * 9 + [tile],
            out_specs=tile,
            scratch_shapes=[pltpu.VMEM((PW, LEAD), jnp.float32)],
        ),
        compiler_params=pltpu.CompilerParams(vmem_limit_bytes=16 << 20),
        name="update",
    )(plan, weight, *pieces, *gathered, base)


def doubling_steps():
    every, spread = [], []
    have = [{(0, 0)}, {(0, 0)}]
    for step in range(4):
        flip = 1 if step % 2 == 0 else 3
        pairs = []
        for z in range(4):
            for x in range(4):
                for core in range(2):
                    to = (z, x ^ flip) if step // 2 == core else (z ^ flip, x)
                    pairs.append(((z * 4 + x) * 2 + core, (to[0] * 4 + to[1]) * 2 + core, (z, x), to, core))
        every.append([pair[:2] for pair in pairs])
        spread.append([pair[:2] for pair in pairs if pair[2] in have[pair[4]]])
        for core in range(2):
            have[core] |= {pair[3] for pair in pairs if pair[4] == core and pair[2] in have[core]}
    return every, spread


def shards(front, ancestor, tile_map):
    height = front.shape[0]
    swap = [(i, i ^ 1) for i in range(32)]
    part = (2, 32, LEAD)
    lead = front[:, :LEAD]

    ring = [[(i, (i + hop) % 4) for i in range(4)] for hop in range(4)]

    blocks = [local_call(corner_kernel, "corner", [(BLOCK, LEAD)])(lead)[0]]
    for to in range(1, 4):
        blocks.append(lax.ppermute(blocks[0], ("row", "col"), [(4 * core, 4 * core + to) for core in range(2)]))

    mate = lax.ppermute(lead, "row", swap)
    parts = list(local_call(share_kernel, "share", [part] * 4)(lead, mate))
    for hop in range(1, 4):
        pairs = [(z * 8 + x * 2 + k, z * 8 + (x + hop) % 4 * 2 + k) for z in range(4) for x in range(4) for k in range(2)]
        parts[hop] = lax.ppermute(parts[hop], "row", pairs)
    parts = list(local_call(sort_kernel, "sort", [part] * 4, 1)(tile_map, *parts))
    for to in range(1, 4):
        parts[to] = lax.ppermute(parts[to], "col", [(0, to)])
    blocks, parts = lax.optimization_barrier((blocks, parts))
    load = local_call(merge_kernel, "merge", [(64 + BLOCK, LEAD)])(*parts, *blocks)[0]

    *pieces, plan = local_call(pick_kernel, "pick", [(height, 2 * PW)] * 4, 1, [(4, 8)])(tile_map, front)

    every, spread = doubling_steps()
    load, lead = lax.optimization_barrier((load, lead))
    copies = [lax.ppermute(lead, "col", [(0, to)]) for to in (1, 2, 3)]
    load = local_call(join_kernel, "join", [(128 + BLOCK, LEAD)])(load, lax.ppermute(load, "row", every[0]))[0]
    load = local_call(join_kernel, "join", [(256 + BLOCK, LEAD)])(load, lax.ppermute(load, "row", every[1]))[0]
    load, copies[0], copies[2], *pieces = lax.optimization_barrier((load, copies[0], copies[2], *pieces))
    gathered, block = local_call(join_kernel, "join", [(512, LEAD), (BLOCK, LEAD)])(load, lax.ppermute(load, "row", every[2]))
    block, gathered, copies[1] = lax.optimization_barrier((block, gathered, copies[1]))
    block = block + lax.ppermute(block, "row", spread[3])
    pieces[3] = lax.ppermute(pieces[3], "col", ring[3])
    block, gathered, *pieces = lax.optimization_barrier((block, gathered, *pieces))
    other = lax.ppermute(block, "row", swap)
    late = lax.ppermute(gathered, "row", every[3])
    other_gathered = lax.ppermute(gathered, "row", swap)
    for hop in (1, 2):
        pieces[hop] = lax.ppermute(pieces[hop], "col", ring[hop])

    inverse = factor(block, other)
    late, inverse = lax.optimization_barrier((late, inverse))
    other_late = lax.ppermute(late, "row", swap)
    inverse, pieces = lax.optimization_barrier((inverse, pieces))
    panel, weight = weigh([lead, *copies], inverse)
    updated = update(plan, weight, pieces, [gathered, late, other_gathered, other_late], ancestor)
    return panel, updated


def solution(mesh):
    return jax.shard_map(
        shards,
        mesh=mesh,
        in_specs=(P("row", "col"), P("row", "col"), P()),
        out_specs=(P("row", None), P("row", "col")),
        check_vma=False,
    )
```

```python
import jax
import jax.numpy as jnp
from jax import lax
from jax.experimental import pallas as pl
from jax.experimental.pallas import tpu as pltpu
from jax.sharding import PartitionSpec as P

PW = 256
LEAD = 512
HALF = 128
STEP = 8
TURN = 2
BLOCK = 160
LARGE = pl.CostEstimate(flops=20 << 30, bytes_accessed=1 << 20, transcendentals=0)
SMALL = pl.CostEstimate(flops=1 << 10, bytes_accessed=1 << 10, transcendentals=0)
HIGHEST = lax.Precision.HIGHEST


def dot(a, b, ca, cb):
    return lax.dot_general(
        a, b, (((ca,), (cb,)), ((), ())), precision=HIGHEST, preferred_element_type=jnp.float32
    )


def spread_lane(rows, index):
    return jnp.broadcast_to(rows[:, index : index + 1], rows.shape)


def spread_row(rows, index):
    return jnp.broadcast_to(rows[index : index + 1, :], rows.shape)


def inverse_factor_128(square):
    n = HALF
    lane = lax.broadcasted_iota(jnp.int32, (STEP, n), 1)
    sub = lax.broadcasted_iota(jnp.int32, (STEP, n), 0)
    lane_turn = lax.broadcasted_iota(jnp.int32, (TURN * STEP, n), 1)
    count = n // STEP
    groups = [square[STEP * t : STEP * (t + 1), :] for t in range(count)]
    for turn in range(0, count, TURN):
        for step in range(turn, turn + TURN):
            start = STEP * step
            inside = (lane >= start) & (lane < start + STEP)
            top = groups[step]
            columns = [spread_lane(top, start + i) for i in range(STEP)]
            entry = [[spread_row(columns[i], j) if i <= j else None for i in range(STEP)] for j in range(STEP)]
            top = jnp.where(inside, jnp.where(lane - start == sub, 1.0, 0.0), top)
            rows = [spread_row(top, j) for j in range(STEP)]
            near = range(step + 1, min(turn + 2 * TURN, count))
            beside = {t: [spread_lane(groups[t], start + i) for i in range(STEP)] for t in near}
            for t in near:
                groups[t] = jnp.where(inside, 0.0, groups[t])
            done = [None] * STEP
            for i in range(STEP):
                scale = lax.rsqrt(entry[i][i])
                below = [None] * STEP
                for j in range(i + 1, STEP):
                    below[j] = entry[j][i] * scale
                    for k in range(i + 1, j + 1):
                        entry[j][k] = entry[j][k] - below[j] * below[k]
                done[i] = rows[i] * scale
                for j in range(i + 1, STEP):
                    rows[j] = rows[j] - below[j] * done[i]
                for t in near:
                    column = beside[t][i] * scale
                    for k in range(i + 1, STEP):
                        beside[t][k] = beside[t][k] - column * below[k]
                    groups[t] = groups[t] - column * done[i]
            solved = done[0]
            for i in range(1, STEP):
                solved = jnp.where(sub == i, done[i], solved)
            for t in range(step):
                groups[t] = jnp.where(inside, 0.0, groups[t])
            groups[step] = solved
        far = range(turn + 2 * TURN, count)
        if far:
            start, end = STEP * turn, STEP * (turn + TURN)
            solved = jnp.concatenate(groups[turn : turn + TURN], 0)
            ahead = jnp.where(lane_turn >= end + STEP * TURN, solved, 0.0)
            product = dot(ahead, solved, 0, 0)
            inside = (lane >= start) & (lane < end)
            for t in far:
                groups[t] = jnp.where(inside, 0.0, groups[t]) - product[STEP * t : STEP * (t + 1), :]
    return jnp.concatenate(groups, 0)


def inverse_factor_256(top, left, bottom):
    first = inverse_factor_128(top)
    across = dot(left, first, 1, 1)
    second = inverse_factor_128(bottom - dot(across, across, 1, 1))
    lower = -dot(second, dot(across, first, 1, 0), 1, 0)
    return jnp.concatenate(
        [
            jnp.concatenate([first, jnp.zeros_like(first)], 1),
            jnp.concatenate([lower, second], 1),
        ],
        0,
    )


def local_call(kernel, name, shapes, scalars=0, plan=(), cost=SMALL):
    whole = pl.BlockSpec(memory_space=pltpu.VMEM)
    small = pl.BlockSpec(memory_space=pltpu.SMEM)

    def call(*args):
        return pl.pallas_call(
            kernel,
            out_shape=[jax.ShapeDtypeStruct(shape, jnp.float32) for shape in shapes]
            + [jax.ShapeDtypeStruct(shape, jnp.int32) for shape in plan],
            in_specs=[small] * scalars + [whole] * (len(args) - scalars),
            out_specs=[whole] * len(shapes) + [small] * len(plan),
            compiler_params=pltpu.CompilerParams(vmem_limit_bytes=16 << 20),
            cost_estimate=cost,
            name=name,
        )(*args)

    return call


def position():
    row = lax.axis_index("row")
    return row // 8, (row // 2) % 4, row % 2, lax.axis_index("col")


def factor_kernel(own_ref, other_ref, inv_a_ref, across_ref, inv_b_ref):
    even = lax.axis_index("row") % 2 == 0
    own, other = own_ref[...], other_ref[...]
    zero = jnp.where(even, own, other)
    one = jnp.where(even, other, own)

    def piece(blocks, index):
        rows = blocks[index * 32 : (index + 1) * 32]
        return jnp.concatenate([rows[:, part * HALF : (part + 1) * HALF] for part in range(4)], 0)

    inv_a = inverse_factor_256(piece(zero, 0), piece(zero, 1), piece(zero, 2))
    across = jnp.concatenate(
        [
            dot(jnp.concatenate([piece(zero, 3), piece(zero, 4)], 0), inv_a, 0, 1),
            dot(jnp.concatenate([piece(one, 3), piece(one, 4)], 1), inv_a, 1, 1),
        ],
        0,
    )
    square = dot(across, across, 1, 1)
    inv_b = inverse_factor_256(
        piece(one, 0) - square[:HALF, :HALF],
        piece(one, 1) - square[HALF:, :HALF],
        piece(one, 2) - square[HALF:, HALF:],
    )
    inv_a_ref[...] = inv_a
    across_ref[...] = across
    inv_b_ref[...] = inv_b


def factor(own, other):
    return local_call(factor_kernel, "factor", [(PW, PW)] * 3, cost=LARGE)(own, other)


def share_kernel(lead_ref, mate_ref, *outs):
    _, line, core, _ = position()
    for hop in range(4):
        rows = pl.ds(pl.multiple_of(32 * (2 * ((line + hop) % 4) + core), 32), 32)
        for parity in range(2):

            @pl.when(core == parity)
            def _():
                outs[hop][parity] = lead_ref[rows, :]
                outs[hop][1 - parity] = mate_ref[rows, :]


def owners_and_ranks(map_ref, group):
    owners = [map_ref[8 * group + t] // 8 for t in range(8)]
    ranks = [sum((owners[p] == owners[t]).astype(jnp.int32) for p in range(t)) + jnp.int32(0) for t in range(8)]
    return owners, ranks


def sort_kernel(map_ref, *refs):
    ins, outs = refs[:4], refs[4:]
    plane, line, _, _ = position()
    owners, ranks = owners_and_ranks(map_ref, plane)
    for tile in range(8):
        for hop in range(4):

            @pl.when((line - tile // 2) % 4 == hop)
            def _():
                piece = ins[hop][tile % 2]
                for owner in range(4):

                    @pl.when(owners[tile] == owner)
                    def _():
                        outs[owner][pl.ds(ranks[tile], 1)] = piece[None]


def corner_kernel(lead_ref, out_ref):
    plane, line, core, col = position()
    out_ref[...] = jnp.zeros_like(out_ref)
    places = [[(0, 0), (1, 0), (1, 1), (0, 2), (1, 2)], [(0, 2), (1, 2), (1, 3), (1, 0), (1, 1)]]
    for holder in range(2):

        @pl.when((col == 0) & (plane == 0) & (line == 0) & (core == holder))
        def _():
            for index, (down, right) in enumerate(places[holder]):
                for part in range(4):
                    rows = slice(down * HALF + part * 32, down * HALF + part * 32 + 32)
                    out_ref[index * 32 : index * 32 + 32, part * HALF : part * HALF + HALF] = lead_ref[
                        rows, right * HALF : right * HALF + HALF
                    ]


def merge_kernel(*refs):
    parts, blocks, out_ref = refs[:4], refs[4:8], refs[8]
    for index, ref in enumerate(parts):

        @pl.when(lax.axis_index("col") == index)
        def _():
            out_ref[:32] = ref[0]
            out_ref[32:64] = ref[1]

    out_ref[64:] = (blocks[0][...] + blocks[1][...]) + (blocks[2][...] + blocks[3][...])


def join_kernel(own_ref, got_ref, *outs):
    rows = own_ref.shape[0] - BLOCK
    outs[0][:rows] = own_ref[:rows]
    outs[0][rows : 2 * rows] = got_ref[:rows]
    block = own_ref[rows:] + got_ref[rows:]
    if len(outs) == 1:
        outs[0][2 * rows :] = block
    else:
        outs[1][...] = block


def pick_kernel(map_ref, front_ref, *refs):
    outs, plan_ref = refs[:4], refs[4]
    col = lax.axis_index("col")
    row = lax.axis_index("row")
    for group in range(4):
        owners, ranks = owners_and_ranks(map_ref, group)

        @pl.when(col == group)
        def _():
            for tile in range(8):
                for hop in range(4):

                    @pl.when((owners[tile] - col) % 4 == hop)
                    def _():
                        column = pl.multiple_of(ranks[tile] * PW, PW)
                        outs[hop][:, pl.ds(column, PW)] = front_ref[:, tile * PW : (tile + 1) * PW]

        for tile in range(8):
            slot = map_ref[8 * group + tile] % 8

            @pl.when(owners[tile] == col)
            def _():
                plan_ref[0, slot] = (col - group) % 4
                plan_ref[1, slot] = jnp.int32(group)
                plan_ref[2, slot] = ranks[tile]
                plan_ref[3, slot] = ((row >= 2) & (8 * group + tile >= 2)).astype(jnp.int32)


def weight_kernel(*refs):
    rows, inverse = refs[:4], refs[4:7]
    panel_ref, weight_ref, rows_ref = refs[7:]
    for index, ref in enumerate(rows):

        @pl.when(lax.axis_index("col") == index)
        def _():
            rows_ref[...] = ref[...]

    inv_a, across, inv_b = [ref[...] for ref in inverse]
    panel_a = dot(rows_ref[:, :PW], inv_a, 1, 1)
    panel_b = dot(rows_ref[:, PW:] - dot(panel_a, across, 1, 1), inv_b, 1, 1)
    weight_b = dot(panel_b, inv_b, 1, 0)
    panel_ref[:, :PW] = panel_a
    panel_ref[:, PW:] = jnp.where(lax.axis_index("row") == 0, 0.0, panel_b)
    weight_ref[:, :PW] = dot(panel_a - dot(weight_b, across, 1, 0), inv_a, 1, 0)
    weight_ref[:, PW:] = weight_b


def weigh(rows, inverse):
    whole = pl.BlockSpec(memory_space=pltpu.VMEM)
    shape = (rows[0].shape[0], LEAD)
    return pl.pallas_call(
        weight_kernel,
        out_shape=[jax.ShapeDtypeStruct(shape, jnp.float32)] * 2,
        in_specs=[whole] * 7,
        out_specs=[whole] * 2,
        scratch_shapes=[pltpu.VMEM(shape, jnp.float32)],
        compiler_params=pltpu.CompilerParams(vmem_limit_bytes=16 << 20),
        cost_estimate=SMALL,
        name="weigh",
    )(*rows, *inverse)


def update_kernel(plan, *refs):
    weight_ref, pieces, gathered = refs[0], refs[1:5], refs[5:9]
    base_ref, out_ref, ahead_ref = refs[9:]
    slot = pl.program_id(0)
    plane, line, core, _ = position()
    group, place = plan[1, slot], plan[2, slot]
    for parity in range(2):
        holder = core if parity == 0 else 1 - core
        for x in range(4):
            off_z, off_x = plane ^ group, line ^ x
            first = jnp.where(holder == 0, off_x, off_z)
            second = jnp.where(holder == 0, off_z, off_x)
            index = ((first & 1) ^ (first >> 1)) + 2 * (first >> 1) + 4 * ((second & 1) ^ (second >> 1))
            rows = pl.ds(pl.multiple_of(index * 64 + place * 32, 32), 32)
            into = pl.ds(pl.multiple_of((2 * x + holder) * 32, 32), 32)
            for late in range(2):

                @pl.when((second >> 1) == late)
                def _():
                    ahead_ref[into, :] = gathered[2 * parity + late][rows, :]

    product = dot(weight_ref[...], ahead_ref[...], 1, 1)
    column = pl.multiple_of(place * PW, PW)
    base = base_ref[...]
    out_ref[...] = base
    for index, ref in enumerate(pieces):

        @pl.when((plan[0, slot] == index) & (plan[3, slot] == 1))
        def _():
            out_ref[...] = base + (ref[:, pl.ds(column, PW)] - product)


def update(plan, weight, pieces, gathered, base):
    height, width = base.shape
    whole = pl.BlockSpec(memory_space=pltpu.VMEM)
    tile = pl.BlockSpec((height, PW), lambda u, plan: (0, u))
    return pl.pallas_call(
        update_kernel,
        out_shape=jax.ShapeDtypeStruct(base.shape, jnp.float32),
        grid_spec=pltpu.PrefetchScalarGridSpec(
            num_scalar_prefetch=1,
            grid=(width // PW,),
            in_specs=[whole] * 9 + [tile],
            out_specs=tile,
            scratch_shapes=[pltpu.VMEM((PW, LEAD), jnp.float32)],
        ),
        compiler_params=pltpu.CompilerParams(vmem_limit_bytes=16 << 20),
        name="update",
    )(plan, weight, *pieces, *gathered, base)


def doubling_steps():
    every, spread = [], []
    have = [{(0, 0)}, {(0, 0)}]
    for step in range(4):
        flip = 1 if step % 2 == 0 else 3
        pairs = []
        for z in range(4):
            for x in range(4):
                for core in range(2):
                    to = (z, x ^ flip) if step // 2 == core else (z ^ flip, x)
                    pairs.append(((z * 4 + x) * 2 + core, (to[0] * 4 + to[1]) * 2 + core, (z, x), to, core))
        every.append([pair[:2] for pair in pairs])
        spread.append([pair[:2] for pair in pairs if pair[2] in have[pair[4]]])
        for core in range(2):
            have[core] |= {pair[3] for pair in pairs if pair[4] == core and pair[2] in have[core]}
    return every, spread


def shards(front, ancestor, tile_map):
    height = front.shape[0]
    swap = [(i, i ^ 1) for i in range(32)]
    part = (2, 32, LEAD)
    lead = front[:, :LEAD]

    ring = [[(i, (i + hop) % 4) for i in range(4)] for hop in range(4)]

    blocks = [local_call(corner_kernel, "corner", [(BLOCK, LEAD)])(lead)[0]]
    for to in range(1, 4):
        blocks.append(lax.ppermute(blocks[0], ("row", "col"), [(4 * core, 4 * core + to) for core in range(2)]))

    mate = lax.ppermute(lead, "row", swap)
    parts = list(local_call(share_kernel, "share", [part] * 4)(lead, mate))
    for hop in range(1, 4):
        pairs = [(z * 8 + x * 2 + k, z * 8 + (x + hop) % 4 * 2 + k) for z in range(4) for x in range(4) for k in range(2)]
        parts[hop] = lax.ppermute(parts[hop], "row", pairs)
    parts = list(local_call(sort_kernel, "sort", [part] * 4, 1)(tile_map, *parts))
    for to in range(1, 4):
        parts[to] = lax.ppermute(parts[to], "col", [(0, to)])
    blocks, parts = lax.optimization_barrier((blocks, parts))
    load = local_call(merge_kernel, "merge", [(64 + BLOCK, LEAD)])(*parts, *blocks)[0]

    *pieces, plan = local_call(pick_kernel, "pick", [(height, 2 * PW)] * 4, 1, [(4, 8)])(tile_map, front)

    every, spread = doubling_steps()
    load, lead = lax.optimization_barrier((load, lead))
    copies = [lax.ppermute(lead, "col", [(0, to)]) for to in (1, 2, 3)]
    load = local_call(join_kernel, "join", [(128 + BLOCK, LEAD)])(load, lax.ppermute(load, "row", every[0]))[0]
    load = local_call(join_kernel, "join", [(256 + BLOCK, LEAD)])(load, lax.ppermute(load, "row", every[1]))[0]
    load, copies[0], copies[2], *pieces = lax.optimization_barrier((load, copies[0], copies[2], *pieces))
    gathered, block = local_call(join_kernel, "join", [(512, LEAD), (BLOCK, LEAD)])(load, lax.ppermute(load, "row", every[2]))
    block, gathered, copies[1] = lax.optimization_barrier((block, gathered, copies[1]))
    block = block + lax.ppermute(block, "row", spread[3])
    pieces[3] = lax.ppermute(pieces[3], "col", ring[3])
    block, gathered, *pieces = lax.optimization_barrier((block, gathered, *pieces))
    other = lax.ppermute(block, "row", swap)
    late = lax.ppermute(gathered, "row", every[3])
    for hop in (1, 2):
        pieces[hop] = lax.ppermute(pieces[hop], "col", ring[hop])

    inverse = factor(block, other)
    late, gathered, inverse, pieces = lax.optimization_barrier((late, gathered, inverse, pieces))
    other_late = lax.ppermute(late, "row", swap)
    other_gathered = lax.ppermute(gathered, "row", swap)
    panel, weight = weigh([lead, *copies], inverse)
    updated = update(plan, weight, pieces, [gathered, late, other_gathered, other_late], ancestor)
    return panel, updated


def solution(mesh):
    return jax.shard_map(
        shards,
        mesh=mesh,
        in_specs=(P("row", "col"), P("row", "col"), P()),
        out_specs=(P("row", None), P("row", "col")),
        check_vma=False,
    )
```

```python
import jax
import jax.numpy as jnp
from jax import lax
from jax.experimental import pallas as pl
from jax.experimental.pallas import tpu as pltpu
from jax.sharding import PartitionSpec as P

PW = 256
LEAD = 512
HALF = 128
STEP = 8
TURN = 2
BLOCK = 160
LARGE = pl.CostEstimate(flops=20 << 30, bytes_accessed=1 << 20, transcendentals=0)
SMALL = pl.CostEstimate(flops=1 << 10, bytes_accessed=1 << 10, transcendentals=0)
HIGHEST = lax.Precision.HIGHEST


def dot(a, b, ca, cb):
    return lax.dot_general(
        a, b, (((ca,), (cb,)), ((), ())), precision=HIGHEST, preferred_element_type=jnp.float32
    )


def spread_lane(rows, index):
    return jnp.broadcast_to(rows[:, index : index + 1], rows.shape)


def spread_row(rows, index):
    return jnp.broadcast_to(rows[index : index + 1, :], rows.shape)


def inverse_factor_128(square):
    n = HALF
    lane = lax.broadcasted_iota(jnp.int32, (STEP, n), 1)
    sub = lax.broadcasted_iota(jnp.int32, (STEP, n), 0)
    lane_turn = lax.broadcasted_iota(jnp.int32, (TURN * STEP, n), 1)
    count = n // STEP
    groups = [square[STEP * t : STEP * (t + 1), :] for t in range(count)]
    for turn in range(0, count, TURN):
        for step in range(turn, turn + TURN):
            start = STEP * step
            inside = (lane >= start) & (lane < start + STEP)
            top = groups[step]
            columns = [spread_lane(top, start + i) for i in range(STEP)]
            entry = [[spread_row(columns[i], j) if i <= j else None for i in range(STEP)] for j in range(STEP)]
            top = jnp.where(inside, jnp.where(lane - start == sub, 1.0, 0.0), top)
            rows = [spread_row(top, j) for j in range(STEP)]
            near = range(step + 1, min(turn + 2 * TURN, count))
            beside = {t: [spread_lane(groups[t], start + i) for i in range(STEP)] for t in near}
            for t in near:
                groups[t] = jnp.where(inside, 0.0, groups[t])
            done = [None] * STEP
            for i in range(STEP):
                scale = lax.rsqrt(entry[i][i])
                below = [None] * STEP
                for j in range(i + 1, STEP):
                    below[j] = entry[j][i] * scale
                    for k in range(i + 1, j + 1):
                        entry[j][k] = entry[j][k] - below[j] * below[k]
                done[i] = rows[i] * scale
                for j in range(i + 1, STEP):
                    rows[j] = rows[j] - below[j] * done[i]
                for t in near:
                    column = beside[t][i] * scale
                    for k in range(i + 1, STEP):
                        beside[t][k] = beside[t][k] - column * below[k]
                    groups[t] = groups[t] - column * done[i]
            solved = done[0]
            for i in range(1, STEP):
                solved = jnp.where(sub == i, done[i], solved)
            for t in range(step):
                groups[t] = jnp.where(inside, 0.0, groups[t])
            groups[step] = solved
        far = range(turn + 2 * TURN, count)
        if far:
            start, end = STEP * turn, STEP * (turn + TURN)
            solved = jnp.concatenate(groups[turn : turn + TURN], 0)
            ahead = jnp.where(lane_turn >= end + STEP * TURN, solved, 0.0)
            product = dot(ahead, solved, 0, 0)
            inside = (lane >= start) & (lane < end)
            for t in far:
                groups[t] = jnp.where(inside, 0.0, groups[t]) - product[STEP * t : STEP * (t + 1), :]
    return jnp.concatenate(groups, 0)


def inverse_factor_256(top, left, bottom):
    first = inverse_factor_128(top)
    across = dot(left, first, 1, 1)
    second = inverse_factor_128(bottom - dot(across, across, 1, 1))
    lower = -dot(second, dot(across, first, 1, 0), 1, 0)
    return jnp.concatenate(
        [
            jnp.concatenate([first, jnp.zeros_like(first)], 1),
            jnp.concatenate([lower, second], 1),
        ],
        0,
    )


def local_call(kernel, name, shapes, scalars=0, plan=(), cost=SMALL):
    whole = pl.BlockSpec(memory_space=pltpu.VMEM)
    small = pl.BlockSpec(memory_space=pltpu.SMEM)

    def call(*args):
        return pl.pallas_call(
            kernel,
            out_shape=[jax.ShapeDtypeStruct(shape, jnp.float32) for shape in shapes]
            + [jax.ShapeDtypeStruct(shape, jnp.int32) for shape in plan],
            in_specs=[small] * scalars + [whole] * (len(args) - scalars),
            out_specs=[whole] * len(shapes) + [small] * len(plan),
            compiler_params=pltpu.CompilerParams(vmem_limit_bytes=16 << 20),
            cost_estimate=cost,
            name=name,
        )(*args)

    return call


def position():
    row = lax.axis_index("row")
    return row // 8, (row // 2) % 4, row % 2, lax.axis_index("col")


def factor_kernel(own_ref, other_ref, inv_a_ref, across_ref, inv_b_ref):
    even = lax.axis_index("row") % 2 == 0
    own, other = own_ref[...], other_ref[...]
    zero = jnp.where(even, own, other)
    one = jnp.where(even, other, own)

    def piece(blocks, index):
        rows = blocks[index * 32 : (index + 1) * 32]
        return jnp.concatenate([rows[:, part * HALF : (part + 1) * HALF] for part in range(4)], 0)

    inv_a = inverse_factor_256(piece(zero, 0), piece(zero, 1), piece(zero, 2))
    across = jnp.concatenate(
        [
            dot(jnp.concatenate([piece(zero, 3), piece(zero, 4)], 0), inv_a, 0, 1),
            dot(jnp.concatenate([piece(one, 3), piece(one, 4)], 1), inv_a, 1, 1),
        ],
        0,
    )
    square = dot(across, across, 1, 1)
    inv_b = inverse_factor_256(
        piece(one, 0) - square[:HALF, :HALF],
        piece(one, 1) - square[HALF:, :HALF],
        piece(one, 2) - square[HALF:, HALF:],
    )
    inv_a_ref[...] = inv_a
    across_ref[...] = across
    inv_b_ref[...] = inv_b


def factor(own, other):
    return local_call(factor_kernel, "factor", [(PW, PW)] * 3, cost=LARGE)(own, other)


def share_kernel(lead_ref, mate_ref, *outs):
    _, line, core, _ = position()
    for hop in range(4):
        rows = pl.ds(pl.multiple_of(32 * (2 * ((line + hop) % 4) + core), 32), 32)
        for parity in range(2):

            @pl.when(core == parity)
            def _():
                outs[hop][parity] = lead_ref[rows, :]
                outs[hop][1 - parity] = mate_ref[rows, :]


def owners_and_ranks(map_ref, group):
    owners = [map_ref[8 * group + t] // 8 for t in range(8)]
    ranks = [sum((owners[p] == owners[t]).astype(jnp.int32) for p in range(t)) + jnp.int32(0) for t in range(8)]
    return owners, ranks


def sort_kernel(map_ref, *refs):
    ins, outs = refs[:4], refs[4:]
    plane, line, _, _ = position()
    owners, ranks = owners_and_ranks(map_ref, plane)
    for tile in range(8):
        for hop in range(4):

            @pl.when((line - tile // 2) % 4 == hop)
            def _():
                piece = ins[hop][tile % 2]
                for owner in range(4):

                    @pl.when(owners[tile] == owner)
                    def _():
                        outs[owner][pl.ds(ranks[tile], 1)] = piece[None]


def corner_kernel(lead_ref, out_ref):
    plane, line, core, col = position()
    out_ref[...] = jnp.zeros_like(out_ref)
    places = [[(0, 0), (1, 0), (1, 1), (0, 2), (1, 2)], [(0, 2), (1, 2), (1, 3), (1, 0), (1, 1)]]
    for holder in range(2):

        @pl.when((col == 0) & (plane == 0) & (line == 0) & (core == holder))
        def _():
            for index, (down, right) in enumerate(places[holder]):
                for part in range(4):
                    rows = slice(down * HALF + part * 32, down * HALF + part * 32 + 32)
                    out_ref[index * 32 : index * 32 + 32, part * HALF : part * HALF + HALF] = lead_ref[
                        rows, right * HALF : right * HALF + HALF
                    ]


def merge_kernel(*refs):
    parts, block_ref, got_ref, out_ref = refs[:4], refs[4], refs[5], refs[6]
    for index, ref in enumerate(parts):

        @pl.when(lax.axis_index("col") == index)
        def _():
            out_ref[:32] = ref[0]
            out_ref[32:64] = ref[1]

    out_ref[64:] = block_ref[...] + got_ref[...]


def join_kernel(own_ref, got_ref, *outs):
    rows = own_ref.shape[0] - BLOCK
    outs[0][:rows] = own_ref[:rows]
    outs[0][rows : 2 * rows] = got_ref[:rows]
    block = own_ref[rows:] + got_ref[rows:]
    if len(outs) == 1:
        outs[0][2 * rows :] = block
    else:
        outs[1][...] = block


def pick_kernel(map_ref, front_ref, *refs):
    outs, plan_ref = refs[:4], refs[4]
    col = lax.axis_index("col")
    row = lax.axis_index("row")
    for group in range(4):
        owners, ranks = owners_and_ranks(map_ref, group)

        @pl.when(col == group)
        def _():
            for tile in range(8):
                for hop in range(4):

                    @pl.when((owners[tile] - col) % 4 == hop)
                    def _():
                        column = pl.multiple_of(ranks[tile] * PW, PW)
                        outs[hop][:, pl.ds(column, PW)] = front_ref[:, tile * PW : (tile + 1) * PW]

        for tile in range(8):
            slot = map_ref[8 * group + tile] % 8

            @pl.when(owners[tile] == col)
            def _():
                plan_ref[0, slot] = (col - group) % 4
                plan_ref[1, slot] = jnp.int32(group)
                plan_ref[2, slot] = ranks[tile]
                plan_ref[3, slot] = ((row >= 2) & (8 * group + tile >= 2)).astype(jnp.int32)


def weight_kernel(*refs):
    rows, inverse = refs[:4], refs[4:7]
    panel_ref, weight_ref, rows_ref = refs[7:]
    for index, ref in enumerate(rows):

        @pl.when(lax.axis_index("col") == index)
        def _():
            rows_ref[...] = ref[...]

    inv_a, across, inv_b = [ref[...] for ref in inverse]
    panel_a = dot(rows_ref[:, :PW], inv_a, 1, 1)
    panel_b = dot(rows_ref[:, PW:] - dot(panel_a, across, 1, 1), inv_b, 1, 1)
    weight_b = dot(panel_b, inv_b, 1, 0)
    panel_ref[:, :PW] = panel_a
    panel_ref[:, PW:] = jnp.where(lax.axis_index("row") == 0, 0.0, panel_b)
    weight_ref[:, :PW] = dot(panel_a - dot(weight_b, across, 1, 0), inv_a, 1, 0)
    weight_ref[:, PW:] = weight_b


def weigh(rows, inverse):
    whole = pl.BlockSpec(memory_space=pltpu.VMEM)
    shape = (rows[0].shape[0], LEAD)
    return pl.pallas_call(
        weight_kernel,
        out_shape=[jax.ShapeDtypeStruct(shape, jnp.float32)] * 2,
        in_specs=[whole] * 7,
        out_specs=[whole] * 2,
        scratch_shapes=[pltpu.VMEM(shape, jnp.float32)],
        compiler_params=pltpu.CompilerParams(vmem_limit_bytes=16 << 20),
        cost_estimate=SMALL,
        name="weigh",
    )(*rows, *inverse)


def update_kernel(plan, *refs):
    weight_ref, pieces, gathered = refs[0], refs[1:5], refs[5:9]
    base_ref, out_ref, ahead_ref = refs[9:]
    slot = pl.program_id(0)
    plane, line, core, _ = position()
    group, place = plan[1, slot], plan[2, slot]
    for parity in range(2):
        holder = core if parity == 0 else 1 - core
        for x in range(4):
            off_z, off_x = plane ^ group, line ^ x
            first = jnp.where(holder == 0, off_x, off_z)
            second = jnp.where(holder == 0, off_z, off_x)
            index = (first >> 1) + 2 * ((second & 1) ^ (second >> 1)) + 4 * (second >> 1)
            rows = pl.ds(pl.multiple_of(index * 64 + place * 32, 32), 32)
            into = pl.ds(pl.multiple_of((2 * x + holder) * 32, 32), 32)
            for late in range(2):

                @pl.when(((first & 1) ^ (first >> 1)) == late)
                def _():
                    ahead_ref[into, :] = gathered[2 * parity + late][rows, :]

    product = dot(weight_ref[...], ahead_ref[...], 1, 1)
    column = pl.multiple_of(place * PW, PW)
    base = base_ref[...]
    out_ref[...] = base
    for index, ref in enumerate(pieces):

        @pl.when((plan[0, slot] == index) & (plan[3, slot] == 1))
        def _():
            out_ref[...] = base + (ref[:, pl.ds(column, PW)] - product)


def update(plan, weight, pieces, gathered, base):
    height, width = base.shape
    whole = pl.BlockSpec(memory_space=pltpu.VMEM)
    tile = pl.BlockSpec((height, PW), lambda u, plan: (0, u))
    return pl.pallas_call(
        update_kernel,
        out_shape=jax.ShapeDtypeStruct(base.shape, jnp.float32),
        grid_spec=pltpu.PrefetchScalarGridSpec(
            num_scalar_prefetch=1,
            grid=(width // PW,),
            in_specs=[whole] * 9 + [tile],
            out_specs=tile,
            scratch_shapes=[pltpu.VMEM((PW, LEAD), jnp.float32)],
        ),
        compiler_params=pltpu.CompilerParams(vmem_limit_bytes=16 << 20),
        name="update",
    )(plan, weight, *pieces, *gathered, base)


def doubling_steps():
    every = []
    for step in range(4):
        flip = 1 if step % 2 == 0 else 3
        pairs = []
        for z in range(4):
            for x in range(4):
                for core in range(2):
                    to = (z, x ^ flip) if step // 2 == core else (z ^ flip, x)
                    pairs.append(((z * 4 + x) * 2 + core, (to[0] * 4 + to[1]) * 2 + core))
        every.append(pairs)
    return every, [pair for pair in every[0] if pair[0] < 2]


def shards(front, ancestor, tile_map):
    height = front.shape[0]
    swap = [(i, i ^ 1) for i in range(32)]
    part = (2, 32, LEAD)
    lead = front[:, :LEAD]

    ring = [[(i, (i + hop) % 4) for i in range(4)] for hop in range(4)]

    blocks = [local_call(corner_kernel, "corner", [(BLOCK, LEAD)])(lead)[0]]
    for to in range(1, 4):
        blocks.append(lax.ppermute(blocks[0], ("row", "col"), [(4 * core, 4 * core + to) for core in range(2)]))

    mate = lax.ppermute(lead, "row", swap)
    parts = list(local_call(share_kernel, "share", [part] * 4)(lead, mate))
    for hop in range(1, 4):
        pairs = [(z * 8 + x * 2 + k, z * 8 + (x + hop) % 4 * 2 + k) for z in range(4) for x in range(4) for k in range(2)]
        parts[hop] = lax.ppermute(parts[hop], "row", pairs)
    parts = list(local_call(sort_kernel, "sort", [part] * 4, 1)(tile_map, *parts))
    blocks, parts = lax.optimization_barrier((blocks, parts))

    every, spread = doubling_steps()
    for to in range(1, 4):
        parts[to] = lax.ppermute(parts[to], "col", [(0, to)])
    block = (blocks[0] + blocks[1]) + (blocks[2] + blocks[3])
    got = lax.ppermute(block, "row", spread)
    block, got, parts = lax.optimization_barrier((block, got, parts))
    load = local_call(merge_kernel, "merge", [(64 + BLOCK, LEAD)])(*parts, block, got)[0]

    *pieces, plan = local_call(pick_kernel, "pick", [(height, 2 * PW)] * 4, 1, [(4, 8)])(tile_map, front)

    load, lead = lax.optimization_barrier((load, lead))
    copies = [lax.ppermute(lead, "col", [(0, to)]) for to in (1, 2, 3)]
    load = local_call(join_kernel, "join", [(128 + BLOCK, LEAD)])(load, lax.ppermute(load, "row", every[1]))[0]
    load, copies[0], copies[2], *pieces = lax.optimization_barrier((load, copies[0], copies[2], *pieces))
    load = local_call(join_kernel, "join", [(256 + BLOCK, LEAD)])(load, lax.ppermute(load, "row", every[2]))[0]
    load, copies[1], *pieces = lax.optimization_barrier((load, copies[1], *pieces))
    gathered, block = local_call(join_kernel, "join", [(512, LEAD), (BLOCK, LEAD)])(load, lax.ppermute(load, "row", every[3]))
    for hop in (1, 3):
        pieces[hop] = lax.ppermute(pieces[hop], "col", ring[hop])
    block, gathered, *pieces = lax.optimization_barrier((block, gathered, *pieces))
    other = lax.ppermute(block, "row", swap)
    late = lax.ppermute(gathered, "row", every[0])
    pieces[2] = lax.ppermute(pieces[2], "col", ring[2])

    inverse = factor(block, other)
    late, gathered, inverse, pieces = lax.optimization_barrier((late, gathered, inverse, pieces))
    other_late = lax.ppermute(late, "row", swap)
    other_gathered = lax.ppermute(gathered, "row", swap)
    panel, weight = weigh([lead, *copies], inverse)
    updated = update(plan, weight, pieces, [gathered, late, other_gathered, other_late], ancestor)
    return panel, updated


def solution(mesh):
    return jax.shard_map(
        shards,
        mesh=mesh,
        in_specs=(P("row", "col"), P("row", "col"), P()),
        out_specs=(P("row", None), P("row", "col")),
        check_vma=False,
    )
```

```python
from functools import partial

import jax
import jax.numpy as jnp
from jax import lax
from jax.experimental import pallas as pl
from jax.experimental.pallas import tpu as pltpu
from jax.sharding import PartitionSpec as P

PW = 256
LEAD = 512
HALF = 128
STEP = 8
TURN = 2
BLOCK = 160
PAD = 40
LARGE = pl.CostEstimate(flops=20 << 30, bytes_accessed=1 << 20, transcendentals=0)
SMALL = pl.CostEstimate(flops=1 << 10, bytes_accessed=1 << 10, transcendentals=0)
HIGHEST = lax.Precision.HIGHEST


def dot(a, b, ca, cb):
    return lax.dot_general(
        a, b, (((ca,), (cb,)), ((), ())), precision=HIGHEST, preferred_element_type=jnp.float32
    )


def spread_lane(rows, index):
    return jnp.broadcast_to(rows[:, index : index + 1], rows.shape)


def spread_row(rows, index):
    return jnp.broadcast_to(rows[index : index + 1, :], rows.shape)


def inverse_factor_128(square):
    n = HALF
    lane = lax.broadcasted_iota(jnp.int32, (STEP, n), 1)
    sub = lax.broadcasted_iota(jnp.int32, (STEP, n), 0)
    lane_turn = lax.broadcasted_iota(jnp.int32, (TURN * STEP, n), 1)
    count = n // STEP
    groups = [square[STEP * t : STEP * (t + 1), :] for t in range(count)]
    for turn in range(0, count, TURN):
        for step in range(turn, turn + TURN):
            start = STEP * step
            inside = (lane >= start) & (lane < start + STEP)
            top = groups[step]
            columns = [spread_lane(top, start + i) for i in range(STEP)]
            entry = [[spread_row(columns[i], j) if i <= j else None for i in range(STEP)] for j in range(STEP)]
            top = jnp.where(inside, jnp.where(lane - start == sub, 1.0, 0.0), top)
            rows = [spread_row(top, j) for j in range(STEP)]
            near = range(step + 1, min(turn + 2 * TURN, count))
            beside = {t: [spread_lane(groups[t], start + i) for i in range(STEP)] for t in near}
            for t in near:
                groups[t] = jnp.where(inside, 0.0, groups[t])
            done = [None] * STEP
            for i in range(STEP):
                scale = lax.rsqrt(entry[i][i])
                below = [None] * STEP
                for j in range(i + 1, STEP):
                    below[j] = entry[j][i] * scale
                    for k in range(i + 1, j + 1):
                        entry[j][k] = entry[j][k] - below[j] * below[k]
                done[i] = rows[i] * scale
                for j in range(i + 1, STEP):
                    rows[j] = rows[j] - below[j] * done[i]
                for t in near:
                    column = beside[t][i] * scale
                    for k in range(i + 1, STEP):
                        beside[t][k] = beside[t][k] - column * below[k]
                    groups[t] = groups[t] - column * done[i]
            solved = done[0]
            for i in range(1, STEP):
                solved = jnp.where(sub == i, done[i], solved)
            for t in range(step):
                groups[t] = jnp.where(inside, 0.0, groups[t])
            groups[step] = solved
        far = range(turn + 2 * TURN, count)
        if far:
            start, end = STEP * turn, STEP * (turn + TURN)
            solved = jnp.concatenate(groups[turn : turn + TURN], 0)
            ahead = jnp.where(lane_turn >= end + STEP * TURN, solved, 0.0)
            product = dot(ahead, solved, 0, 0)
            inside = (lane >= start) & (lane < end)
            for t in far:
                groups[t] = jnp.where(inside, 0.0, groups[t]) - product[STEP * t : STEP * (t + 1), :]
    return jnp.concatenate(groups, 0)


def inverse_factor_256(top, left, bottom):
    first = inverse_factor_128(top)
    across = dot(left, first, 1, 1)
    second = inverse_factor_128(bottom - dot(across, across, 1, 1))
    lower = -dot(second, dot(across, first, 1, 0), 1, 0)
    return jnp.concatenate(
        [
            jnp.concatenate([first, jnp.zeros_like(first)], 1),
            jnp.concatenate([lower, second], 1),
        ],
        0,
    )


def local_call(kernel, name, shapes, scalars=0, plan=(), cost=SMALL):
    whole = pl.BlockSpec(memory_space=pltpu.VMEM)
    small = pl.BlockSpec(memory_space=pltpu.SMEM)

    def call(*args):
        return pl.pallas_call(
            kernel,
            out_shape=[jax.ShapeDtypeStruct(shape, jnp.float32) for shape in shapes]
            + [jax.ShapeDtypeStruct(shape, jnp.int32) for shape in plan],
            in_specs=[small] * scalars + [whole] * (len(args) - scalars),
            out_specs=[whole] * len(shapes) + [small] * len(plan),
            compiler_params=pltpu.CompilerParams(vmem_limit_bytes=16 << 20),
            cost_estimate=cost,
            name=name,
        )(*args)

    return call


def position():
    row = lax.axis_index("row")
    return row // 8, (row // 2) % 4, row % 2, lax.axis_index("col")


def factor_kernel(own_ref, other_ref, inv_a_ref, across_ref, inv_b_ref):
    even = lax.axis_index("row") % 2 == 0
    own, other = own_ref[...], other_ref[...]
    zero = jnp.where(even, own, other)
    one = jnp.where(even, other, own)

    def piece(blocks, index):
        rows = blocks[index * 32 : (index + 1) * 32]
        return jnp.concatenate([rows[:, part * HALF : (part + 1) * HALF] for part in range(4)], 0)

    inv_a = inverse_factor_256(piece(zero, 0), piece(zero, 1), piece(zero, 2))
    across = jnp.concatenate(
        [
            dot(jnp.concatenate([piece(zero, 3), piece(zero, 4)], 0), inv_a, 0, 1),
            dot(jnp.concatenate([piece(one, 3), piece(one, 4)], 1), inv_a, 1, 1),
        ],
        0,
    )
    square = dot(across, across, 1, 1)
    inv_b = inverse_factor_256(
        piece(one, 0) - square[:HALF, :HALF],
        piece(one, 1) - square[HALF:, :HALF],
        piece(one, 2) - square[HALF:, HALF:],
    )
    inv_a_ref[...] = inv_a
    across_ref[...] = across
    inv_b_ref[...] = inv_b


def factor(own, other):
    return local_call(factor_kernel, "factor", [(PW, PW)] * 3, cost=LARGE)(own, other)


def share_kernel(lead_ref, mate_ref, *outs):
    _, line, core, _ = position()
    for hop in range(4):
        rows = pl.ds(pl.multiple_of(32 * (2 * ((line + hop) % 4) + core), 32), 32)
        for parity in range(2):

            @pl.when(core == parity)
            def _():
                outs[hop][parity] = lead_ref[rows, :]
                outs[hop][1 - parity] = mate_ref[rows, :]


def owners_and_ranks(map_ref, group):
    owners = [map_ref[8 * group + t] // 8 for t in range(8)]
    ranks = [sum((owners[p] == owners[t]).astype(jnp.int32) for p in range(t)) + jnp.int32(0) for t in range(8)]
    return owners, ranks


def sort_kernel(map_ref, *refs):
    ins, outs = refs[:4], refs[4:]
    plane, line, _, _ = position()
    owners, ranks = owners_and_ranks(map_ref, plane)
    for tile in range(8):
        for hop in range(4):

            @pl.when((line - tile // 2) % 4 == hop)
            def _():
                piece = ins[hop][tile % 2]
                for owner in range(4):

                    @pl.when(owners[tile] == owner)
                    def _():
                        outs[owner][pl.ds(ranks[tile], 1)] = piece[None]


def corner_kernel(lead_ref, out_ref):
    plane, line, core, col = position()
    out_ref[...] = jnp.zeros_like(out_ref)
    places = [[(0, 0), (1, 0), (1, 1), (0, 2), (1, 2)], [(0, 2), (1, 2), (1, 3), (1, 0), (1, 1)]]
    for holder in range(2):

        @pl.when((col == 0) & (plane == 0) & (line == 0) & (core == holder))
        def _():
            for index, (down, right) in enumerate(places[holder]):
                for part in range(4):
                    rows = slice(down * HALF + part * 32, down * HALF + part * 32 + 32)
                    out_ref[index * 32 : index * 32 + 32, part * HALF : part * HALF + HALF] = lead_ref[
                        rows, right * HALF : right * HALF + HALF
                    ]


def merge_kernel(*refs):
    parts, block_ref, got_ref, out_ref = refs[:4], refs[4], refs[5], refs[6]
    for index, ref in enumerate(parts):

        @pl.when(lax.axis_index("col") == index)
        def _():
            out_ref[:32] = ref[0]
            out_ref[32:64] = ref[1]

    out_ref[64 : 64 + BLOCK] = block_ref[...] + got_ref[...]
    out_ref[64 + BLOCK :] = jnp.zeros((PAD, LEAD), jnp.float32)


def join_kernel(rows, own_ref, got_ref, *outs):
    outs[0][:rows] = own_ref[:rows]
    outs[0][rows : 2 * rows] = got_ref[:rows]
    block = own_ref[rows : rows + BLOCK] + got_ref[rows : rows + BLOCK]
    if len(outs) == 1:
        outs[0][2 * rows :] = block
    else:
        outs[1][...] = block


def pick_kernel(map_ref, front_ref, *refs):
    outs, plan_ref = refs[:4], refs[4]
    col = lax.axis_index("col")
    row = lax.axis_index("row")
    for group in range(4):
        owners, ranks = owners_and_ranks(map_ref, group)

        @pl.when(col == group)
        def _():
            for tile in range(8):
                for hop in range(4):

                    @pl.when((owners[tile] - col) % 4 == hop)
                    def _():
                        column = pl.multiple_of(ranks[tile] * PW, PW)
                        outs[hop][:, pl.ds(column, PW)] = front_ref[:, tile * PW : (tile + 1) * PW]

        for tile in range(8):
            slot = map_ref[8 * group + tile] % 8

            @pl.when(owners[tile] == col)
            def _():
                plan_ref[0, slot] = (col - group) % 4
                plan_ref[1, slot] = jnp.int32(group)
                plan_ref[2, slot] = ranks[tile]
                plan_ref[3, slot] = ((row >= 2) & (8 * group + tile >= 2)).astype(jnp.int32)


def weight_kernel(*refs):
    rows, inverse = refs[:3], refs[3:6]
    panel_ref, weight_ref, rows_ref = refs[6:]
    for index, ref in enumerate(rows):

        @pl.when(jnp.minimum(lax.axis_index("col"), 2) == index)
        def _():
            rows_ref[...] = ref[...]

    inv_a, across, inv_b = [ref[...] for ref in inverse]
    panel_a = dot(rows_ref[:, :PW], inv_a, 1, 1)
    panel_b = dot(rows_ref[:, PW:] - dot(panel_a, across, 1, 1), inv_b, 1, 1)
    weight_b = dot(panel_b, inv_b, 1, 0)
    panel_ref[:, :PW] = panel_a
    panel_ref[:, PW:] = jnp.where(lax.axis_index("row") == 0, 0.0, panel_b)
    weight_ref[:, :PW] = dot(panel_a - dot(weight_b, across, 1, 0), inv_a, 1, 0)
    weight_ref[:, PW:] = weight_b


def weigh(rows, inverse):
    whole = pl.BlockSpec(memory_space=pltpu.VMEM)
    shape = (rows[0].shape[0], LEAD)
    return pl.pallas_call(
        weight_kernel,
        out_shape=[jax.ShapeDtypeStruct(shape, jnp.float32)] * 2,
        in_specs=[whole] * 6,
        out_specs=[whole] * 2,
        scratch_shapes=[pltpu.VMEM(shape, jnp.float32)],
        compiler_params=pltpu.CompilerParams(vmem_limit_bytes=16 << 20),
        cost_estimate=SMALL,
        name="weigh",
    )(*rows, *inverse)


def update_kernel(plan, *refs):
    weight_ref, pieces, gathered = refs[0], refs[1:5], refs[5:9]
    base_ref, out_ref, ahead_ref = refs[9:]
    slot = pl.program_id(0)
    plane, line, core, _ = position()
    group, place = plan[1, slot], plan[2, slot]
    for parity in range(2):
        holder = core if parity == 0 else 1 - core
        for x in range(4):
            off_z, off_x = plane ^ group, line ^ x
            first = jnp.where(holder == 0, off_x, off_z)
            second = jnp.where(holder == 0, off_z, off_x)
            index = (first >> 1) + 2 * ((second & 1) ^ (second >> 1)) + 4 * (second >> 1)
            rows = pl.ds(pl.multiple_of(index * 64 + place * 32, 32), 32)
            into = pl.ds(pl.multiple_of((2 * x + holder) * 32, 32), 32)
            for late in range(2):

                @pl.when(((first & 1) ^ (first >> 1)) == late)
                def _():
                    ahead_ref[into, :] = gathered[2 * parity + late][rows, :]

    product = dot(weight_ref[...], ahead_ref[...], 1, 1)
    column = pl.multiple_of(place * PW, PW)
    base = base_ref[...]
    out_ref[...] = base
    for index, ref in enumerate(pieces):

        @pl.when((plan[0, slot] == index) & (plan[3, slot] == 1))
        def _():
            out_ref[...] = base + (ref[:, pl.ds(column, PW)] - product)


def update(plan, weight, pieces, gathered, base):
    height, width = base.shape
    whole = pl.BlockSpec(memory_space=pltpu.VMEM)
    tile = pl.BlockSpec((height, PW), lambda u, plan: (0, u))
    return pl.pallas_call(
        update_kernel,
        out_shape=jax.ShapeDtypeStruct(base.shape, jnp.float32),
        grid_spec=pltpu.PrefetchScalarGridSpec(
            num_scalar_prefetch=1,
            grid=(width // PW,),
            in_specs=[whole] * 9 + [tile],
            out_specs=tile,
            scratch_shapes=[pltpu.VMEM((PW, LEAD), jnp.float32)],
        ),
        compiler_params=pltpu.CompilerParams(vmem_limit_bytes=16 << 20),
        name="update",
    )(plan, weight, *pieces, *gathered, base)


def doubling_steps():
    every = []
    for step in range(4):
        flip = 1 if step % 2 == 0 else 3
        pairs = []
        for z in range(4):
            for x in range(4):
                for core in range(2):
                    to = (z, x ^ flip) if step // 2 == core else (z ^ flip, x)
                    pairs.append(((z * 4 + x) * 2 + core, (to[0] * 4 + to[1]) * 2 + core))
        every.append(pairs)
    return every, [pair for pair in every[0] if pair[0] < 2]


def shards(front, ancestor, tile_map):
    height = front.shape[0]
    swap = [(i, i ^ 1) for i in range(32)]
    part = (2, 32, LEAD)
    lead = front[:, :LEAD]

    ring = [[(i, (i + hop) % 4) for i in range(4)] for hop in range(4)]

    blocks = [local_call(corner_kernel, "corner", [(BLOCK, LEAD)])(lead)[0]]
    for to in range(1, 4):
        blocks.append(lax.ppermute(blocks[0], ("row", "col"), [(4 * core, 4 * core + to) for core in range(2)]))

    mate = lax.ppermute(lead, "row", swap)
    parts = list(local_call(share_kernel, "share", [part] * 4)(lead, mate))
    for hop in range(1, 4):
        pairs = [(i, i // 8 * 8 + (i + 2 * hop) % 8) for i in range(2, 32)]
        parts[hop] = lax.ppermute(parts[hop], "row", pairs)
    parts = list(local_call(sort_kernel, "sort", [part] * 4, 1)(tile_map, *parts))
    blocks, parts = lax.optimization_barrier((blocks, parts))

    every, spread = doubling_steps()
    for to in range(1, 4):
        parts[to] = lax.ppermute(parts[to], "col", [(0, to)])
    block = (blocks[0] + blocks[1]) + (blocks[2] + blocks[3])
    got = lax.ppermute(block, "row", spread)
    block, got, parts = lax.optimization_barrier((block, got, parts))
    load = local_call(merge_kernel, "merge", [(64 + BLOCK + PAD, LEAD)])(*parts, block, got)[0]

    *pieces, plan = local_call(pick_kernel, "pick", [(height, 2 * PW)] * 4, 1, [(4, 8)])(tile_map, front)

    load, lead = lax.optimization_barrier((load, lead))
    near = lax.ppermute(lead, "col", [(0, 1)])
    load = local_call(partial(join_kernel, 64), "join", [(128 + BLOCK, LEAD)])(load, lax.ppermute(load, "row", every[1]))[0]
    load, near, *pieces = lax.optimization_barrier((load, near, *pieces))
    far = lax.ppermute(jnp.where(lax.axis_index("col") == 1, near, lead), "col", [(0, 3), (1, 2)])
    load = local_call(partial(join_kernel, 128), "join", [(256 + BLOCK, LEAD)])(load, lax.ppermute(load, "row", every[2]))[0]
    load, far, *pieces = lax.optimization_barrier((load, far, *pieces))
    gathered, block = local_call(partial(join_kernel, 256), "join", [(512, LEAD), (BLOCK, LEAD)])(
        load, lax.ppermute(load, "row", every[3])
    )
    for hop in (1, 3):
        pieces[hop] = lax.ppermute(pieces[hop], "col", ring[hop])
    block, gathered, *pieces = lax.optimization_barrier((block, gathered, *pieces))
    other = lax.ppermute(block, "row", swap)
    late = lax.ppermute(gathered, "row", every[0])
    pieces[2] = lax.ppermute(pieces[2], "col", ring[2])

    inverse = factor(block, other)
    late, gathered, inverse, pieces = lax.optimization_barrier((late, gathered, inverse, pieces))
    other_late = lax.ppermute(late, "row", swap)
    other_gathered = lax.ppermute(gathered, "row", swap)
    panel, weight = weigh([lead, near, far], inverse)
    updated = update(plan, weight, pieces, [gathered, late, other_gathered, other_late], ancestor)
    return panel, updated


def solution(mesh):
    return jax.shard_map(
        shards,
        mesh=mesh,
        in_specs=(P("row", "col"), P("row", "col"), P()),
        out_specs=(P("row", None), P("row", "col")),
        check_vma=False,
    )
```

```python
from functools import partial

import jax
import jax.numpy as jnp
from jax import lax
from jax.experimental import pallas as pl
from jax.experimental.pallas import tpu as pltpu
from jax.sharding import PartitionSpec as P

PW = 256
LEAD = 512
HALF = 128
STEP = 8
TURN = 2
BLOCK = 160
LARGE = pl.CostEstimate(flops=20 << 30, bytes_accessed=1 << 20, transcendentals=0)
SMALL = pl.CostEstimate(flops=1 << 10, bytes_accessed=1 << 10, transcendentals=0)
HIGHEST = lax.Precision.HIGHEST


def dot(a, b, ca, cb):
    return lax.dot_general(
        a, b, (((ca,), (cb,)), ((), ())), precision=HIGHEST, preferred_element_type=jnp.float32
    )


def spread_lane(rows, index):
    return jnp.broadcast_to(rows[:, index : index + 1], rows.shape)


def spread_row(rows, index):
    return jnp.broadcast_to(rows[index : index + 1, :], rows.shape)


def inverse_factor_128(square):
    n = HALF
    lane = lax.broadcasted_iota(jnp.int32, (STEP, n), 1)
    sub = lax.broadcasted_iota(jnp.int32, (STEP, n), 0)
    lane_turn = lax.broadcasted_iota(jnp.int32, (TURN * STEP, n), 1)
    count = n // STEP
    groups = [square[STEP * t : STEP * (t + 1), :] for t in range(count)]
    for turn in range(0, count, TURN):
        for step in range(turn, turn + TURN):
            start = STEP * step
            inside = (lane >= start) & (lane < start + STEP)
            top = groups[step]
            columns = [spread_lane(top, start + i) for i in range(STEP)]
            entry = [[spread_row(columns[i], j) if i <= j else None for i in range(STEP)] for j in range(STEP)]
            top = jnp.where(inside, jnp.where(lane - start == sub, 1.0, 0.0), top)
            rows = [spread_row(top, j) for j in range(STEP)]
            near = range(step + 1, min(turn + 2 * TURN, count))
            beside = {t: [spread_lane(groups[t], start + i) for i in range(STEP)] for t in near}
            for t in near:
                groups[t] = jnp.where(inside, 0.0, groups[t])
            done = [None] * STEP
            for i in range(STEP):
                scale = lax.rsqrt(entry[i][i])
                below = [None] * STEP
                for j in range(i + 1, STEP):
                    below[j] = entry[j][i] * scale
                    for k in range(i + 1, j + 1):
                        entry[j][k] = entry[j][k] - below[j] * below[k]
                done[i] = rows[i] * scale
                for j in range(i + 1, STEP):
                    rows[j] = rows[j] - below[j] * done[i]
                for t in near:
                    column = beside[t][i] * scale
                    for k in range(i + 1, STEP):
                        beside[t][k] = beside[t][k] - column * below[k]
                    groups[t] = groups[t] - column * done[i]
            solved = done[0]
            for i in range(1, STEP):
                solved = jnp.where(sub == i, done[i], solved)
            for t in range(step):
                groups[t] = jnp.where(inside, 0.0, groups[t])
            groups[step] = solved
        far = range(turn + 2 * TURN, count)
        if far:
            start, end = STEP * turn, STEP * (turn + TURN)
            solved = jnp.concatenate(groups[turn : turn + TURN], 0)
            ahead = jnp.where(lane_turn >= end + STEP * TURN, solved, 0.0)
            product = dot(ahead, solved, 0, 0)
            inside = (lane >= start) & (lane < end)
            for t in far:
                groups[t] = jnp.where(inside, 0.0, groups[t]) - product[STEP * t : STEP * (t + 1), :]
    return jnp.concatenate(groups, 0)


def inverse_factor_256(top, left, bottom):
    first = inverse_factor_128(top)
    across = dot(left, first, 1, 1)
    second = inverse_factor_128(bottom - dot(across, across, 1, 1))
    lower = -dot(second, dot(across, first, 1, 0), 1, 0)
    return jnp.concatenate(
        [
            jnp.concatenate([first, jnp.zeros_like(first)], 1),
            jnp.concatenate([lower, second], 1),
        ],
        0,
    )


def local_call(kernel, name, shapes, scalars=0, plan=(), cost=SMALL):
    whole = pl.BlockSpec(memory_space=pltpu.VMEM)
    small = pl.BlockSpec(memory_space=pltpu.SMEM)

    def call(*args):
        return pl.pallas_call(
            kernel,
            out_shape=[jax.ShapeDtypeStruct(shape, jnp.float32) for shape in shapes]
            + [jax.ShapeDtypeStruct(shape, jnp.int32) for shape in plan],
            in_specs=[small] * scalars + [whole] * (len(args) - scalars),
            out_specs=[whole] * len(shapes) + [small] * len(plan),
            compiler_params=pltpu.CompilerParams(vmem_limit_bytes=16 << 20),
            cost_estimate=cost,
            name=name,
        )(*args)

    return call


def position():
    row = lax.axis_index("row")
    return row // 8, (row // 2) % 4, row % 2, lax.axis_index("col")


def factor_kernel(own_ref, other_ref, inv_a_ref, across_ref, inv_b_ref):
    even = lax.axis_index("row") % 2 == 0
    own, other = own_ref[...], other_ref[...]
    zero = jnp.where(even, own, other)
    one = jnp.where(even, other, own)

    def piece(blocks, index):
        rows = blocks[index * 32 : (index + 1) * 32]
        return jnp.concatenate([rows[:, part * HALF : (part + 1) * HALF] for part in range(4)], 0)

    inv_a = inverse_factor_256(piece(zero, 0), piece(zero, 1), piece(zero, 2))
    across = jnp.concatenate(
        [
            dot(jnp.concatenate([piece(zero, 3), piece(zero, 4)], 0), inv_a, 0, 1),
            dot(jnp.concatenate([piece(one, 3), piece(one, 4)], 1), inv_a, 1, 1),
        ],
        0,
    )
    square = dot(across, across, 1, 1)
    inv_b = inverse_factor_256(
        piece(one, 0) - square[:HALF, :HALF],
        piece(one, 1) - square[HALF:, :HALF],
        piece(one, 2) - square[HALF:, HALF:],
    )
    inv_a_ref[...] = inv_a
    across_ref[...] = across
    inv_b_ref[...] = inv_b


def factor(own, other):
    return local_call(factor_kernel, "factor", [(PW, PW)] * 3, cost=LARGE)(own, other)


def share_kernel(lead_ref, mate_ref, *outs):
    _, line, core, _ = position()
    for hop in range(4):
        rows = pl.ds(pl.multiple_of(32 * (2 * ((line + hop) % 4) + core), 32), 32)
        for parity in range(2):

            @pl.when(core == parity)
            def _():
                outs[hop][parity] = lead_ref[rows, :]
                outs[hop][1 - parity] = mate_ref[rows, :]


def owners_and_ranks(map_ref, group):
    owners = [map_ref[8 * group + t] // 8 for t in range(8)]
    ranks = [sum((owners[p] == owners[t]).astype(jnp.int32) for p in range(t)) + jnp.int32(0) for t in range(8)]
    return owners, ranks


def sort_kernel(map_ref, *refs):
    ins, outs = refs[:4], refs[4:]
    plane, line, _, _ = position()
    owners, ranks = owners_and_ranks(map_ref, plane)
    for tile in range(8):
        for hop in range(4):

            @pl.when((line - tile // 2) % 4 == hop)
            def _():
                piece = ins[hop][tile % 2]
                for owner in range(4):

                    @pl.when(owners[tile] == owner)
                    def _():
                        outs[owner][pl.ds(ranks[tile], 1)] = piece[None]


def corner_kernel(lead_ref, out_ref):
    plane, line, core, col = position()
    out_ref[...] = jnp.zeros_like(out_ref)
    places = [[(0, 0), (1, 0), (1, 1), (0, 2), (1, 2)], [(0, 2), (1, 2), (1, 3), (1, 0), (1, 1)]]
    for holder in range(2):

        @pl.when((col == 0) & (plane == 0) & (line == 0) & (core == holder))
        def _():
            for index, (down, right) in enumerate(places[holder]):
                for part in range(4):
                    rows = slice(down * HALF + part * 32, down * HALF + part * 32 + 32)
                    out_ref[index * 32 : index * 32 + 32, part * HALF : part * HALF + HALF] = lead_ref[
                        rows, right * HALF : right * HALF + HALF
                    ]


def merge_kernel(*refs):
    parts, out_ref = refs[:4], refs[4]
    for index, ref in enumerate(parts):

        @pl.when(lax.axis_index("col") == index)
        def _():
            out_ref[:32] = ref[0]
            out_ref[32:] = ref[1]


def load_kernel(own_ref, got_ref, *refs):
    blocks, out_ref = refs[:4], refs[4]
    out_ref[:64] = own_ref[...]
    out_ref[64:128] = got_ref[...]
    out_ref[128:] = (blocks[0][...] + blocks[1][...]) + (blocks[2][...] + blocks[3][...])


def join_kernel(rows, own_ref, got_ref, *outs):
    outs[0][:rows] = own_ref[:rows]
    outs[0][rows : 2 * rows] = got_ref[:rows]
    block = own_ref[rows : rows + BLOCK] + got_ref[rows : rows + BLOCK]
    if len(outs) == 1:
        outs[0][2 * rows :] = block
    else:
        outs[1][...] = block


def pick_kernel(map_ref, front_ref, *refs):
    outs, plan_ref = refs[:4], refs[4]
    col = lax.axis_index("col")
    row = lax.axis_index("row")
    for group in range(4):
        owners, ranks = owners_and_ranks(map_ref, group)

        @pl.when(col == group)
        def _():
            for tile in range(8):
                for hop in range(4):

                    @pl.when((owners[tile] - col) % 4 == hop)
                    def _():
                        column = pl.multiple_of(ranks[tile] * PW, PW)
                        outs[hop][:, pl.ds(column, PW)] = front_ref[:, tile * PW : (tile + 1) * PW]

        for tile in range(8):
            slot = map_ref[8 * group + tile] % 8

            @pl.when(owners[tile] == col)
            def _():
                plan_ref[0, slot] = (col - group) % 4
                plan_ref[1, slot] = jnp.int32(group)
                plan_ref[2, slot] = ranks[tile]
                plan_ref[3, slot] = ((row >= 2) & (8 * group + tile >= 2)).astype(jnp.int32)


def weight_kernel(*refs):
    rows, inverse = refs[:3], refs[3:6]
    panel_ref, weight_ref, rows_ref = refs[6:]
    for index, ref in enumerate(rows):

        @pl.when(jnp.minimum(lax.axis_index("col"), 2) == index)
        def _():
            rows_ref[...] = ref[...]

    inv_a, across, inv_b = [ref[...] for ref in inverse]
    panel_a = dot(rows_ref[:, :PW], inv_a, 1, 1)
    panel_b = dot(rows_ref[:, PW:] - dot(panel_a, across, 1, 1), inv_b, 1, 1)
    weight_b = dot(panel_b, inv_b, 1, 0)
    panel_ref[:, :PW] = panel_a
    panel_ref[:, PW:] = jnp.where(lax.axis_index("row") == 0, 0.0, panel_b)
    weight_ref[:, :PW] = dot(panel_a - dot(weight_b, across, 1, 0), inv_a, 1, 0)
    weight_ref[:, PW:] = weight_b


def weigh(rows, inverse):
    whole = pl.BlockSpec(memory_space=pltpu.VMEM)
    shape = (rows[0].shape[0], LEAD)
    return pl.pallas_call(
        weight_kernel,
        out_shape=[jax.ShapeDtypeStruct(shape, jnp.float32)] * 2,
        in_specs=[whole] * 6,
        out_specs=[whole] * 2,
        scratch_shapes=[pltpu.VMEM(shape, jnp.float32)],
        compiler_params=pltpu.CompilerParams(vmem_limit_bytes=16 << 20),
        cost_estimate=SMALL,
        name="weigh",
    )(*rows, *inverse)


def update_kernel(plan, *refs):
    weight_ref, pieces, gathered = refs[0], refs[1:5], refs[5:9]
    base_ref, out_ref, ahead_ref = refs[9:]
    slot = pl.program_id(0)
    plane, line, core, _ = position()
    group, place = plan[1, slot], plan[2, slot]
    for parity in range(2):
        holder = core if parity == 0 else 1 - core
        for x in range(4):
            off_z, off_x = plane ^ group, line ^ x
            first = jnp.where(holder == 0, off_x, off_z)
            second = jnp.where(holder == 0, off_z, off_x)
            index = ((first & 1) ^ (first >> 1)) + 2 * ((second & 1) ^ (second >> 1)) + 4 * (second >> 1)
            rows = pl.ds(pl.multiple_of(index * 64 + place * 32, 32), 32)
            into = pl.ds(pl.multiple_of((2 * x + holder) * 32, 32), 32)
            for late in range(2):

                @pl.when((first >> 1) == late)
                def _():
                    ahead_ref[into, :] = gathered[2 * parity + late][rows, :]

    product = dot(weight_ref[...], ahead_ref[...], 1, 1)
    column = pl.multiple_of(place * PW, PW)
    base = base_ref[...]
    out_ref[...] = base
    for index, ref in enumerate(pieces):

        @pl.when((plan[0, slot] == index) & (plan[3, slot] == 1))
        def _():
            out_ref[...] = base + (ref[:, pl.ds(column, PW)] - product)


def update(plan, weight, pieces, gathered, base):
    height, width = base.shape
    whole = pl.BlockSpec(memory_space=pltpu.VMEM)
    tile = pl.BlockSpec((height, PW), lambda u, plan: (0, u))
    return pl.pallas_call(
        update_kernel,
        out_shape=jax.ShapeDtypeStruct(base.shape, jnp.float32),
        grid_spec=pltpu.PrefetchScalarGridSpec(
            num_scalar_prefetch=1,
            grid=(width // PW,),
            in_specs=[whole] * 9 + [tile],
            out_specs=tile,
            scratch_shapes=[pltpu.VMEM((PW, LEAD), jnp.float32)],
        ),
        compiler_params=pltpu.CompilerParams(vmem_limit_bytes=16 << 20),
        name="update",
    )(plan, weight, *pieces, *gathered, base)


def doubling_steps():
    every = []
    for step in range(4):
        flip = 1 if step % 2 == 0 else 3
        pairs = {}
        for z in range(4):
            for x in range(4):
                for core in range(2):
                    to = (z, x ^ flip) if step // 2 == core else (z ^ flip, x)
                    pairs[(z * 4 + x) * 2 + core] = (to[0] * 4 + to[1]) * 2 + core
        every.append(pairs)
    return every


def shards(front, ancestor, tile_map):
    height = front.shape[0]
    swap = [(i, i ^ 1) for i in range(32)]
    part = (2, 32, LEAD)
    lead = front[:, :LEAD]

    ring = [[(i, (i + hop) % 4) for i in range(4)] for hop in range(4)]

    steps = doubling_steps()
    every = [list(step.items()) for step in steps]

    have = [0, 1]
    block = local_call(corner_kernel, "corner", [(BLOCK, LEAD)])(lead)[0]
    got = lax.ppermute(block, ("row", "col"), [(4 * i, 4 * steps[0][i]) for i in have])
    have += [steps[0][i] for i in have]

    mate = lax.ppermute(lead, "row", swap)
    parts = list(local_call(share_kernel, "share", [part] * 4)(lead, mate))
    for hop in range(1, 4):
        pairs = [(i, i // 8 * 8 + (i + 2 * hop) % 8) for i in range(2, 32)]
        parts[hop] = lax.ppermute(parts[hop], "row", pairs)
    parts = list(local_call(sort_kernel, "sort", [part] * 4, 1)(tile_map, *parts))
    block, got, parts = lax.optimization_barrier((block, got, parts))

    for to in range(1, 4):
        parts[to] = lax.ppermute(parts[to], "col", [(0, to)])
    block = block + got
    got = lax.ppermute(block, ("row", "col"), [(4 * i, 4 * steps[1][i]) for i in have])
    have += [steps[1][i] for i in have]
    block, got, parts = lax.optimization_barrier((block, got, parts))

    part = local_call(merge_kernel, "merge", [(64, LEAD)])(*parts)[0]
    beside = lax.ppermute(part, "row", every[0])
    blocks = [block + got]
    for to in range(1, 4):
        blocks.append(lax.ppermute(blocks[0], ("row", "col"), [(4 * i, 4 * i + to) for i in have]))

    *pieces, plan = local_call(pick_kernel, "pick", [(height, 2 * PW)] * 4, 1, [(4, 8)])(tile_map, front)

    load = local_call(load_kernel, "load", [(128 + BLOCK, LEAD)])(part, beside, *blocks)[0]
    load, lead, *pieces = lax.optimization_barrier((load, lead, *pieces))
    near = lax.ppermute(lead, "col", [(0, 1)])
    pieces[3] = lax.ppermute(pieces[3], "col", ring[3])
    load = local_call(partial(join_kernel, 128), "join", [(256 + BLOCK, LEAD)])(load, lax.ppermute(load, "row", every[2]))[0]
    load, near, *pieces = lax.optimization_barrier((load, near, *pieces))
    far = lax.ppermute(jnp.where(lax.axis_index("col") == 1, near, lead), "col", [(0, 3), (1, 2)])
    gathered, block = local_call(partial(join_kernel, 256), "join", [(512, LEAD), (BLOCK, LEAD)])(
        load, lax.ppermute(load, "row", every[3])
    )
    block, gathered, far, *pieces = lax.optimization_barrier((block, gathered, far, *pieces))
    other = lax.ppermute(block, "row", swap)
    late = lax.ppermute(gathered, "row", every[1])
    for hop in (1, 2):
        pieces[hop] = lax.ppermute(pieces[hop], "col", ring[hop])

    inverse = factor(block, other)
    late, gathered, inverse, pieces = lax.optimization_barrier((late, gathered, inverse, pieces))
    other_late = lax.ppermute(late, "row", swap)
    other_gathered = lax.ppermute(gathered, "row", swap)
    panel, weight = weigh([lead, near, far], inverse)
    updated = update(plan, weight, pieces, [gathered, late, other_gathered, other_late], ancestor)
    return panel, updated


def solution(mesh):
    return jax.shard_map(
        shards,
        mesh=mesh,
        in_specs=(P("row", "col"), P("row", "col"), P()),
        out_specs=(P("row", None), P("row", "col")),
        check_vma=False,
    )
```

```python
import jax
import jax.numpy as jnp
from jax import lax
from jax.experimental import pallas as pl
from jax.experimental.pallas import tpu as pltpu
from jax.sharding import PartitionSpec as P

PW = 256
LEAD = 512
HALF = 128
STEP = 8
TURN = 2
BLOCK = 160
PAD = 40
LARGE = pl.CostEstimate(flops=20 << 30, bytes_accessed=1 << 20, transcendentals=0)
SMALL = pl.CostEstimate(flops=1 << 10, bytes_accessed=1 << 10, transcendentals=0)
HIGHEST = lax.Precision.HIGHEST


def dot(a, b, ca, cb):
    return lax.dot_general(
        a, b, (((ca,), (cb,)), ((), ())), precision=HIGHEST, preferred_element_type=jnp.float32
    )


def spread_lane(rows, index):
    return jnp.broadcast_to(rows[:, index : index + 1], rows.shape)


def spread_row(rows, index):
    return jnp.broadcast_to(rows[index : index + 1, :], rows.shape)


def inverse_factor_128(square):
    n = HALF
    lane = lax.broadcasted_iota(jnp.int32, (STEP, n), 1)
    sub = lax.broadcasted_iota(jnp.int32, (STEP, n), 0)
    lane_turn = lax.broadcasted_iota(jnp.int32, (TURN * STEP, n), 1)
    count = n // STEP
    groups = [square[STEP * t : STEP * (t + 1), :] for t in range(count)]
    for turn in range(0, count, TURN):
        for step in range(turn, turn + TURN):
            start = STEP * step
            inside = (lane >= start) & (lane < start + STEP)
            top = groups[step]
            columns = [spread_lane(top, start + i) for i in range(STEP)]
            entry = [[spread_row(columns[i], j) if i <= j else None for i in range(STEP)] for j in range(STEP)]
            top = jnp.where(inside, jnp.where(lane - start == sub, 1.0, 0.0), top)
            rows = [spread_row(top, j) for j in range(STEP)]
            near = range(step + 1, min(turn + 2 * TURN, count))
            beside = {t: [spread_lane(groups[t], start + i) for i in range(STEP)] for t in near}
            for t in near:
                groups[t] = jnp.where(inside, 0.0, groups[t])
            done = [None] * STEP
            for i in range(STEP):
                scale = lax.rsqrt(entry[i][i])
                below = [None] * STEP
                for j in range(i + 1, STEP):
                    below[j] = entry[j][i] * scale
                    for k in range(i + 1, j + 1):
                        entry[j][k] = entry[j][k] - below[j] * below[k]
                done[i] = rows[i] * scale
                for j in range(i + 1, STEP):
                    rows[j] = rows[j] - below[j] * done[i]
                for t in near:
                    column = beside[t][i] * scale
                    for k in range(i + 1, STEP):
                        beside[t][k] = beside[t][k] - column * below[k]
                    groups[t] = groups[t] - column * done[i]
            solved = done[0]
            for i in range(1, STEP):
                solved = jnp.where(sub == i, done[i], solved)
            for t in range(step):
                groups[t] = jnp.where(inside, 0.0, groups[t])
            groups[step] = solved
        far = range(turn + 2 * TURN, count)
        if far:
            start, end = STEP * turn, STEP * (turn + TURN)
            solved = jnp.concatenate(groups[turn : turn + TURN], 0)
            ahead = jnp.where(lane_turn >= end + STEP * TURN, solved, 0.0)
            product = dot(ahead, solved, 0, 0)
            inside = (lane >= start) & (lane < end)
            for t in far:
                groups[t] = jnp.where(inside, 0.0, groups[t]) - product[STEP * t : STEP * (t + 1), :]
    return jnp.concatenate(groups, 0)


def inverse_factor_256(top, left, bottom):
    first = inverse_factor_128(top)
    across = dot(left, first, 1, 1)
    second = inverse_factor_128(bottom - dot(across, across, 1, 1))
    lower = -dot(second, dot(across, first, 1, 0), 1, 0)
    return jnp.concatenate(
        [
            jnp.concatenate([first, jnp.zeros_like(first)], 1),
            jnp.concatenate([lower, second], 1),
        ],
        0,
    )


def local_call(kernel, name, shapes, scalars=0, plan=(), cost=SMALL):
    whole = pl.BlockSpec(memory_space=pltpu.VMEM)
    small = pl.BlockSpec(memory_space=pltpu.SMEM)

    def call(*args):
        return pl.pallas_call(
            kernel,
            out_shape=[jax.ShapeDtypeStruct(shape, jnp.float32) for shape in shapes]
            + [jax.ShapeDtypeStruct(shape, jnp.int32) for shape in plan],
            in_specs=[small] * scalars + [whole] * (len(args) - scalars),
            out_specs=[whole] * len(shapes) + [small] * len(plan),
            compiler_params=pltpu.CompilerParams(vmem_limit_bytes=16 << 20),
            cost_estimate=cost,
            name=name,
        )(*args)

    return call


def position():
    row = lax.axis_index("row")
    return row // 8, (row // 2) % 4, row % 2, lax.axis_index("col")


def factor_kernel(own_ref, other_ref, inv_a_ref, across_ref, inv_b_ref):
    even = lax.axis_index("row") % 2 == 0
    own, other = own_ref[...], other_ref[...]
    zero = jnp.where(even, own, other)
    one = jnp.where(even, other, own)

    def piece(blocks, index):
        rows = blocks[index * 32 : (index + 1) * 32]
        return jnp.concatenate([rows[:, part * HALF : (part + 1) * HALF] for part in range(4)], 0)

    inv_a = inverse_factor_256(piece(zero, 0), piece(zero, 1), piece(zero, 2))
    across = jnp.concatenate(
        [
            dot(jnp.concatenate([piece(zero, 3), piece(zero, 4)], 0), inv_a, 0, 1),
            dot(jnp.concatenate([piece(one, 3), piece(one, 4)], 1), inv_a, 1, 1),
        ],
        0,
    )
    square = dot(across, across, 1, 1)
    inv_b = inverse_factor_256(
        piece(one, 0) - square[:HALF, :HALF],
        piece(one, 1) - square[HALF:, :HALF],
        piece(one, 2) - square[HALF:, HALF:],
    )
    inv_a_ref[...] = inv_a
    across_ref[...] = across
    inv_b_ref[...] = inv_b


def factor(own, other):
    return local_call(factor_kernel, "factor", [(PW, PW)] * 3, cost=LARGE)(own, other)


def share_kernel(lead_ref, mate_ref, *outs):
    _, line, core, _ = position()
    for hop in range(4):
        rows = pl.ds(pl.multiple_of(32 * (2 * ((line + hop) % 4) + core), 32), 32)
        for parity in range(2):

            @pl.when(core == parity)
            def _():
                outs[hop][parity] = lead_ref[rows, :]
                outs[hop][1 - parity] = mate_ref[rows, :]


def owners_and_ranks(map_ref, group):
    owners = [map_ref[8 * group + t] // 8 for t in range(8)]
    ranks = [sum((owners[p] == owners[t]).astype(jnp.int32) for p in range(t)) + jnp.int32(0) for t in range(8)]
    return owners, ranks


def sort_kernel(map_ref, *refs):
    ins, outs = refs[:4], refs[4:]
    plane, line, _, _ = position()
    owners, ranks = owners_and_ranks(map_ref, plane)
    for tile in range(8):
        for hop in range(4):

            @pl.when((line - tile // 2) % 4 == hop)
            def _():
                piece = ins[hop][tile % 2]
                for owner in range(4):

                    @pl.when(owners[tile] == owner)
                    def _():
                        outs[owner][pl.ds(ranks[tile], 1)] = piece[None]


def corner_kernel(lead_ref, out_ref):
    plane, line, core, col = position()
    out_ref[...] = jnp.zeros_like(out_ref)
    places = [[(0, 0), (1, 0), (1, 1), (0, 2), (1, 2)], [(0, 2), (1, 2), (1, 3), (1, 0), (1, 1)]]
    for holder in range(2):

        @pl.when((col == 0) & (plane == 0) & (line == 0) & (core == holder))
        def _():
            for index, (down, right) in enumerate(places[holder]):
                for part in range(4):
                    rows = slice(down * HALF + part * 32, down * HALF + part * 32 + 32)
                    out_ref[index * 32 : index * 32 + 32, part * HALF : part * HALF + HALF] = lead_ref[
                        rows, right * HALF : right * HALF + HALF
                    ]


def merge_kernel(*refs):
    parts, block_ref, got_ref, out_ref = refs[:4], refs[4], refs[5], refs[6]
    for index, ref in enumerate(parts):

        @pl.when(lax.axis_index("col") == index)
        def _():
            out_ref[:32] = ref[0]
            out_ref[32:64] = ref[1]

    out_ref[64 : 64 + BLOCK] = block_ref[...] + got_ref[...]
    out_ref[64 + BLOCK :] = jnp.zeros((PAD, LEAD), jnp.float32)


def join_kernel(own_ref, got_ref, *outs):
    if len(outs) == 1:
        outs[0][:128] = jnp.concatenate([own_ref[:64], got_ref[:64]], 0)
        outs[0][128:] = own_ref[64 : 64 + BLOCK] + got_ref[64 : 64 + BLOCK]
    else:
        outs[0][...] = jnp.concatenate([own_ref[:128], got_ref[:128]], 0)
        outs[1][...] = own_ref[128:] + got_ref[128:]


def pick_kernel(map_ref, front_ref, *refs):
    outs, plan_ref = refs[:4], refs[4]
    col = lax.axis_index("col")
    row = lax.axis_index("row")
    for group in range(4):
        owners, ranks = owners_and_ranks(map_ref, group)

        @pl.when(col == group)
        def _():
            for tile in range(8):
                for hop in range(4):

                    @pl.when((owners[tile] - col) % 4 == hop)
                    def _():
                        column = pl.multiple_of(ranks[tile] * PW, PW)
                        outs[hop][:, pl.ds(column, PW)] = front_ref[:, tile * PW : (tile + 1) * PW]

        for tile in range(8):
            slot = map_ref[8 * group + tile] % 8

            @pl.when(owners[tile] == col)
            def _():
                plan_ref[0, slot] = (col - group) % 4
                plan_ref[1, slot] = jnp.int32(group)
                plan_ref[2, slot] = ranks[tile]
                plan_ref[3, slot] = ((row >= 2) & (8 * group + tile >= 2)).astype(jnp.int32)


def weight_kernel(*refs):
    rows, inverse = refs[:3], refs[3:6]
    panel_ref, weight_ref, rows_ref = refs[6:]
    for index, ref in enumerate(rows):

        @pl.when(jnp.minimum(lax.axis_index("col"), 2) == index)
        def _():
            rows_ref[...] = ref[...]

    inv_a, across, inv_b = [ref[...] for ref in inverse]
    panel_a = dot(rows_ref[:, :PW], inv_a, 1, 1)
    panel_b = dot(rows_ref[:, PW:] - dot(panel_a, across, 1, 1), inv_b, 1, 1)
    weight_b = dot(panel_b, inv_b, 1, 0)
    panel_ref[:, :PW] = panel_a
    panel_ref[:, PW:] = jnp.where(lax.axis_index("row") == 0, 0.0, panel_b)
    weight_ref[:, :PW] = dot(panel_a - dot(weight_b, across, 1, 0), inv_a, 1, 0)
    weight_ref[:, PW:] = weight_b


def weigh(rows, inverse):
    whole = pl.BlockSpec(memory_space=pltpu.VMEM)
    shape = (rows[0].shape[0], LEAD)
    return pl.pallas_call(
        weight_kernel,
        out_shape=[jax.ShapeDtypeStruct(shape, jnp.float32)] * 2,
        in_specs=[whole] * 6,
        out_specs=[whole] * 2,
        scratch_shapes=[pltpu.VMEM(shape, jnp.float32)],
        compiler_params=pltpu.CompilerParams(vmem_limit_bytes=16 << 20),
        cost_estimate=SMALL,
        name="weigh",
    )(*rows, *inverse)


def update_kernel(plan, *refs):
    weight_ref, pieces, gathered = refs[0], refs[1:5], refs[5:9]
    base_ref, out_ref, ahead_ref = refs[9:]
    slot = pl.program_id(0)
    plane, line, core, _ = position()
    group, place = plan[1, slot], plan[2, slot]
    for parity in range(2):
        holder = core if parity == 0 else 1 - core
        for x in range(4):
            off_z, off_x = plane ^ group, line ^ x
            first = jnp.where(holder == 0, off_x, off_z)
            second = jnp.where(holder == 0, off_z, off_x)
            index = ((first & 1) ^ (first >> 1)) + 2 * (first >> 1) + 4 * ((second & 1) ^ (second >> 1))
            rows = pl.ds(pl.multiple_of(index * 64 + place * 32, 32), 32)
            into = pl.ds(pl.multiple_of((2 * x + holder) * 32, 32), 32)
            for late in range(2):

                @pl.when((second >> 1) == late)
                def _():
                    ahead_ref[into, :] = gathered[2 * parity + late][rows, :]

    product = dot(weight_ref[...], ahead_ref[...], 1, 1)
    column = pl.multiple_of(place * PW, PW)
    base = base_ref[...]
    out_ref[...] = base
    for index, ref in enumerate(pieces):

        @pl.when((plan[0, slot] == index) & (plan[3, slot] == 1))
        def _():
            out_ref[...] = base + (ref[:, pl.ds(column, PW)] - product)


def update(plan, weight, pieces, gathered, base):
    height, width = base.shape
    whole = pl.BlockSpec(memory_space=pltpu.VMEM)
    tile = pl.BlockSpec((height, PW), lambda u, plan: (0, u))
    return pl.pallas_call(
        update_kernel,
        out_shape=jax.ShapeDtypeStruct(base.shape, jnp.float32),
        grid_spec=pltpu.PrefetchScalarGridSpec(
            num_scalar_prefetch=1,
            grid=(width // PW,),
            in_specs=[whole] * 9 + [tile],
            out_specs=tile,
            scratch_shapes=[pltpu.VMEM((PW, LEAD), jnp.float32)],
        ),
        compiler_params=pltpu.CompilerParams(vmem_limit_bytes=16 << 20),
        name="update",
    )(plan, weight, *pieces, *gathered, base)


def doubling_steps():
    every, spread = [], []
    have = {0, 1}
    for step in range(4):
        flip = 1 if step % 2 == 0 else 3
        pairs = []
        for z in range(4):
            for x in range(4):
                for core in range(2):
                    to = (z, x ^ flip) if step // 2 == core else (z ^ flip, x)
                    pairs.append(((z * 4 + x) * 2 + core, (to[0] * 4 + to[1]) * 2 + core))
        every.append(pairs)
        spread.append([pair for pair in pairs if pair[0] in have])
        have |= {pair[1] for pair in spread[-1]}
    return every, spread


def shards(front, ancestor, tile_map):
    height = front.shape[0]
    swap = [(i, i ^ 1) for i in range(32)]
    part = (2, 32, LEAD)
    lead = front[:, :LEAD]

    ring = [[(i, (i + hop) % 4) for i in range(4)] for hop in range(4)]

    block = local_call(corner_kernel, "corner", [(BLOCK, LEAD)])(lead)[0]
    got = lax.ppermute(block, ("row", "col"), [(4 * i, 4 * i + 1) for i in (0, 1)])

    mate = lax.ppermute(lead, "row", swap)
    parts = list(local_call(share_kernel, "share", [part] * 4)(lead, mate))
    for hop in range(1, 4):
        pairs = [(i, i // 8 * 8 + (i + 2 * hop) % 8) for i in range(2, 32)]
        parts[hop] = lax.ppermute(parts[hop], "row", pairs)
    parts = list(local_call(sort_kernel, "sort", [part] * 4, 1)(tile_map, *parts))
    block, got, parts = lax.optimization_barrier((block, got, parts))

    every, spread = doubling_steps()
    for to in range(1, 4):
        parts[to] = lax.ppermute(parts[to], "col", [(0, to)])
    block = block + got
    got = lax.ppermute(block, ("row", "col"), [(4 * i + y, 4 * i + to) for i in (0, 1) for y, to in ((0, 3), (1, 2))])
    block, got, parts = lax.optimization_barrier((block, got, parts))
    load = local_call(merge_kernel, "merge", [(64 + BLOCK + PAD, LEAD)])(*parts, block, got)[0]

    *pieces, plan = local_call(pick_kernel, "pick", [(height, 2 * PW)] * 4, 1, [(4, 8)])(tile_map, front)

    load, lead = lax.optimization_barrier((load, lead))
    near = lax.ppermute(lead, "col", [(0, 1)])
    load = local_call(join_kernel, "join", [(128 + BLOCK, LEAD)])(load, lax.ppermute(load, "row", every[0]))[0]
    load, near, *pieces = lax.optimization_barrier((load, near, *pieces))
    far = lax.ppermute(jnp.where(lax.axis_index("col") == 1, near, lead), "col", [(0, 3), (1, 2)])
    gathered, block = local_call(join_kernel, "join", [(256, LEAD), (BLOCK, LEAD)])(load, lax.ppermute(load, "row", every[1]))
    block, gathered, far, *pieces = lax.optimization_barrier((block, gathered, far, *pieces))

    block = block + lax.ppermute(block, "row", spread[2])
    block, gathered = lax.optimization_barrier((block, gathered))
    pieces[3] = lax.ppermute(pieces[3], "col", ring[3])
    block = block + lax.ppermute(block, "row", spread[3])
    gathered = jnp.concatenate([gathered, lax.ppermute(gathered, "row", every[2])], 0)
    block, gathered, *pieces = lax.optimization_barrier((block, gathered, *pieces))
    other = lax.ppermute(block, "row", swap)
    late = lax.ppermute(gathered, "row", every[3])
    for hop in (1, 2):
        pieces[hop] = lax.ppermute(pieces[hop], "col", ring[hop])

    inverse = factor(block, other)
    late, gathered, inverse, pieces = lax.optimization_barrier((late, gathered, inverse, pieces))
    other_late = lax.ppermute(late, "row", swap)
    other_gathered = lax.ppermute(gathered, "row", swap)
    panel, weight = weigh([lead, near, far], inverse)
    updated = update(plan, weight, pieces, [gathered, late, other_gathered, other_late], ancestor)
    return panel, updated


def solution(mesh):
    return jax.shard_map(
        shards,
        mesh=mesh,
        in_specs=(P("row", "col"), P("row", "col"), P()),
        out_specs=(P("row", None), P("row", "col")),
        check_vma=False,
    )
```

```python
from functools import partial

import jax
import jax.numpy as jnp
from jax import lax
from jax.experimental import pallas as pl
from jax.experimental.pallas import tpu as pltpu
from jax.sharding import PartitionSpec as P

PW = 256
LEAD = 512
HALF = 128
STEP = 8
TURN = 2
BLOCK = 160
PAD = 40
LARGE = pl.CostEstimate(flops=20 << 30, bytes_accessed=1 << 20, transcendentals=0)
SMALL = pl.CostEstimate(flops=1 << 10, bytes_accessed=1 << 10, transcendentals=0)
HIGHEST = lax.Precision.HIGHEST


def dot(a, b, ca, cb):
    return lax.dot_general(
        a, b, (((ca,), (cb,)), ((), ())), precision=HIGHEST, preferred_element_type=jnp.float32
    )


def spread_lane(rows, index):
    return jnp.broadcast_to(rows[:, index : index + 1], rows.shape)


def spread_row(rows, index):
    return jnp.broadcast_to(rows[index : index + 1, :], rows.shape)


def inverse_factor_128(square):
    n = HALF
    lane = lax.broadcasted_iota(jnp.int32, (STEP, n), 1)
    sub = lax.broadcasted_iota(jnp.int32, (STEP, n), 0)
    lane_turn = lax.broadcasted_iota(jnp.int32, (TURN * STEP, n), 1)
    count = n // STEP
    groups = [square[STEP * t : STEP * (t + 1), :] for t in range(count)]
    for turn in range(0, count, TURN):
        for step in range(turn, turn + TURN):
            start = STEP * step
            inside = (lane >= start) & (lane < start + STEP)
            top = groups[step]
            columns = [spread_lane(top, start + i) for i in range(STEP)]
            entry = [[spread_row(columns[i], j) if i <= j else None for i in range(STEP)] for j in range(STEP)]
            top = jnp.where(inside, jnp.where(lane - start == sub, 1.0, 0.0), top)
            rows = [spread_row(top, j) for j in range(STEP)]
            near = range(step + 1, min(turn + 2 * TURN, count))
            beside = {t: [spread_lane(groups[t], start + i) for i in range(STEP)] for t in near}
            for t in near:
                groups[t] = jnp.where(inside, 0.0, groups[t])
            done = [None] * STEP
            for i in range(STEP):
                scale = lax.rsqrt(entry[i][i])
                below = [None] * STEP
                for j in range(i + 1, STEP):
                    below[j] = entry[j][i] * scale
                    for k in range(i + 1, j + 1):
                        entry[j][k] = entry[j][k] - below[j] * below[k]
                done[i] = rows[i] * scale
                for j in range(i + 1, STEP):
                    rows[j] = rows[j] - below[j] * done[i]
                for t in near:
                    column = beside[t][i] * scale
                    for k in range(i + 1, STEP):
                        beside[t][k] = beside[t][k] - column * below[k]
                    groups[t] = groups[t] - column * done[i]
            solved = done[0]
            for i in range(1, STEP):
                solved = jnp.where(sub == i, done[i], solved)
            for t in range(step):
                groups[t] = jnp.where(inside, 0.0, groups[t])
            groups[step] = solved
        far = range(turn + 2 * TURN, count)
        if far:
            start, end = STEP * turn, STEP * (turn + TURN)
            solved = jnp.concatenate(groups[turn : turn + TURN], 0)
            ahead = jnp.where(lane_turn >= end + STEP * TURN, solved, 0.0)
            product = dot(ahead, solved, 0, 0)
            inside = (lane >= start) & (lane < end)
            for t in far:
                groups[t] = jnp.where(inside, 0.0, groups[t]) - product[STEP * t : STEP * (t + 1), :]
    return jnp.concatenate(groups, 0)


def inverse_factor_256(top, left, bottom):
    first = inverse_factor_128(top)
    across = dot(left, first, 1, 1)
    second = inverse_factor_128(bottom - dot(across, across, 1, 1))
    lower = -dot(second, dot(across, first, 1, 0), 1, 0)
    return jnp.concatenate(
        [
            jnp.concatenate([first, jnp.zeros_like(first)], 1),
            jnp.concatenate([lower, second], 1),
        ],
        0,
    )


def local_call(kernel, name, shapes, scalars=0, plan=(), cost=SMALL):
    whole = pl.BlockSpec(memory_space=pltpu.VMEM)
    small = pl.BlockSpec(memory_space=pltpu.SMEM)

    def call(*args):
        return pl.pallas_call(
            kernel,
            out_shape=[jax.ShapeDtypeStruct(shape, jnp.float32) for shape in shapes]
            + [jax.ShapeDtypeStruct(shape, jnp.int32) for shape in plan],
            in_specs=[small] * scalars + [whole] * (len(args) - scalars),
            out_specs=[whole] * len(shapes) + [small] * len(plan),
            compiler_params=pltpu.CompilerParams(vmem_limit_bytes=16 << 20),
            cost_estimate=cost,
            name=name,
        )(*args)

    return call


def position():
    row = lax.axis_index("row")
    return row // 8, (row // 2) % 4, row % 2, lax.axis_index("col")


def factor_kernel(own_ref, other_ref, inv_a_ref, across_ref, inv_b_ref):
    even = lax.axis_index("row") % 2 == 0
    own, other = own_ref[...], other_ref[...]
    zero = jnp.where(even, own, other)
    one = jnp.where(even, other, own)

    def piece(blocks, index):
        rows = blocks[index * 32 : (index + 1) * 32]
        return jnp.concatenate([rows[:, part * HALF : (part + 1) * HALF] for part in range(4)], 0)

    inv_a = inverse_factor_256(piece(zero, 0), piece(zero, 1), piece(zero, 2))
    across = jnp.concatenate(
        [
            dot(jnp.concatenate([piece(zero, 3), piece(zero, 4)], 0), inv_a, 0, 1),
            dot(jnp.concatenate([piece(one, 3), piece(one, 4)], 1), inv_a, 1, 1),
        ],
        0,
    )
    square = dot(across, across, 1, 1)
    inv_b = inverse_factor_256(
        piece(one, 0) - square[:HALF, :HALF],
        piece(one, 1) - square[HALF:, :HALF],
        piece(one, 2) - square[HALF:, HALF:],
    )
    inv_a_ref[...] = inv_a
    across_ref[...] = across
    inv_b_ref[...] = inv_b


def factor(own, other):
    return local_call(factor_kernel, "factor", [(PW, PW)] * 3, cost=LARGE)(own, other)


def share_kernel(lead_ref, mate_ref, *outs):
    _, line, core, _ = position()
    for hop in range(4):
        rows = pl.ds(pl.multiple_of(32 * (2 * ((line + hop) % 4) + core), 32), 32)
        for parity in range(2):

            @pl.when(core == parity)
            def _():
                outs[hop][parity] = lead_ref[rows, :]
                outs[hop][1 - parity] = mate_ref[rows, :]


def owners_and_ranks(map_ref, group):
    owners = [map_ref[8 * group + t] // 8 for t in range(8)]
    ranks = [sum((owners[p] == owners[t]).astype(jnp.int32) for p in range(t)) + jnp.int32(0) for t in range(8)]
    return owners, ranks


def sort_kernel(map_ref, *refs):
    ins, outs = refs[:4], refs[4:]
    plane, line, _, _ = position()
    owners, ranks = owners_and_ranks(map_ref, plane)
    for tile in range(8):
        for hop in range(4):

            @pl.when((line - tile // 2) % 4 == hop)
            def _():
                piece = ins[hop][tile % 2]
                for owner in range(4):

                    @pl.when(owners[tile] == owner)
                    def _():
                        outs[owner][pl.ds(ranks[tile], 1)] = piece[None]


def corner_kernel(lead_ref, out_ref):
    plane, line, core, col = position()
    out_ref[...] = jnp.zeros_like(out_ref)
    places = [[(0, 0), (1, 0), (1, 1), (0, 2), (1, 2)], [(0, 2), (1, 2), (1, 3), (1, 0), (1, 1)]]
    for holder in range(2):

        @pl.when((col == 0) & (plane == 0) & (line == 0) & (core == holder))
        def _():
            for index, (down, right) in enumerate(places[holder]):
                for part in range(4):
                    rows = slice(down * HALF + part * 32, down * HALF + part * 32 + 32)
                    out_ref[index * 32 : index * 32 + 32, part * HALF : part * HALF + HALF] = lead_ref[
                        rows, right * HALF : right * HALF + HALF
                    ]


def merge_kernel(*refs):
    parts, block_ref, got_ref, out_ref = refs[:4], refs[4], refs[5], refs[6]
    for index, ref in enumerate(parts):

        @pl.when(lax.axis_index("col") == index)
        def _():
            out_ref[:32] = ref[0]
            out_ref[32:64] = ref[1]

    out_ref[64 : 64 + BLOCK] = block_ref[...] + got_ref[...]
    out_ref[64 + BLOCK :] = jnp.zeros((PAD, LEAD), jnp.float32)


def join_kernel(rows, own_ref, got_ref, *outs):
    outs[0][:rows] = own_ref[:rows]
    outs[0][rows : 2 * rows] = got_ref[:rows]
    block = own_ref[rows : rows + BLOCK] + got_ref[rows : rows + BLOCK]
    if len(outs) == 1:
        outs[0][2 * rows :] = block
    else:
        outs[1][...] = block


def pick_kernel(map_ref, front_ref, *refs):
    outs, plan_ref = refs[:4], refs[4]
    col = lax.axis_index("col")
    row = lax.axis_index("row")
    for group in range(4):
        owners, ranks = owners_and_ranks(map_ref, group)

        @pl.when(col == group)
        def _():
            for tile in range(8):
                for hop in range(4):

                    @pl.when((owners[tile] - col) % 4 == hop)
                    def _():
                        column = pl.multiple_of(ranks[tile] * PW, PW)
                        outs[hop][:, pl.ds(column, PW)] = front_ref[:, tile * PW : (tile + 1) * PW]

        for tile in range(8):
            slot = map_ref[8 * group + tile] % 8

            @pl.when(owners[tile] == col)
            def _():
                plan_ref[0, slot] = (col - group) % 4
                plan_ref[1, slot] = jnp.int32(group)
                plan_ref[2, slot] = ranks[tile]
                plan_ref[3, slot] = ((row >= 2) & (8 * group + tile >= 2)).astype(jnp.int32)


def weight_kernel(*refs):
    rows, inverse = refs[:3], refs[3:6]
    panel_ref, weight_ref, rows_ref = refs[6:]
    for index, ref in enumerate(rows):

        @pl.when(jnp.minimum(lax.axis_index("col"), 2) == index)
        def _():
            rows_ref[...] = ref[...]

    inv_a, across, inv_b = [ref[...] for ref in inverse]
    panel_a = dot(rows_ref[:, :PW], inv_a, 1, 1)
    panel_b = dot(rows_ref[:, PW:] - dot(panel_a, across, 1, 1), inv_b, 1, 1)
    weight_b = dot(panel_b, inv_b, 1, 0)
    panel_ref[:, :PW] = panel_a
    panel_ref[:, PW:] = jnp.where(lax.axis_index("row") == 0, 0.0, panel_b)
    weight_ref[:, :PW] = dot(panel_a - dot(weight_b, across, 1, 0), inv_a, 1, 0)
    weight_ref[:, PW:] = weight_b


def weigh(rows, inverse):
    whole = pl.BlockSpec(memory_space=pltpu.VMEM)
    shape = (rows[0].shape[0], LEAD)
    return pl.pallas_call(
        weight_kernel,
        out_shape=[jax.ShapeDtypeStruct(shape, jnp.float32)] * 2,
        in_specs=[whole] * 6,
        out_specs=[whole] * 2,
        scratch_shapes=[pltpu.VMEM(shape, jnp.float32)],
        compiler_params=pltpu.CompilerParams(vmem_limit_bytes=16 << 20),
        cost_estimate=SMALL,
        name="weigh",
    )(*rows, *inverse)


def update_kernel(plan, *refs):
    weight_ref, pieces, gathered = refs[0], refs[1:5], refs[5:9]
    base_ref, out_ref, ahead_ref = refs[9:]
    plane, line, core, _ = position()
    for half in range(2):
        slot = 2 * pl.program_id(0) + half
        group, place = plan[1, slot], plan[2, slot]
        for parity in range(2):
            holder = core if parity == 0 else 1 - core
            for x in range(4):
                off_z, off_x = plane ^ group, line ^ x
                first = jnp.where(holder == 0, off_x, off_z)
                second = jnp.where(holder == 0, off_z, off_x)
                index = (first >> 1) + 2 * ((second & 1) ^ (second >> 1)) + 4 * (second >> 1)
                rows = pl.ds(pl.multiple_of(index * 64 + place * 32, 32), 32)
                into = pl.ds(pl.multiple_of((2 * x + holder) * 32, 32), 32)
                for late in range(2):

                    @pl.when(((first & 1) ^ (first >> 1)) == late)
                    def _():
                        ahead_ref[half, into, :] = gathered[2 * parity + late][rows, :]

        product = dot(weight_ref[...], ahead_ref[half], 1, 1)
        column = pl.multiple_of(place * PW, PW)
        here = slice(half * PW, half * PW + PW)

        @pl.when(plan[3, slot] == 0)
        def _():
            out_ref[:, here] = base_ref[:, here]

        for index, ref in enumerate(pieces):

            @pl.when((plan[0, slot] == index) & (plan[3, slot] == 1))
            def _():
                out_ref[:, here] = base_ref[:, here] + (ref[:, pl.ds(column, PW)] - product)


def update(plan, weight, pieces, gathered, base):
    height, width = base.shape
    whole = pl.BlockSpec(memory_space=pltpu.VMEM)
    tile = pl.BlockSpec((height, 2 * PW), lambda u, plan: (0, u))
    return pl.pallas_call(
        update_kernel,
        out_shape=jax.ShapeDtypeStruct(base.shape, jnp.float32),
        grid_spec=pltpu.PrefetchScalarGridSpec(
            num_scalar_prefetch=1,
            grid=(width // (2 * PW),),
            in_specs=[whole] * 9 + [tile],
            out_specs=tile,
            scratch_shapes=[pltpu.VMEM((2, PW, LEAD), jnp.float32)],
        ),
        compiler_params=pltpu.CompilerParams(vmem_limit_bytes=16 << 20),
        name="update",
    )(plan, weight, *pieces, *gathered, base)


def doubling_steps():
    every = []
    for step in range(4):
        flip = 1 if step % 2 == 0 else 3
        pairs = []
        for z in range(4):
            for x in range(4):
                for core in range(2):
                    to = (z, x ^ flip) if step // 2 == core else (z ^ flip, x)
                    pairs.append(((z * 4 + x) * 2 + core, (to[0] * 4 + to[1]) * 2 + core))
        every.append(pairs)
    return every, [pair for pair in every[0] if pair[0] < 2]


def shards(front, ancestor, tile_map):
    height = front.shape[0]
    swap = [(i, i ^ 1) for i in range(32)]
    part = (2, 32, LEAD)
    lead = front[:, :LEAD]

    ring = [[(i, (i + hop) % 4) for i in range(4)] for hop in range(4)]

    blocks = [local_call(corner_kernel, "corner", [(BLOCK, LEAD)])(lead)[0]]
    for to in range(1, 4):
        blocks.append(lax.ppermute(blocks[0], ("row", "col"), [(4 * core, 4 * core + to) for core in range(2)]))

    mate = lax.ppermute(lead, "row", swap)
    parts = list(local_call(share_kernel, "share", [part] * 4)(lead, mate))
    for hop in range(1, 4):
        pairs = [(i, i // 8 * 8 + (i + 2 * hop) % 8) for i in range(2, 32)]
        parts[hop] = lax.ppermute(parts[hop], "row", pairs)
    parts = list(local_call(sort_kernel, "sort", [part] * 4, 1)(tile_map, *parts))
    blocks, parts = lax.optimization_barrier((blocks, parts))

    every, spread = doubling_steps()
    for to in range(1, 4):
        parts[to] = lax.ppermute(parts[to], "col", [(0, to)])
    block = (blocks[0] + blocks[1]) + (blocks[2] + blocks[3])
    got = lax.ppermute(block, "row", spread)
    block, got, parts = lax.optimization_barrier((block, got, parts))
    load = local_call(merge_kernel, "merge", [(64 + BLOCK + PAD, LEAD)])(*parts, block, got)[0]

    *pieces, plan = local_call(pick_kernel, "pick", [(height, 2 * PW)] * 4, 1, [(4, 8)])(tile_map, front)

    load, lead = lax.optimization_barrier((load, lead))
    near = lax.ppermute(lead, "col", [(0, 1)])
    load = local_call(partial(join_kernel, 64), "join", [(128 + BLOCK, LEAD)])(load, lax.ppermute(load, "row", every[1]))[0]
    load, near, *pieces = lax.optimization_barrier((load, near, *pieces))
    load = local_call(partial(join_kernel, 128), "join", [(256 + BLOCK, LEAD)])(load, lax.ppermute(load, "row", every[2]))[0]
    load, near, lead, *pieces = lax.optimization_barrier((load, near, lead, *pieces))
    far = lax.ppermute(jnp.where(lax.axis_index("col") == 1, near, lead), "col", [(0, 3), (1, 2)])
    pieces[3] = lax.ppermute(pieces[3], "col", ring[3])
    gathered, block = local_call(partial(join_kernel, 256), "join", [(512, LEAD), (BLOCK, LEAD)])(
        load, lax.ppermute(load, "row", every[3])
    )
    block, gathered, far, *pieces = lax.optimization_barrier((block, gathered, far, *pieces))
    other = lax.ppermute(block, "row", swap)
    late = lax.ppermute(gathered, "row", every[0])
    for hop in (1, 2):
        pieces[hop] = lax.ppermute(pieces[hop], "col", ring[hop])

    inverse = factor(block, other)
    late, gathered, inverse, pieces = lax.optimization_barrier((late, gathered, inverse, pieces))
    other_late = lax.ppermute(late, "row", swap)
    other_gathered = lax.ppermute(gathered, "row", swap)
    panel, weight = weigh([lead, near, far], inverse)
    updated = update(plan, weight, pieces, [gathered, late, other_gathered, other_late], ancestor)
    return panel, updated


def solution(mesh):
    return jax.shard_map(
        shards,
        mesh=mesh,
        in_specs=(P("row", "col"), P("row", "col"), P()),
        out_specs=(P("row", None), P("row", "col")),
        check_vma=False,
    )
```

```python
from functools import partial

import jax
import jax.numpy as jnp
from jax import lax
from jax.experimental import pallas as pl
from jax.experimental.pallas import tpu as pltpu
from jax.sharding import PartitionSpec as P

PW = 256
LEAD = 512
HALF = 128
STEP = 8
TURN = 2
BLOCK = 136
PAD = 64
LARGE = pl.CostEstimate(flops=20 << 30, bytes_accessed=1 << 20, transcendentals=0)
SMALL = pl.CostEstimate(flops=1 << 10, bytes_accessed=1 << 10, transcendentals=0)
HIGHEST = lax.Precision.HIGHEST


def dot(a, b, ca, cb):
    return lax.dot_general(
        a, b, (((ca,), (cb,)), ((), ())), precision=HIGHEST, preferred_element_type=jnp.float32
    )


def spread_lane(rows, index):
    return jnp.broadcast_to(rows[:, index : index + 1], rows.shape)


def spread_row(rows, index):
    return jnp.broadcast_to(rows[index : index + 1, :], rows.shape)


def inverse_factor_128(square):
    n = HALF
    lane = lax.broadcasted_iota(jnp.int32, (STEP, n), 1)
    sub = lax.broadcasted_iota(jnp.int32, (STEP, n), 0)
    lane_turn = lax.broadcasted_iota(jnp.int32, (TURN * STEP, n), 1)
    count = n // STEP
    groups = [square[STEP * t : STEP * (t + 1), :] for t in range(count)]
    for turn in range(0, count, TURN):
        for step in range(turn, turn + TURN):
            start = STEP * step
            inside = (lane >= start) & (lane < start + STEP)
            top = groups[step]
            columns = [spread_lane(top, start + i) for i in range(STEP)]
            entry = [[spread_row(columns[i], j) if i <= j else None for i in range(STEP)] for j in range(STEP)]
            top = jnp.where(inside, jnp.where(lane - start == sub, 1.0, 0.0), top)
            rows = [spread_row(top, j) for j in range(STEP)]
            near = range(step + 1, min(turn + 2 * TURN, count))
            beside = {t: [spread_lane(groups[t], start + i) for i in range(STEP)] for t in near}
            for t in near:
                groups[t] = jnp.where(inside, 0.0, groups[t])
            done = [None] * STEP
            for i in range(STEP):
                scale = lax.rsqrt(entry[i][i])
                below = [None] * STEP
                for j in range(i + 1, STEP):
                    below[j] = entry[j][i] * scale
                    for k in range(i + 1, j + 1):
                        entry[j][k] = entry[j][k] - below[j] * below[k]
                done[i] = rows[i] * scale
                for j in range(i + 1, STEP):
                    rows[j] = rows[j] - below[j] * done[i]
                for t in near:
                    column = beside[t][i] * scale
                    for k in range(i + 1, STEP):
                        beside[t][k] = beside[t][k] - column * below[k]
                    groups[t] = groups[t] - column * done[i]
            solved = done[0]
            for i in range(1, STEP):
                solved = jnp.where(sub == i, done[i], solved)
            for t in range(step):
                groups[t] = jnp.where(inside, 0.0, groups[t])
            groups[step] = solved
        far = range(turn + 2 * TURN, count)
        if far:
            start, end = STEP * turn, STEP * (turn + TURN)
            solved = jnp.concatenate(groups[turn : turn + TURN], 0)
            ahead = jnp.where(lane_turn >= end + STEP * TURN, solved, 0.0)
            product = dot(ahead, solved, 0, 0)
            inside = (lane >= start) & (lane < end)
            for t in far:
                groups[t] = jnp.where(inside, 0.0, groups[t]) - product[STEP * t : STEP * (t + 1), :]
    return jnp.concatenate(groups, 0)


def inverse_factor_256(top, left, bottom):
    first = inverse_factor_128(top)
    across = dot(left, first, 1, 1)
    second = inverse_factor_128(bottom - dot(across, across, 1, 1))
    lower = -dot(second, dot(across, first, 1, 0), 1, 0)
    return jnp.concatenate(
        [
            jnp.concatenate([first, jnp.zeros_like(first)], 1),
            jnp.concatenate([lower, second], 1),
        ],
        0,
    )


def local_call(kernel, name, shapes, scalars=0, plan=(), cost=SMALL):
    whole = pl.BlockSpec(memory_space=pltpu.VMEM)
    small = pl.BlockSpec(memory_space=pltpu.SMEM)

    def call(*args):
        return pl.pallas_call(
            kernel,
            out_shape=[jax.ShapeDtypeStruct(shape, jnp.float32) for shape in shapes]
            + [jax.ShapeDtypeStruct(shape, jnp.int32) for shape in plan],
            in_specs=[small] * scalars + [whole] * (len(args) - scalars),
            out_specs=[whole] * len(shapes) + [small] * len(plan),
            compiler_params=pltpu.CompilerParams(vmem_limit_bytes=16 << 20),
            cost_estimate=cost,
            name=name,
        )(*args)

    return call


def position():
    row = lax.axis_index("row")
    return row // 8, (row // 2) % 4, row % 2, lax.axis_index("col")


def factor_kernel(own_ref, other_ref, inv_a_ref, across_ref, inv_b_ref):
    even = lax.axis_index("row") % 2 == 0
    own, other = own_ref[...], other_ref[...]
    zero = jnp.where(even, own, other)
    one = jnp.where(even, other, own)
    down = lax.broadcasted_iota(jnp.int32, (HALF, HALF), 0)
    right = lax.broadcasted_iota(jnp.int32, (HALF, HALF), 1)

    def piece(blocks, index):
        rows = blocks[index * 32 : (index + 1) * 32]
        return jnp.concatenate([rows[:, part * HALF : (part + 1) * HALF] for part in range(4)], 0)

    def diagonal(blocks):
        packed = piece(blocks, 0)
        low = jnp.where(down > right, packed, 0.0)
        high = jnp.where(down < right, packed, 0.0)
        edge = jnp.broadcast_to(blocks[128:129, :HALF], (HALF, HALF))
        first = jnp.where(down >= right, packed, jnp.transpose(low))
        second = jnp.where(down < right, packed, jnp.where(down == right, edge, jnp.transpose(high)))
        return first, second

    top, bottom = diagonal(zero)
    inv_a = inverse_factor_256(top, piece(zero, 1), bottom)
    across = jnp.concatenate(
        [
            dot(jnp.concatenate([piece(zero, 2), piece(zero, 3)], 0), inv_a, 0, 1),
            dot(jnp.concatenate([piece(one, 2), piece(one, 3)], 1), inv_a, 1, 1),
        ],
        0,
    )
    square = dot(across, across, 1, 1)
    top, bottom = diagonal(one)
    inv_b = inverse_factor_256(
        top - square[:HALF, :HALF],
        piece(one, 1) - square[HALF:, :HALF],
        bottom - square[HALF:, HALF:],
    )
    inv_a_ref[...] = inv_a
    across_ref[...] = across
    inv_b_ref[...] = inv_b


def factor(own, other):
    return local_call(factor_kernel, "factor", [(PW, PW)] * 3, cost=LARGE)(own, other)


def share_kernel(lead_ref, mate_ref, *outs):
    _, line, core, _ = position()
    for hop in range(4):
        rows = pl.ds(pl.multiple_of(32 * (2 * ((line + hop) % 4) + core), 32), 32)
        for parity in range(2):

            @pl.when(core == parity)
            def _():
                outs[hop][parity] = lead_ref[rows, :]
                outs[hop][1 - parity] = mate_ref[rows, :]


def owners_and_ranks(map_ref, group):
    owners = [map_ref[8 * group + t] // 8 for t in range(8)]
    ranks = [sum((owners[p] == owners[t]).astype(jnp.int32) for p in range(t)) + jnp.int32(0) for t in range(8)]
    return owners, ranks


def sort_kernel(map_ref, *refs):
    ins, outs = refs[:4], refs[4:]
    plane, line, _, _ = position()
    owners, ranks = owners_and_ranks(map_ref, plane)
    for tile in range(8):
        for hop in range(4):

            @pl.when((line - tile // 2) % 4 == hop)
            def _():
                piece = ins[hop][tile % 2]
                for owner in range(4):

                    @pl.when(owners[tile] == owner)
                    def _():
                        outs[owner][pl.ds(ranks[tile], 1)] = piece[None]


def corner_kernel(lead_ref, out_ref):
    plane, line, core, col = position()
    out_ref[...] = jnp.zeros_like(out_ref)
    down = lax.broadcasted_iota(jnp.int32, (HALF, HALF), 0)
    right = lax.broadcasted_iota(jnp.int32, (HALF, HALF), 1)
    places = [[(0, 0), (1, 1), (1, 0), (0, 2), (1, 2)], [(0, 2), (1, 3), (1, 2), (1, 0), (1, 1)]]
    for holder in range(2):

        @pl.when((col == 0) & (plane == 0) & (line == 0) & (core == holder))
        def _():
            blocks = [lead_ref[i * HALF : i * HALF + HALF, j * HALF : j * HALF + HALF] for i, j in places[holder]]
            first, second = blocks[:2]
            for index, block in enumerate([jnp.where(down >= right, first, second)] + blocks[2:]):
                for part in range(4):
                    out_ref[index * 32 : index * 32 + 32, part * HALF : part * HALF + HALF] = block[part * 32 : part * 32 + 32]
            diagonal = jnp.sum(jnp.where(down == right, second, 0.0), axis=0, keepdims=True)
            out_ref[128:, :HALF] = jnp.broadcast_to(diagonal, (8, HALF))


def merge_kernel(*refs):
    parts, block_ref, got_ref, out_ref = refs[:4], refs[4], refs[5], refs[6]
    for index, ref in enumerate(parts):

        @pl.when(lax.axis_index("col") == index)
        def _():
            out_ref[:32] = ref[0]
            out_ref[32:64] = ref[1]

    out_ref[64 : 64 + BLOCK] = block_ref[...] + got_ref[...]
    out_ref[64 + BLOCK :] = jnp.zeros((PAD, LEAD), jnp.float32)


def join_kernel(rows, own_ref, got_ref, *outs):
    outs[0][:rows] = own_ref[:rows]
    outs[0][rows : 2 * rows] = got_ref[:rows]
    block = own_ref[rows : rows + BLOCK] + got_ref[rows : rows + BLOCK]
    if len(outs) == 1:
        outs[0][2 * rows :] = block
    else:
        outs[1][...] = block


def pick_kernel(map_ref, front_ref, *refs):
    outs, plan_ref = refs[:4], refs[4]
    col = lax.axis_index("col")
    row = lax.axis_index("row")
    for group in range(4):
        owners, ranks = owners_and_ranks(map_ref, group)

        @pl.when(col == group)
        def _():
            for tile in range(8):
                for hop in range(4):

                    @pl.when((owners[tile] - col) % 4 == hop)
                    def _():
                        column = pl.multiple_of(ranks[tile] * PW, PW)
                        outs[hop][:, pl.ds(column, PW)] = front_ref[:, tile * PW : (tile + 1) * PW]

        for tile in range(8):
            slot = map_ref[8 * group + tile] % 8

            @pl.when(owners[tile] == col)
            def _():
                plan_ref[0, slot] = (col - group) % 4
                plan_ref[1, slot] = jnp.int32(group)
                plan_ref[2, slot] = ranks[tile]
                plan_ref[3, slot] = ((row >= 2) & (8 * group + tile >= 2)).astype(jnp.int32)


def weight_kernel(*refs):
    rows, inverse = refs[:3], refs[3:6]
    panel_ref, weight_ref, rows_ref = refs[6:]
    for index, ref in enumerate(rows):

        @pl.when(jnp.minimum(lax.axis_index("col"), 2) == index)
        def _():
            rows_ref[...] = ref[...]

    inv_a, across, inv_b = [ref[...] for ref in inverse]
    panel_a = dot(rows_ref[:, :PW], inv_a, 1, 1)
    panel_b = dot(rows_ref[:, PW:] - dot(panel_a, across, 1, 1), inv_b, 1, 1)
    weight_b = dot(panel_b, inv_b, 1, 0)
    panel_ref[:, :PW] = panel_a
    panel_ref[:, PW:] = jnp.where(lax.axis_index("row") == 0, 0.0, panel_b)
    weight_ref[:, :PW] = dot(panel_a - dot(weight_b, across, 1, 0), inv_a, 1, 0)
    weight_ref[:, PW:] = weight_b


def weigh(rows, inverse):
    whole = pl.BlockSpec(memory_space=pltpu.VMEM)
    shape = (rows[0].shape[0], LEAD)
    return pl.pallas_call(
        weight_kernel,
        out_shape=[jax.ShapeDtypeStruct(shape, jnp.float32)] * 2,
        in_specs=[whole] * 6,
        out_specs=[whole] * 2,
        scratch_shapes=[pltpu.VMEM(shape, jnp.float32)],
        compiler_params=pltpu.CompilerParams(vmem_limit_bytes=16 << 20),
        cost_estimate=SMALL,
        name="weigh",
    )(*rows, *inverse)


def update_kernel(plan, *refs):
    weight_ref, pieces, gathered = refs[0], refs[1:5], refs[5:9]
    base_ref, out_ref, ahead_ref = refs[9:]
    slot = pl.program_id(0)
    plane, line, core, _ = position()
    group, place = plan[1, slot], plan[2, slot]
    for parity in range(2):
        holder = core if parity == 0 else 1 - core
        for x in range(4):
            off_z, off_x = plane ^ group, line ^ x
            first = jnp.where(holder == 0, off_x, off_z)
            second = jnp.where(holder == 0, off_z, off_x)
            index = (first >> 1) + 2 * ((second & 1) ^ (second >> 1)) + 4 * (second >> 1)
            rows = pl.ds(pl.multiple_of(index * 64 + place * 32, 32), 32)
            into = pl.ds(pl.multiple_of((2 * x + holder) * 32, 32), 32)
            late = ((first & 1) ^ (first >> 1)) == 1
            ahead_ref[into, :] = jnp.where(late, gathered[2 * parity + 1][rows, :], gathered[2 * parity][rows, :])

    product = dot(weight_ref[...], ahead_ref[...], 1, 1)
    column = pl.multiple_of(place * PW, PW)
    base = base_ref[...]

    @pl.when(plan[3, slot] == 0)
    def _():
        out_ref[...] = base

    for index, ref in enumerate(pieces):

        @pl.when((plan[0, slot] == index) & (plan[3, slot] == 1))
        def _():
            out_ref[...] = base + (ref[:, pl.ds(column, PW)] - product)


def update(plan, weight, pieces, gathered, base):
    height, width = base.shape
    whole = pl.BlockSpec(memory_space=pltpu.VMEM)
    tile = pl.BlockSpec((height, PW), lambda u, plan: (0, u))
    return pl.pallas_call(
        update_kernel,
        out_shape=jax.ShapeDtypeStruct(base.shape, jnp.float32),
        grid_spec=pltpu.PrefetchScalarGridSpec(
            num_scalar_prefetch=1,
            grid=(width // PW,),
            in_specs=[whole] * 9 + [tile],
            out_specs=tile,
            scratch_shapes=[pltpu.VMEM((PW, LEAD), jnp.float32)],
        ),
        compiler_params=pltpu.CompilerParams(vmem_limit_bytes=16 << 20),
        name="update",
    )(plan, weight, *pieces, *gathered, base)


def doubling_steps():
    every = []
    for step in range(4):
        flip = 1 if step % 2 == 0 else 3
        pairs = []
        for z in range(4):
            for x in range(4):
                for core in range(2):
                    to = (z, x ^ flip) if step // 2 == core else (z ^ flip, x)
                    pairs.append(((z * 4 + x) * 2 + core, (to[0] * 4 + to[1]) * 2 + core))
        every.append(pairs)
    return every, [pair for pair in every[0] if pair[0] < 2]


def shards(front, ancestor, tile_map):
    height = front.shape[0]
    swap = [(i, i ^ 1) for i in range(32)]
    part = (2, 32, LEAD)
    lead = front[:, :LEAD]

    ring = [[(i, (i + hop) % 4) for i in range(4)] for hop in range(4)]

    blocks = [local_call(corner_kernel, "corner", [(BLOCK, LEAD)])(lead)[0]]
    for to in range(1, 4):
        blocks.append(lax.ppermute(blocks[0], ("row", "col"), [(4 * core, 4 * core + to) for core in range(2)]))

    mate = lax.ppermute(lead, "row", swap)
    parts = list(local_call(share_kernel, "share", [part] * 4)(lead, mate))
    for hop in range(1, 4):
        pairs = [(i, i // 8 * 8 + (i + 2 * hop) % 8) for i in range(2, 32)]
        parts[hop] = lax.ppermute(parts[hop], "row", pairs)
    parts = list(local_call(sort_kernel, "sort", [part] * 4, 1)(tile_map, *parts))
    blocks, parts = lax.optimization_barrier((blocks, parts))

    every, spread = doubling_steps()
    for to in range(1, 4):
        parts[to] = lax.ppermute(parts[to], "col", [(0, to)])
    block = (blocks[0] + blocks[1]) + (blocks[2] + blocks[3])
    got = lax.ppermute(block, "row", spread)
    block, got, parts = lax.optimization_barrier((block, got, parts))
    load = local_call(merge_kernel, "merge", [(64 + BLOCK + PAD, LEAD)])(*parts, block, got)[0]

    *pieces, plan = local_call(pick_kernel, "pick", [(height, 2 * PW)] * 4, 1, [(4, 8)])(tile_map, front)

    load, lead = lax.optimization_barrier((load, lead))
    near = lax.ppermute(lead, "col", [(0, 1)])
    load = local_call(partial(join_kernel, 64), "join", [(128 + BLOCK, LEAD)])(load, lax.ppermute(load, "row", every[1]))[0]
    load, near, *pieces = lax.optimization_barrier((load, near, *pieces))
    far = lax.ppermute(jnp.where(lax.axis_index("col") == 1, near, lead), "col", [(0, 3), (1, 2)])
    load = local_call(partial(join_kernel, 128), "join", [(256 + BLOCK, LEAD)])(load, lax.ppermute(load, "row", every[2]))[0]
    load, far, *pieces = lax.optimization_barrier((load, far, *pieces))
    gathered, block = local_call(partial(join_kernel, 256), "join", [(512, LEAD), (BLOCK, LEAD)])(
        load, lax.ppermute(load, "row", every[3])
    )
    for hop in (1, 3):
        pieces[hop] = lax.ppermute(pieces[hop], "col", ring[hop])
    block, gathered, *pieces = lax.optimization_barrier((block, gathered, *pieces))
    other = lax.ppermute(block, "row", swap)
    late = lax.ppermute(gathered, "row", every[0])
    pieces[2] = lax.ppermute(pieces[2], "col", ring[2])

    inverse = factor(block, other)
    late, gathered, inverse, pieces = lax.optimization_barrier((late, gathered, inverse, pieces))
    other_late = lax.ppermute(late, "row", swap)
    other_gathered = lax.ppermute(gathered, "row", swap)
    panel, weight = weigh([lead, near, far], inverse)
    updated = update(plan, weight, pieces, [gathered, late, other_gathered, other_late], ancestor)
    return panel, updated


def solution(mesh):
    return jax.shard_map(
        shards,
        mesh=mesh,
        in_specs=(P("row", "col"), P("row", "col"), P()),
        out_specs=(P("row", None), P("row", "col")),
        check_vma=False,
    )
```

```python
from functools import partial

import jax
import jax.numpy as jnp
from jax import lax
from jax.experimental import pallas as pl
from jax.experimental.pallas import tpu as pltpu
from jax.sharding import PartitionSpec as P

PW = 256
LEAD = 512
HALF = 128
STEP = 8
TURN = 2
BLOCK = 136
PAD = 64
LARGE = pl.CostEstimate(flops=20 << 30, bytes_accessed=1 << 20, transcendentals=0)
SMALL = pl.CostEstimate(flops=1 << 10, bytes_accessed=1 << 10, transcendentals=0)
HIGHEST = lax.Precision.HIGHEST


def dot(a, b, ca, cb):
    return lax.dot_general(
        a, b, (((ca,), (cb,)), ((), ())), precision=HIGHEST, preferred_element_type=jnp.float32
    )


def spread_lane(rows, index):
    return jnp.broadcast_to(rows[:, index : index + 1], rows.shape)


def spread_row(rows, index):
    return jnp.broadcast_to(rows[index : index + 1, :], rows.shape)


def inverse_factor_128(square):
    n = HALF
    lane = lax.broadcasted_iota(jnp.int32, (STEP, n), 1)
    sub = lax.broadcasted_iota(jnp.int32, (STEP, n), 0)
    lane_turn = lax.broadcasted_iota(jnp.int32, (TURN * STEP, n), 1)
    count = n // STEP
    groups = [square[STEP * t : STEP * (t + 1), :] for t in range(count)]
    for turn in range(0, count, TURN):
        for step in range(turn, turn + TURN):
            start = STEP * step
            inside = (lane >= start) & (lane < start + STEP)
            top = groups[step]
            columns = [spread_lane(top, start + i) for i in range(STEP)]
            entry = [[spread_row(columns[i], j) if i <= j else None for i in range(STEP)] for j in range(STEP)]
            top = jnp.where(inside, jnp.where(lane - start == sub, 1.0, 0.0), top)
            rows = [spread_row(top, j) for j in range(STEP)]
            near = range(step + 1, min(turn + 2 * TURN, count))
            beside = {t: [spread_lane(groups[t], start + i) for i in range(STEP)] for t in near}
            for t in near:
                groups[t] = jnp.where(inside, 0.0, groups[t])
            done = [None] * STEP
            for i in range(STEP):
                scale = lax.rsqrt(entry[i][i])
                below = [None] * STEP
                for j in range(i + 1, STEP):
                    below[j] = entry[j][i] * scale
                    for k in range(i + 1, j + 1):
                        entry[j][k] = entry[j][k] - below[j] * below[k]
                done[i] = rows[i] * scale
                for j in range(i + 1, STEP):
                    rows[j] = rows[j] - below[j] * done[i]
                for t in near:
                    column = beside[t][i] * scale
                    for k in range(i + 1, STEP):
                        beside[t][k] = beside[t][k] - column * below[k]
                    groups[t] = groups[t] - column * done[i]
            solved = done[0]
            for i in range(1, STEP):
                solved = jnp.where(sub == i, done[i], solved)
            for t in range(step):
                groups[t] = jnp.where(inside, 0.0, groups[t])
            groups[step] = solved
        far = range(turn + 2 * TURN, count)
        if far:
            start, end = STEP * turn, STEP * (turn + TURN)
            solved = jnp.concatenate(groups[turn : turn + TURN], 0)
            ahead = jnp.where(lane_turn >= end + STEP * TURN, solved, 0.0)
            product = dot(ahead, solved, 0, 0)
            inside = (lane >= start) & (lane < end)
            for t in far:
                groups[t] = jnp.where(inside, 0.0, groups[t]) - product[STEP * t : STEP * (t + 1), :]
    return jnp.concatenate(groups, 0)


def inverse_factor_256(top, left, bottom):
    first = inverse_factor_128(top)
    across = dot(left, first, 1, 1)
    second = inverse_factor_128(bottom - dot(across, across, 1, 1))
    lower = -dot(second, dot(across, first, 1, 0), 1, 0)
    return jnp.concatenate(
        [
            jnp.concatenate([first, jnp.zeros_like(first)], 1),
            jnp.concatenate([lower, second], 1),
        ],
        0,
    )


def local_call(kernel, name, shapes, scalars=0, plan=(), cost=SMALL):
    whole = pl.BlockSpec(memory_space=pltpu.VMEM)
    small = pl.BlockSpec(memory_space=pltpu.SMEM)

    def call(*args):
        return pl.pallas_call(
            kernel,
            out_shape=[jax.ShapeDtypeStruct(shape, jnp.float32) for shape in shapes]
            + [jax.ShapeDtypeStruct(shape, jnp.int32) for shape in plan],
            in_specs=[small] * scalars + [whole] * (len(args) - scalars),
            out_specs=[whole] * len(shapes) + [small] * len(plan),
            compiler_params=pltpu.CompilerParams(vmem_limit_bytes=16 << 20),
            cost_estimate=cost,
            name=name,
        )(*args)

    return call


def position():
    row = lax.axis_index("row")
    return row // 8, (row // 2) % 4, row % 2, lax.axis_index("col")


def factor_kernel(own_ref, other_ref, inv_a_ref, across_ref, inv_b_ref):
    even = lax.axis_index("row") % 2 == 0
    own, other = own_ref[...], other_ref[...]
    zero = jnp.where(even, own, other)
    one = jnp.where(even, other, own)
    down = lax.broadcasted_iota(jnp.int32, (HALF, HALF), 0)
    right = lax.broadcasted_iota(jnp.int32, (HALF, HALF), 1)

    def piece(blocks, index):
        rows = blocks[index * 32 : (index + 1) * 32]
        return jnp.concatenate([rows[:, part * HALF : (part + 1) * HALF] for part in range(4)], 0)

    def diagonal(blocks):
        packed = piece(blocks, 0)
        low = jnp.where(down > right, packed, 0.0)
        high = jnp.where(down < right, packed, 0.0)
        edge = jnp.broadcast_to(blocks[128:129, :HALF], (HALF, HALF))
        first = jnp.where(down >= right, packed, jnp.transpose(low))
        second = jnp.where(down < right, packed, jnp.where(down == right, edge, jnp.transpose(high)))
        return first, second

    top, bottom = diagonal(zero)
    inv_a = inverse_factor_256(top, piece(zero, 1), bottom)
    across = jnp.concatenate(
        [
            dot(jnp.concatenate([piece(zero, 2), piece(zero, 3)], 0), inv_a, 0, 1),
            dot(jnp.concatenate([piece(one, 2), piece(one, 3)], 1), inv_a, 1, 1),
        ],
        0,
    )
    square = dot(across, across, 1, 1)
    top, bottom = diagonal(one)
    inv_b = inverse_factor_256(
        top - square[:HALF, :HALF],
        piece(one, 1) - square[HALF:, :HALF],
        bottom - square[HALF:, HALF:],
    )
    inv_a_ref[...] = inv_a
    across_ref[...] = across
    inv_b_ref[...] = inv_b


def factor(own, other):
    return local_call(factor_kernel, "factor", [(PW, PW)] * 3, cost=LARGE)(own, other)


def share_kernel(lead_ref, mate_ref, *outs):
    _, line, core, _ = position()
    for hop in range(4):
        rows = pl.ds(pl.multiple_of(32 * (2 * ((line + hop) % 4) + core), 32), 32)
        for parity in range(2):

            @pl.when(core == parity)
            def _():
                outs[hop][parity] = lead_ref[rows, :]
                outs[hop][1 - parity] = mate_ref[rows, :]


def owners_and_ranks(map_ref, group):
    owners = [map_ref[8 * group + t] // 8 for t in range(8)]
    ranks = [sum((owners[p] == owners[t]).astype(jnp.int32) for p in range(t)) + jnp.int32(0) for t in range(8)]
    return owners, ranks


def sort_kernel(map_ref, *refs):
    ins, outs = refs[:4], refs[4:]
    plane, line, _, _ = position()
    owners, ranks = owners_and_ranks(map_ref, plane)
    for tile in range(8):
        for hop in range(4):

            @pl.when((line - tile // 2) % 4 == hop)
            def _():
                piece = ins[hop][tile % 2]
                for owner in range(4):

                    @pl.when(owners[tile] == owner)
                    def _():
                        outs[owner][pl.ds(ranks[tile], 1)] = piece[None]


def corner_kernel(lead_ref, out_ref):
    plane, line, core, col = position()
    out_ref[...] = jnp.zeros_like(out_ref)
    down = lax.broadcasted_iota(jnp.int32, (HALF, HALF), 0)
    right = lax.broadcasted_iota(jnp.int32, (HALF, HALF), 1)
    places = [[(0, 0), (1, 1), (1, 0), (0, 2), (1, 2)], [(0, 2), (1, 3), (1, 2), (1, 0), (1, 1)]]
    for holder in range(2):

        @pl.when((col == 0) & (plane == 0) & (line == 0) & (core == holder))
        def _():
            blocks = [lead_ref[i * HALF : i * HALF + HALF, j * HALF : j * HALF + HALF] for i, j in places[holder]]
            first, second = blocks[:2]
            for index, block in enumerate([jnp.where(down >= right, first, second)] + blocks[2:]):
                for part in range(4):
                    out_ref[index * 32 : index * 32 + 32, part * HALF : part * HALF + HALF] = block[part * 32 : part * 32 + 32]
            diagonal = jnp.sum(jnp.where(down == right, second, 0.0), axis=0, keepdims=True)
            out_ref[128:, :HALF] = jnp.broadcast_to(diagonal, (8, HALF))


def merge_kernel(*refs):
    parts, block_ref, got_ref, out_ref = refs[:4], refs[4], refs[5], refs[6]
    for index, ref in enumerate(parts):

        @pl.when(lax.axis_index("col") == index)
        def _():
            out_ref[:32] = ref[0]
            out_ref[32:64] = ref[1]

    out_ref[64 : 64 + BLOCK] = block_ref[...] + got_ref[...]
    out_ref[64 + BLOCK :] = jnp.zeros((PAD, LEAD), jnp.float32)


def join_kernel(rows, own_ref, got_ref, *outs):
    outs[0][:rows] = own_ref[:rows]
    outs[0][rows : 2 * rows] = got_ref[:rows]
    block = own_ref[rows : rows + BLOCK] + got_ref[rows : rows + BLOCK]
    if len(outs) == 1:
        outs[0][2 * rows :] = block
    else:
        outs[1][...] = block


def pick_kernel(map_ref, front_ref, *refs):
    outs, plan_ref = refs[:4], refs[4]
    col = lax.axis_index("col")
    row = lax.axis_index("row")
    for group in range(4):
        owners, ranks = owners_and_ranks(map_ref, group)

        @pl.when(col == group)
        def _():
            for tile in range(8):
                for hop in range(4):

                    @pl.when((owners[tile] - col) % 4 == hop)
                    def _():
                        column = pl.multiple_of(ranks[tile] * PW, PW)
                        outs[hop][:, pl.ds(column, PW)] = front_ref[:, tile * PW : (tile + 1) * PW]

        for tile in range(8):
            slot = map_ref[8 * group + tile] % 8

            @pl.when(owners[tile] == col)
            def _():
                plan_ref[0, slot] = (col - group) % 4
                plan_ref[1, slot] = jnp.int32(group)
                plan_ref[2, slot] = ranks[tile]
                plan_ref[3, slot] = ((row >= 2) & (8 * group + tile >= 2)).astype(jnp.int32)


def weight_kernel(*refs):
    rows, inverse = refs[:4], refs[4:7]
    panel_ref, weight_ref, rows_ref = refs[7:]
    for index, ref in enumerate(rows):

        @pl.when(lax.axis_index("col") == index)
        def _():
            rows_ref[...] = ref[...]

    inv_a, across, inv_b = [ref[...] for ref in inverse]
    panel_a = dot(rows_ref[:, :PW], inv_a, 1, 1)
    panel_b = dot(rows_ref[:, PW:] - dot(panel_a, across, 1, 1), inv_b, 1, 1)
    weight_b = dot(panel_b, inv_b, 1, 0)
    panel_ref[:, :PW] = panel_a
    panel_ref[:, PW:] = jnp.where(lax.axis_index("row") == 0, 0.0, panel_b)
    weight_ref[:, :PW] = dot(panel_a - dot(weight_b, across, 1, 0), inv_a, 1, 0)
    weight_ref[:, PW:] = weight_b


def weigh(rows, inverse):
    whole = pl.BlockSpec(memory_space=pltpu.VMEM)
    shape = (rows[0].shape[0], LEAD)
    return pl.pallas_call(
        weight_kernel,
        out_shape=[jax.ShapeDtypeStruct(shape, jnp.float32)] * 2,
        in_specs=[whole] * 7,
        out_specs=[whole] * 2,
        scratch_shapes=[pltpu.VMEM(shape, jnp.float32)],
        compiler_params=pltpu.CompilerParams(vmem_limit_bytes=16 << 20),
        cost_estimate=SMALL,
        name="weigh",
    )(*rows, *inverse)


def update_kernel(plan, *refs):
    weight_ref, pieces, gathered = refs[0], refs[1:5], refs[5:9]
    base_ref, out_ref, ahead_ref = refs[9:]
    slot = pl.program_id(0)
    plane, line, core, _ = position()
    group, place = plan[1, slot], plan[2, slot]
    for parity in range(2):
        holder = core if parity == 0 else 1 - core
        for x in range(4):
            off_z, off_x = plane ^ group, line ^ x
            first = jnp.where(holder == 0, off_x, off_z)
            second = jnp.where(holder == 0, off_z, off_x)
            index = (first >> 1) + 2 * ((second & 1) ^ (second >> 1)) + 4 * (second >> 1)
            rows = pl.ds(pl.multiple_of(index * 64 + place * 32, 32), 32)
            into = pl.ds(pl.multiple_of((2 * x + holder) * 32, 32), 32)
            late = ((first & 1) ^ (first >> 1)) == 1
            ahead_ref[into, :] = jnp.where(late, gathered[2 * parity + 1][rows, :], gathered[2 * parity][rows, :])

    product = dot(weight_ref[...], ahead_ref[...], 1, 1)
    column = pl.multiple_of(place * PW, PW)
    base = base_ref[...]

    @pl.when(plan[3, slot] == 0)
    def _():
        out_ref[...] = base

    for index, ref in enumerate(pieces):

        @pl.when((plan[0, slot] == index) & (plan[3, slot] == 1))
        def _():
            out_ref[...] = base + (ref[:, pl.ds(column, PW)] - product)


def update(plan, weight, pieces, gathered, base):
    height, width = base.shape
    whole = pl.BlockSpec(memory_space=pltpu.VMEM)
    tile = pl.BlockSpec((height, PW), lambda u, plan: (0, u))
    return pl.pallas_call(
        update_kernel,
        out_shape=jax.ShapeDtypeStruct(base.shape, jnp.float32),
        grid_spec=pltpu.PrefetchScalarGridSpec(
            num_scalar_prefetch=1,
            grid=(width // PW,),
            in_specs=[whole] * 9 + [tile],
            out_specs=tile,
            scratch_shapes=[pltpu.VMEM((PW, LEAD), jnp.float32)],
        ),
        compiler_params=pltpu.CompilerParams(vmem_limit_bytes=16 << 20),
        name="update",
    )(plan, weight, *pieces, *gathered, base)


def doubling_steps():
    every = []
    for step in range(4):
        flip = 1 if step % 2 == 0 else 3
        pairs = []
        for z in range(4):
            for x in range(4):
                for core in range(2):
                    to = (z, x ^ flip) if step // 2 == core else (z ^ flip, x)
                    pairs.append(((z * 4 + x) * 2 + core, (to[0] * 4 + to[1]) * 2 + core))
        every.append(pairs)
    return every, [pair for pair in every[0] if pair[0] < 2]


def shards(front, ancestor, tile_map):
    height = front.shape[0]
    swap = [(i, i ^ 1) for i in range(32)]
    part = (2, 32, LEAD)
    lead = front[:, :LEAD]

    ring = [[(i, (i + hop) % 4) for i in range(4)] for hop in range(4)]

    blocks = [local_call(corner_kernel, "corner", [(BLOCK, LEAD)])(lead)[0]]
    for to in range(1, 4):
        blocks.append(lax.ppermute(blocks[0], ("row", "col"), [(4 * core, 4 * core + to) for core in range(2)]))

    mate = lax.ppermute(lead, "row", swap)
    parts = list(local_call(share_kernel, "share", [part] * 4)(lead, mate))
    for hop in range(1, 4):
        pairs = [(i, i // 8 * 8 + (i + 2 * hop) % 8) for i in range(2, 32)]
        parts[hop] = lax.ppermute(parts[hop], "row", pairs)
    parts = list(local_call(sort_kernel, "sort", [part] * 4, 1)(tile_map, *parts))
    blocks, parts = lax.optimization_barrier((blocks, parts))

    every, spread = doubling_steps()
    for to in range(1, 4):
        parts[to] = lax.ppermute(parts[to], "col", [(0, to)])
    block = (blocks[0] + blocks[1]) + (blocks[2] + blocks[3])
    got = lax.ppermute(block, "row", spread)
    block, got, parts = lax.optimization_barrier((block, got, parts))
    load = local_call(merge_kernel, "merge", [(64 + BLOCK + PAD, LEAD)])(*parts, block, got)[0]

    *pieces, plan = local_call(pick_kernel, "pick", [(height, 2 * PW)] * 4, 1, [(4, 8)])(tile_map, front)

    load, lead = lax.optimization_barrier((load, lead))
    copies = [lax.ppermute(lead, "col", [(0, to)]) for to in (1, 2, 3)]
    load = local_call(partial(join_kernel, 64), "join", [(128 + BLOCK, LEAD)])(load, lax.ppermute(load, "row", every[1]))[0]
    load, copies[0], copies[2], *pieces = lax.optimization_barrier((load, copies[0], copies[2], *pieces))
    load = local_call(partial(join_kernel, 128), "join", [(256 + BLOCK, LEAD)])(load, lax.ppermute(load, "row", every[2]))[0]
    load, copies[1], *pieces = lax.optimization_barrier((load, copies[1], *pieces))
    gathered, block = local_call(partial(join_kernel, 256), "join", [(512, LEAD), (BLOCK, LEAD)])(
        load, lax.ppermute(load, "row", every[3])
    )
    for hop in (1, 3):
        pieces[hop] = lax.ppermute(pieces[hop], "col", ring[hop])
    block, gathered, *pieces = lax.optimization_barrier((block, gathered, *pieces))
    other = lax.ppermute(block, "row", swap)
    late = lax.ppermute(gathered, "row", every[0])
    pieces[2] = lax.ppermute(pieces[2], "col", ring[2])
    other_gathered = lax.ppermute(gathered, "row", swap)

    inverse = factor(block, other)
    late, other_gathered, inverse, pieces = lax.optimization_barrier((late, other_gathered, inverse, pieces))
    other_late = lax.ppermute(late, "row", swap)
    panel, weight = weigh([lead, *copies], inverse)
    updated = update(plan, weight, pieces, [gathered, late, other_gathered, other_late], ancestor)
    return panel, updated


def solution(mesh):
    return jax.shard_map(
        shards,
        mesh=mesh,
        in_specs=(P("row", "col"), P("row", "col"), P()),
        out_specs=(P("row", None), P("row", "col")),
        check_vma=False,
    )
```

```python
from functools import partial

import jax
import jax.numpy as jnp
from jax import lax
from jax.experimental import pallas as pl
from jax.experimental.pallas import tpu as pltpu
from jax.sharding import PartitionSpec as P

PW = 256
LEAD = 512
HALF = 128
STEP = 8
TURN = 2
BLOCK = 136
PAD = 64
LARGE = pl.CostEstimate(flops=20 << 30, bytes_accessed=1 << 20, transcendentals=0)
SMALL = pl.CostEstimate(flops=1 << 10, bytes_accessed=1 << 10, transcendentals=0)
HIGHEST = lax.Precision.HIGHEST


def dot(a, b, ca, cb):
    return lax.dot_general(
        a, b, (((ca,), (cb,)), ((), ())), precision=HIGHEST, preferred_element_type=jnp.float32
    )


def spread_lane(rows, index):
    return jnp.broadcast_to(rows[:, index : index + 1], rows.shape)


def spread_row(rows, index):
    return jnp.broadcast_to(rows[index : index + 1, :], rows.shape)


def inverse_factor_128(square):
    n = HALF
    lane = lax.broadcasted_iota(jnp.int32, (STEP, n), 1)
    sub = lax.broadcasted_iota(jnp.int32, (STEP, n), 0)
    lane_turn = lax.broadcasted_iota(jnp.int32, (TURN * STEP, n), 1)
    count = n // STEP
    groups = [square[STEP * t : STEP * (t + 1), :] for t in range(count)]
    for turn in range(0, count, TURN):
        for step in range(turn, turn + TURN):
            start = STEP * step
            inside = (lane >= start) & (lane < start + STEP)
            top = groups[step]
            columns = [spread_lane(top, start + i) for i in range(STEP)]
            entry = [[spread_row(columns[i], j) if i <= j else None for i in range(STEP)] for j in range(STEP)]
            top = jnp.where(inside, jnp.where(lane - start == sub, 1.0, 0.0), top)
            rows = [spread_row(top, j) for j in range(STEP)]
            near = range(step + 1, min(turn + 2 * TURN, count))
            beside = {t: [spread_lane(groups[t], start + i) for i in range(STEP)] for t in near}
            for t in near:
                groups[t] = jnp.where(inside, 0.0, groups[t])
            done = [None] * STEP
            for i in range(STEP):
                scale = lax.rsqrt(entry[i][i])
                below = [None] * STEP
                for j in range(i + 1, STEP):
                    below[j] = entry[j][i] * scale
                    for k in range(i + 1, j + 1):
                        entry[j][k] = entry[j][k] - below[j] * below[k]
                done[i] = rows[i] * scale
                for j in range(i + 1, STEP):
                    rows[j] = rows[j] - below[j] * done[i]
                for t in near:
                    column = beside[t][i] * scale
                    for k in range(i + 1, STEP):
                        beside[t][k] = beside[t][k] - column * below[k]
                    groups[t] = groups[t] - column * done[i]
            solved = done[0]
            for i in range(1, STEP):
                solved = jnp.where(sub == i, done[i], solved)
            for t in range(step):
                groups[t] = jnp.where(inside, 0.0, groups[t])
            groups[step] = solved
        far = range(turn + 2 * TURN, count)
        if far:
            start, end = STEP * turn, STEP * (turn + TURN)
            solved = jnp.concatenate(groups[turn : turn + TURN], 0)
            ahead = jnp.where(lane_turn >= end + STEP * TURN, solved, 0.0)
            product = dot(ahead, solved, 0, 0)
            inside = (lane >= start) & (lane < end)
            for t in far:
                groups[t] = jnp.where(inside, 0.0, groups[t]) - product[STEP * t : STEP * (t + 1), :]
    return jnp.concatenate(groups, 0)


def inverse_factor_256(top, left, bottom):
    first = inverse_factor_128(top)
    across = dot(left, first, 1, 1)
    second = inverse_factor_128(bottom - dot(across, across, 1, 1))
    lower = -dot(second, dot(across, first, 1, 0), 1, 0)
    return jnp.concatenate(
        [
            jnp.concatenate([first, jnp.zeros_like(first)], 1),
            jnp.concatenate([lower, second], 1),
        ],
        0,
    )


def local_call(kernel, name, shapes, scalars=0, plan=(), cost=SMALL):
    whole = pl.BlockSpec(memory_space=pltpu.VMEM)
    small = pl.BlockSpec(memory_space=pltpu.SMEM)

    def call(*args):
        return pl.pallas_call(
            kernel,
            out_shape=[jax.ShapeDtypeStruct(shape, jnp.float32) for shape in shapes]
            + [jax.ShapeDtypeStruct(shape, jnp.int32) for shape in plan],
            in_specs=[small] * scalars + [whole] * (len(args) - scalars),
            out_specs=[whole] * len(shapes) + [small] * len(plan),
            compiler_params=pltpu.CompilerParams(vmem_limit_bytes=16 << 20),
            cost_estimate=cost,
            name=name,
        )(*args)

    return call


def position():
    row = lax.axis_index("row")
    return row // 8, (row // 2) % 4, row % 2, lax.axis_index("col")


def factor_kernel(own_ref, other_ref, inv_a_ref, across_ref, inv_b_ref):
    even = lax.axis_index("row") % 2 == 0
    own, other = own_ref[...], other_ref[...]
    zero = jnp.where(even, own, other)
    one = jnp.where(even, other, own)
    down = lax.broadcasted_iota(jnp.int32, (HALF, HALF), 0)
    right = lax.broadcasted_iota(jnp.int32, (HALF, HALF), 1)

    def piece(blocks, index):
        rows = blocks[index * 32 : (index + 1) * 32]
        return jnp.concatenate([rows[:, part * HALF : (part + 1) * HALF] for part in range(4)], 0)

    def diagonal(blocks):
        packed = piece(blocks, 0)
        low = jnp.where(down > right, packed, 0.0)
        high = jnp.where(down < right, packed, 0.0)
        edge = jnp.broadcast_to(blocks[128:129, :HALF], (HALF, HALF))
        first = jnp.where(down >= right, packed, jnp.transpose(low))
        second = jnp.where(down < right, packed, jnp.where(down == right, edge, jnp.transpose(high)))
        return first, second

    top, bottom = diagonal(zero)
    inv_a = inverse_factor_256(top, piece(zero, 1), bottom)
    across = jnp.concatenate(
        [
            dot(jnp.concatenate([piece(zero, 2), piece(zero, 3)], 0), inv_a, 0, 1),
            dot(jnp.concatenate([piece(one, 2), piece(one, 3)], 1), inv_a, 1, 1),
        ],
        0,
    )
    square = dot(across, across, 1, 1)
    top, bottom = diagonal(one)
    inv_b = inverse_factor_256(
        top - square[:HALF, :HALF],
        piece(one, 1) - square[HALF:, :HALF],
        bottom - square[HALF:, HALF:],
    )
    inv_a_ref[...] = inv_a
    across_ref[...] = across
    inv_b_ref[...] = inv_b


def factor(own, other):
    return local_call(factor_kernel, "factor", [(PW, PW)] * 3, cost=LARGE)(own, other)


def share_kernel(lead_ref, mate_ref, *outs):
    _, line, core, _ = position()
    for hop in range(4):
        rows = pl.ds(pl.multiple_of(32 * (2 * ((line + hop) % 4) + core), 32), 32)
        for parity in range(2):

            @pl.when(core == parity)
            def _():
                outs[hop][parity] = lead_ref[rows, :]
                outs[hop][1 - parity] = mate_ref[rows, :]


def owners_and_ranks(map_ref, group):
    owners = [map_ref[8 * group + t] // 8 for t in range(8)]
    ranks = [sum((owners[p] == owners[t]).astype(jnp.int32) for p in range(t)) + jnp.int32(0) for t in range(8)]
    return owners, ranks


def sort_kernel(map_ref, *refs):
    ins, outs = refs[:4], refs[4:]
    plane, line, _, _ = position()
    owners, ranks = owners_and_ranks(map_ref, plane)
    for tile in range(8):
        for hop in range(4):

            @pl.when((line - tile // 2) % 4 == hop)
            def _():
                piece = ins[hop][tile % 2]
                for owner in range(4):

                    @pl.when(owners[tile] == owner)
                    def _():
                        outs[owner][pl.ds(ranks[tile], 1)] = piece[None]


def corner_kernel(lead_ref, out_ref):
    plane, line, core, col = position()
    out_ref[...] = jnp.zeros_like(out_ref)
    down = lax.broadcasted_iota(jnp.int32, (HALF, HALF), 0)
    right = lax.broadcasted_iota(jnp.int32, (HALF, HALF), 1)
    places = [[(0, 0), (1, 1), (1, 0), (0, 2), (1, 2)], [(0, 2), (1, 3), (1, 2), (1, 0), (1, 1)]]
    for holder in range(2):

        @pl.when((col == 0) & (plane == 0) & (line == 0) & (core == holder))
        def _():
            blocks = [lead_ref[i * HALF : i * HALF + HALF, j * HALF : j * HALF + HALF] for i, j in places[holder]]
            first, second = blocks[:2]
            for index, block in enumerate([jnp.where(down >= right, first, second)] + blocks[2:]):
                for part in range(4):
                    out_ref[index * 32 : index * 32 + 32, part * HALF : part * HALF + HALF] = block[part * 32 : part * 32 + 32]
            diagonal = jnp.sum(jnp.where(down == right, second, 0.0), axis=0, keepdims=True)
            out_ref[128:, :HALF] = jnp.broadcast_to(diagonal, (8, HALF))


def merge_kernel(*refs):
    parts, block_ref, got_ref, out_ref = refs[:4], refs[4], refs[5], refs[6]
    for index, ref in enumerate(parts):

        @pl.when(lax.axis_index("col") == index)
        def _():
            out_ref[:32] = ref[0]
            out_ref[32:64] = ref[1]

    out_ref[64 : 64 + BLOCK] = block_ref[...] + got_ref[...]
    out_ref[64 + BLOCK :] = jnp.zeros((PAD, LEAD), jnp.float32)


def join_kernel(rows, own_ref, got_ref, *outs):
    outs[0][:rows] = own_ref[:rows]
    outs[0][rows : 2 * rows] = got_ref[:rows]
    block = own_ref[rows : rows + BLOCK] + got_ref[rows : rows + BLOCK]
    if len(outs) == 1:
        outs[0][2 * rows :] = block
    else:
        outs[1][...] = block


def pick_kernel(map_ref, front_ref, *refs):
    outs, plan_ref = refs[:4], refs[4]
    col = lax.axis_index("col")
    row = lax.axis_index("row")
    for group in range(4):
        owners, ranks = owners_and_ranks(map_ref, group)

        @pl.when(col == group)
        def _():
            for tile in range(8):
                for hop in range(4):

                    @pl.when((owners[tile] - col) % 4 == hop)
                    def _():
                        column = pl.multiple_of(ranks[tile] * PW, PW)
                        outs[hop][:, pl.ds(column, PW)] = front_ref[:, tile * PW : (tile + 1) * PW]

        for tile in range(8):
            slot = map_ref[8 * group + tile] % 8

            @pl.when(owners[tile] == col)
            def _():
                plan_ref[0, slot] = (col - group) % 4
                plan_ref[1, slot] = jnp.int32(group)
                plan_ref[2, slot] = ranks[tile]
                plan_ref[3, slot] = ((row >= 2) & (8 * group + tile >= 2)).astype(jnp.int32)


def weight_kernel(*refs):
    rows, inverse = refs[:3], refs[3:6]
    panel_ref, weight_ref, rows_ref = refs[6:]
    for index, ref in enumerate(rows):

        @pl.when(jnp.minimum(lax.axis_index("col"), 2) == index)
        def _():
            rows_ref[...] = ref[...]

    inv_a, across, inv_b = [ref[...] for ref in inverse]
    panel_a = dot(rows_ref[:, :PW], inv_a, 1, 1)
    panel_b = dot(rows_ref[:, PW:] - dot(panel_a, across, 1, 1), inv_b, 1, 1)
    weight_b = dot(panel_b, inv_b, 1, 0)
    panel_ref[:, :PW] = panel_a
    panel_ref[:, PW:] = jnp.where(lax.axis_index("row") == 0, 0.0, panel_b)
    weight_ref[:, :PW] = dot(panel_a - dot(weight_b, across, 1, 0), inv_a, 1, 0)
    weight_ref[:, PW:] = weight_b


def weigh(rows, inverse):
    whole = pl.BlockSpec(memory_space=pltpu.VMEM)
    shape = (rows[0].shape[0], LEAD)
    return pl.pallas_call(
        weight_kernel,
        out_shape=[jax.ShapeDtypeStruct(shape, jnp.float32)] * 2,
        in_specs=[whole] * 6,
        out_specs=[whole] * 2,
        scratch_shapes=[pltpu.VMEM(shape, jnp.float32)],
        compiler_params=pltpu.CompilerParams(vmem_limit_bytes=16 << 20),
        cost_estimate=SMALL,
        name="weigh",
    )(*rows, *inverse)


def update_kernel(plan, *refs):
    weight_ref, pieces, gathered = refs[0], refs[1:5], refs[5:9]
    base_ref, out_ref, ahead_ref = refs[9:]
    slot = pl.program_id(0)
    plane, line, core, _ = position()
    group, place = plan[1, slot], plan[2, slot]
    for parity in range(2):
        holder = core if parity == 0 else 1 - core
        for x in range(4):
            off_z, off_x = plane ^ group, line ^ x
            first = jnp.where(holder == 0, off_x, off_z)
            second = jnp.where(holder == 0, off_z, off_x)
            index = (first >> 1) + 2 * ((second & 1) ^ (second >> 1)) + 4 * (second >> 1)
            rows = pl.ds(pl.multiple_of(index * 64 + place * 32, 32), 32)
            into = pl.ds(pl.multiple_of((2 * x + holder) * 32, 32), 32)
            late = ((first & 1) ^ (first >> 1)) == 1
            ahead_ref[into, :] = jnp.where(late, gathered[2 * parity + 1][rows, :], gathered[2 * parity][rows, :])

    product = dot(weight_ref[...], ahead_ref[...], 1, 1)
    column = pl.multiple_of(place * PW, PW)
    base = base_ref[...]

    @pl.when(plan[3, slot] == 0)
    def _():
        out_ref[...] = base

    for index, ref in enumerate(pieces):

        @pl.when((plan[0, slot] == index) & (plan[3, slot] == 1))
        def _():
            out_ref[...] = base + (ref[:, pl.ds(column, PW)] - product)


def update(plan, weight, pieces, gathered, base):
    height, width = base.shape
    whole = pl.BlockSpec(memory_space=pltpu.VMEM)
    tile = pl.BlockSpec((height, PW), lambda u, plan: (0, u))
    return pl.pallas_call(
        update_kernel,
        out_shape=jax.ShapeDtypeStruct(base.shape, jnp.float32),
        grid_spec=pltpu.PrefetchScalarGridSpec(
            num_scalar_prefetch=1,
            grid=(width // PW,),
            in_specs=[whole] * 9 + [tile],
            out_specs=tile,
            scratch_shapes=[pltpu.VMEM((PW, LEAD), jnp.float32)],
        ),
        compiler_params=pltpu.CompilerParams(vmem_limit_bytes=16 << 20),
        name="update",
    )(plan, weight, *pieces, *gathered, base)


def doubling_steps():
    every = []
    for step in range(4):
        flip = 1 if step % 2 == 0 else 3
        pairs = []
        for z in range(4):
            for x in range(4):
                for core in range(2):
                    to = (z, x ^ flip) if step // 2 == core else (z ^ flip, x)
                    pairs.append(((z * 4 + x) * 2 + core, (to[0] * 4 + to[1]) * 2 + core))
        every.append(pairs)
    return every, [pair for pair in every[0] if pair[0] < 2]


def shards(front, ancestor, tile_map):
    height = front.shape[0]
    swap = [(i, i ^ 1) for i in range(32)]
    part = (2, 32, LEAD)
    lead = front[:, :LEAD]

    ring = [[(i, (i + hop) % 4) for i in range(4)] for hop in range(4)]

    blocks = [local_call(corner_kernel, "corner", [(BLOCK, LEAD)])(lead)[0]]
    for to in range(1, 4):
        blocks.append(lax.ppermute(blocks[0], ("row", "col"), [(4 * core, 4 * core + to) for core in range(2)]))

    mate = lax.ppermute(lead, "row", swap)
    parts = list(local_call(share_kernel, "share", [part] * 4)(lead, mate))
    for hop in range(1, 4):
        pairs = [(i, i // 8 * 8 + (i + 2 * hop) % 8) for i in range(2, 32)]
        parts[hop] = lax.ppermute(parts[hop], "row", pairs)
    parts = list(local_call(sort_kernel, "sort", [part] * 4, 1)(tile_map, *parts))
    blocks, parts = lax.optimization_barrier((blocks, parts))

    every, spread = doubling_steps()
    for to in range(1, 4):
        parts[to] = lax.ppermute(parts[to], "col", [(0, to)])
    block = (blocks[0] + blocks[1]) + (blocks[2] + blocks[3])
    got = lax.ppermute(block, "row", spread)
    block, got, parts = lax.optimization_barrier((block, got, parts))
    load = local_call(merge_kernel, "merge", [(64 + BLOCK + PAD, LEAD)])(*parts, block, got)[0]

    *pieces, plan = local_call(pick_kernel, "pick", [(height, 2 * PW)] * 4, 1, [(4, 8)])(tile_map, front)

    load, lead = lax.optimization_barrier((load, lead))
    near = lax.ppermute(lead, "col", [(0, 1)])
    load = local_call(partial(join_kernel, 64), "join", [(128 + BLOCK, LEAD)])(load, lax.ppermute(load, "row", every[1]))[0]
    load, near, *pieces = lax.optimization_barrier((load, near, *pieces))
    far = lax.ppermute(jnp.where(lax.axis_index("col") == 1, near, lead), "col", [(0, 3), (1, 2)])
    load = local_call(partial(join_kernel, 128), "join", [(256 + BLOCK, LEAD)])(load, lax.ppermute(load, "row", every[2]))[0]
    load, far, *pieces = lax.optimization_barrier((load, far, *pieces))
    gathered, block = local_call(partial(join_kernel, 256), "join", [(512, LEAD), (BLOCK, LEAD)])(
        load, lax.ppermute(load, "row", every[3])
    )
    for hop in (1, 3):
        pieces[hop] = lax.ppermute(pieces[hop], "col", ring[hop])
    block, gathered, *pieces = lax.optimization_barrier((block, gathered, *pieces))
    other = lax.ppermute(block, "row", swap)
    late = lax.ppermute(gathered, "row", every[0])
    pieces[2] = lax.ppermute(pieces[2], "col", ring[2])
    other_gathered = lax.ppermute(gathered, "row", swap)

    inverse = factor(block, other)
    late, other_gathered, inverse, pieces = lax.optimization_barrier((late, other_gathered, inverse, pieces))
    other_late = lax.ppermute(late, "row", swap)
    panel, weight = weigh([lead, near, far], inverse)
    updated = update(plan, weight, pieces, [gathered, late, other_gathered, other_late], ancestor)
    return panel, updated


def solution(mesh):
    return jax.shard_map(
        shards,
        mesh=mesh,
        in_specs=(P("row", "col"), P("row", "col"), P()),
        out_specs=(P("row", None), P("row", "col")),
        check_vma=False,
    )
```

```python
from functools import partial

import jax
import jax.numpy as jnp
from jax import lax
from jax.experimental import pallas as pl
from jax.experimental.pallas import tpu as pltpu
from jax.sharding import PartitionSpec as P

PW = 256
LEAD = 512
HALF = 128
STEP = 8
TURN = 2
BLOCK = 136
PAD = 64
LARGE = pl.CostEstimate(flops=20 << 30, bytes_accessed=1 << 20, transcendentals=0)
SMALL = pl.CostEstimate(flops=1 << 10, bytes_accessed=1 << 10, transcendentals=0)
HIGHEST = lax.Precision.HIGHEST


def dot(a, b, ca, cb):
    return lax.dot_general(
        a, b, (((ca,), (cb,)), ((), ())), precision=HIGHEST, preferred_element_type=jnp.float32
    )


def spread_lane(rows, index):
    return jnp.broadcast_to(rows[:, index : index + 1], rows.shape)


def spread_row(rows, index):
    return jnp.broadcast_to(rows[index : index + 1, :], rows.shape)


def inverse_factor_128(square):
    n = HALF
    lane = lax.broadcasted_iota(jnp.int32, (STEP, n), 1)
    sub = lax.broadcasted_iota(jnp.int32, (STEP, n), 0)
    lane_turn = lax.broadcasted_iota(jnp.int32, (TURN * STEP, n), 1)
    count = n // STEP
    groups = [square[STEP * t : STEP * (t + 1), :] for t in range(count)]
    for turn in range(0, count, TURN):
        for step in range(turn, turn + TURN):
            start = STEP * step
            inside = (lane >= start) & (lane < start + STEP)
            top = groups[step]
            columns = [spread_lane(top, start + i) for i in range(STEP)]
            entry = [[spread_row(columns[i], j) if i <= j else None for i in range(STEP)] for j in range(STEP)]
            top = jnp.where(inside, jnp.where(lane - start == sub, 1.0, 0.0), top)
            rows = [spread_row(top, j) for j in range(STEP)]
            near = range(step + 1, min(turn + 2 * TURN, count))
            beside = {t: [spread_lane(groups[t], start + i) for i in range(STEP)] for t in near}
            for t in near:
                groups[t] = jnp.where(inside, 0.0, groups[t])
            done = [None] * STEP
            for i in range(STEP):
                scale = lax.rsqrt(entry[i][i])
                below = [None] * STEP
                for j in range(i + 1, STEP):
                    below[j] = entry[j][i] * scale
                    for k in range(i + 1, j + 1):
                        entry[j][k] = entry[j][k] - below[j] * below[k]
                done[i] = rows[i] * scale
                for j in range(i + 1, STEP):
                    rows[j] = rows[j] - below[j] * done[i]
                for t in near:
                    column = beside[t][i] * scale
                    for k in range(i + 1, STEP):
                        beside[t][k] = beside[t][k] - column * below[k]
                    groups[t] = groups[t] - column * done[i]
            solved = done[0]
            for i in range(1, STEP):
                solved = jnp.where(sub == i, done[i], solved)
            for t in range(step):
                groups[t] = jnp.where(inside, 0.0, groups[t])
            groups[step] = solved
        far = range(turn + 2 * TURN, count)
        if far:
            start, end = STEP * turn, STEP * (turn + TURN)
            solved = jnp.concatenate(groups[turn : turn + TURN], 0)
            ahead = jnp.where(lane_turn >= end + STEP * TURN, solved, 0.0)
            product = dot(ahead, solved, 0, 0)
            inside = (lane >= start) & (lane < end)
            for t in far:
                groups[t] = jnp.where(inside, 0.0, groups[t]) - product[STEP * t : STEP * (t + 1), :]
    return jnp.concatenate(groups, 0)


def inverse_factor_256(top, left, bottom):
    first = inverse_factor_128(top)
    across = dot(left, first, 1, 1)
    second = inverse_factor_128(bottom - dot(across, across, 1, 1))
    lower = -dot(second, dot(across, first, 1, 0), 1, 0)
    return jnp.concatenate(
        [
            jnp.concatenate([first, jnp.zeros_like(first)], 1),
            jnp.concatenate([lower, second], 1),
        ],
        0,
    )


def local_call(kernel, name, shapes, scalars=0, plan=(), cost=SMALL):
    whole = pl.BlockSpec(memory_space=pltpu.VMEM)
    small = pl.BlockSpec(memory_space=pltpu.SMEM)

    def call(*args):
        return pl.pallas_call(
            kernel,
            out_shape=[jax.ShapeDtypeStruct(shape, jnp.float32) for shape in shapes]
            + [jax.ShapeDtypeStruct(shape, jnp.int32) for shape in plan],
            in_specs=[small] * scalars + [whole] * (len(args) - scalars),
            out_specs=[whole] * len(shapes) + [small] * len(plan),
            compiler_params=pltpu.CompilerParams(vmem_limit_bytes=16 << 20),
            cost_estimate=cost,
            name=name,
        )(*args)

    return call


def position():
    row = lax.axis_index("row")
    return row // 8, (row // 2) % 4, row % 2, lax.axis_index("col")


def factor_kernel(own_ref, other_ref, inv_a_ref, across_ref, inv_b_ref):
    even = lax.axis_index("row") % 2 == 0
    own, other = own_ref[...], other_ref[...]
    zero = jnp.where(even, own, other)
    one = jnp.where(even, other, own)
    down = lax.broadcasted_iota(jnp.int32, (HALF, HALF), 0)
    right = lax.broadcasted_iota(jnp.int32, (HALF, HALF), 1)

    def piece(blocks, index):
        rows = blocks[index * 32 : (index + 1) * 32]
        return jnp.concatenate([rows[:, part * HALF : (part + 1) * HALF] for part in range(4)], 0)

    def diagonal(blocks):
        packed = piece(blocks, 0)
        low = jnp.where(down > right, packed, 0.0)
        high = jnp.where(down < right, packed, 0.0)
        edge = jnp.broadcast_to(blocks[128:129, :HALF], (HALF, HALF))
        first = jnp.where(down >= right, packed, jnp.transpose(low))
        second = jnp.where(down < right, packed, jnp.where(down == right, edge, jnp.transpose(high)))
        return first, second

    top, bottom = diagonal(zero)
    inv_a = inverse_factor_256(top, piece(zero, 1), bottom)
    across = jnp.concatenate(
        [
            dot(jnp.concatenate([piece(zero, 2), piece(zero, 3)], 0), inv_a, 0, 1),
            dot(jnp.concatenate([piece(one, 2), piece(one, 3)], 1), inv_a, 1, 1),
        ],
        0,
    )
    square = dot(across, across, 1, 1)
    top, bottom = diagonal(one)
    inv_b = inverse_factor_256(
        top - square[:HALF, :HALF],
        piece(one, 1) - square[HALF:, :HALF],
        bottom - square[HALF:, HALF:],
    )
    inv_a_ref[...] = inv_a
    across_ref[...] = across
    inv_b_ref[...] = inv_b


def factor(own, other):
    return local_call(factor_kernel, "factor", [(PW, PW)] * 3, cost=LARGE)(own, other)


def share_kernel(lead_ref, mate_ref, *outs):
    _, line, core, _ = position()
    for hop in range(4):
        rows = pl.ds(pl.multiple_of(32 * (2 * ((line + hop) % 4) + core), 32), 32)
        for parity in range(2):

            @pl.when(core == parity)
            def _():
                outs[hop][parity] = lead_ref[rows, :]
                outs[hop][1 - parity] = mate_ref[rows, :]


def owners_and_ranks(map_ref, group):
    owners = [map_ref[8 * group + t] // 8 for t in range(8)]
    ranks = [sum((owners[p] == owners[t]).astype(jnp.int32) for p in range(t)) + jnp.int32(0) for t in range(8)]
    return owners, ranks


def sort_kernel(map_ref, *refs):
    ins, outs = refs[:4], refs[4:]
    plane, line, _, _ = position()
    owners, ranks = owners_and_ranks(map_ref, plane)
    for tile in range(8):
        for hop in range(4):

            @pl.when((line - tile // 2) % 4 == hop)
            def _():
                piece = ins[hop][tile % 2]
                for owner in range(4):

                    @pl.when(owners[tile] == owner)
                    def _():
                        outs[owner][pl.ds(ranks[tile], 1)] = piece[None]


def corner_kernel(lead_ref, out_ref):
    plane, line, core, col = position()
    out_ref[...] = jnp.zeros_like(out_ref)
    down = lax.broadcasted_iota(jnp.int32, (HALF, HALF), 0)
    right = lax.broadcasted_iota(jnp.int32, (HALF, HALF), 1)
    places = [[(0, 0), (1, 1), (1, 0), (0, 2), (1, 2)], [(0, 2), (1, 3), (1, 2), (1, 0), (1, 1)]]
    for holder in range(2):

        @pl.when((col == 0) & (plane == 0) & (line == 0) & (core == holder))
        def _():
            blocks = [lead_ref[i * HALF : i * HALF + HALF, j * HALF : j * HALF + HALF] for i, j in places[holder]]
            first, second = blocks[:2]
            for index, block in enumerate([jnp.where(down >= right, first, second)] + blocks[2:]):
                for part in range(4):
                    out_ref[index * 32 : index * 32 + 32, part * HALF : part * HALF + HALF] = block[part * 32 : part * 32 + 32]
            diagonal = jnp.sum(jnp.where(down == right, second, 0.0), axis=0, keepdims=True)
            out_ref[128:, :HALF] = jnp.broadcast_to(diagonal, (8, HALF))


def merge_kernel(*refs):
    parts, block_ref, got_ref, out_ref = refs[:4], refs[4], refs[5], refs[6]
    for index, ref in enumerate(parts):

        @pl.when(lax.axis_index("col") == index)
        def _():
            out_ref[:32] = ref[0]
            out_ref[32:64] = ref[1]

    out_ref[64 : 64 + BLOCK] = block_ref[...] + got_ref[...]
    out_ref[64 + BLOCK :] = jnp.zeros((PAD, LEAD), jnp.float32)


def join_kernel(rows, own_ref, got_ref, *outs):
    outs[0][:rows] = own_ref[:rows]
    outs[0][rows : 2 * rows] = got_ref[:rows]
    block = own_ref[rows : rows + BLOCK] + got_ref[rows : rows + BLOCK]
    if len(outs) == 1:
        outs[0][2 * rows :] = block
    else:
        outs[1][...] = block


def pick_kernel(map_ref, front_ref, *refs):
    outs, plan_ref = refs[:4], refs[4]
    col = lax.axis_index("col")
    row = lax.axis_index("row")
    for group in range(4):
        owners, ranks = owners_and_ranks(map_ref, group)

        @pl.when(col == group)
        def _():
            for tile in range(8):
                for hop in range(4):

                    @pl.when((owners[tile] - col) % 4 == hop)
                    def _():
                        column = pl.multiple_of(ranks[tile] * PW, PW)
                        outs[hop][:, pl.ds(column, PW)] = front_ref[:, tile * PW : (tile + 1) * PW]

        for tile in range(8):
            slot = map_ref[8 * group + tile] % 8

            @pl.when(owners[tile] == col)
            def _():
                plan_ref[0, slot] = (col - group) % 4
                plan_ref[1, slot] = jnp.int32(group)
                plan_ref[2, slot] = ranks[tile]
                plan_ref[3, slot] = ((row >= 2) & (8 * group + tile >= 2)).astype(jnp.int32)


def weight_kernel(*refs):
    rows, inverse = refs[:3], refs[3:6]
    panel_ref, weight_ref, rows_ref = refs[6:]
    for index, ref in enumerate(rows):

        @pl.when(jnp.minimum(lax.axis_index("col"), 2) == index)
        def _():
            rows_ref[...] = ref[...]

    inv_a, across, inv_b = [ref[...] for ref in inverse]
    panel_a = dot(rows_ref[:, :PW], inv_a, 1, 1)
    panel_b = dot(rows_ref[:, PW:] - dot(panel_a, across, 1, 1), inv_b, 1, 1)
    weight_b = dot(panel_b, inv_b, 1, 0)
    panel_ref[:, :PW] = panel_a
    panel_ref[:, PW:] = jnp.where(lax.axis_index("row") == 0, 0.0, panel_b)
    weight_ref[:, :PW] = dot(panel_a - dot(weight_b, across, 1, 0), inv_a, 1, 0)
    weight_ref[:, PW:] = weight_b


def weigh(rows, inverse):
    whole = pl.BlockSpec(memory_space=pltpu.VMEM)
    shape = (rows[0].shape[0], LEAD)
    return pl.pallas_call(
        weight_kernel,
        out_shape=[jax.ShapeDtypeStruct(shape, jnp.float32)] * 2,
        in_specs=[whole] * 6,
        out_specs=[whole] * 2,
        scratch_shapes=[pltpu.VMEM(shape, jnp.float32)],
        compiler_params=pltpu.CompilerParams(vmem_limit_bytes=16 << 20),
        cost_estimate=SMALL,
        name="weigh",
    )(*rows, *inverse)


def update_kernel(plan, *refs):
    weight_ref, pieces, gathered = refs[0], refs[1:5], refs[5:9]
    base_ref, out_ref, ahead_ref = refs[9:]
    slot = pl.program_id(0)
    plane, line, core, _ = position()
    group, place = plan[1, slot], plan[2, slot]
    for parity in range(2):
        holder = core if parity == 0 else 1 - core
        for x in range(4):
            off_z, off_x = plane ^ group, line ^ x
            first = jnp.where(holder == 0, off_x, off_z)
            second = jnp.where(holder == 0, off_z, off_x)
            index = (first >> 1) + 2 * ((second & 1) ^ (second >> 1)) + 4 * (second >> 1)
            rows = pl.ds(pl.multiple_of(index * 64 + place * 32, 32), 32)
            into = pl.ds(pl.multiple_of((2 * x + holder) * 32, 32), 32)
            late = ((first & 1) ^ (first >> 1)) == 1
            ahead_ref[into, :] = jnp.where(late, gathered[2 * parity + 1][rows, :], gathered[2 * parity][rows, :])

    product = dot(weight_ref[...], ahead_ref[...], 1, 1)
    column = pl.multiple_of(place * PW, PW)
    base = base_ref[:, pl.ds(pl.multiple_of(slot * PW, PW), PW)]

    @pl.when(plan[3, slot] == 0)
    def _():
        out_ref[...] = base

    for index, ref in enumerate(pieces):

        @pl.when((plan[0, slot] == index) & (plan[3, slot] == 1))
        def _():
            out_ref[...] = base + (ref[:, pl.ds(column, PW)] - product)


def update(plan, weight, pieces, gathered, base):
    height, width = base.shape
    whole = pl.BlockSpec(memory_space=pltpu.VMEM)
    tile = pl.BlockSpec((height, PW), lambda u, plan: (0, u))
    return pl.pallas_call(
        update_kernel,
        out_shape=jax.ShapeDtypeStruct(base.shape, jnp.float32),
        grid_spec=pltpu.PrefetchScalarGridSpec(
            num_scalar_prefetch=1,
            grid=(width // PW,),
            in_specs=[whole] * 10,
            out_specs=tile,
            scratch_shapes=[pltpu.VMEM((PW, LEAD), jnp.float32)],
        ),
        compiler_params=pltpu.CompilerParams(vmem_limit_bytes=16 << 20),
        name="update",
    )(plan, weight, *pieces, *gathered, base)


def doubling_steps():
    every = []
    for step in range(4):
        flip = 1 if step % 2 == 0 else 3
        pairs = []
        for z in range(4):
            for x in range(4):
                for core in range(2):
                    to = (z, x ^ flip) if step // 2 == core else (z ^ flip, x)
                    pairs.append(((z * 4 + x) * 2 + core, (to[0] * 4 + to[1]) * 2 + core))
        every.append(pairs)
    return every, [pair for pair in every[0] if pair[0] < 2]


def shards(front, ancestor, tile_map):
    height = front.shape[0]
    swap = [(i, i ^ 1) for i in range(32)]
    part = (2, 32, LEAD)
    lead = front[:, :LEAD]

    ring = [[(i, (i + hop) % 4) for i in range(4)] for hop in range(4)]

    blocks = [local_call(corner_kernel, "corner", [(BLOCK, LEAD)])(lead)[0]]
    for to in range(1, 4):
        blocks.append(lax.ppermute(blocks[0], ("row", "col"), [(4 * core, 4 * core + to) for core in range(2)]))

    mate = lax.ppermute(lead, "row", swap)
    parts = list(local_call(share_kernel, "share", [part] * 4)(lead, mate))
    for hop in range(1, 4):
        pairs = [(i, i // 8 * 8 + (i + 2 * hop) % 8) for i in range(2, 32)]
        parts[hop] = lax.ppermute(parts[hop], "row", pairs)
    parts = list(local_call(sort_kernel, "sort", [part] * 4, 1)(tile_map, *parts))
    blocks, parts = lax.optimization_barrier((blocks, parts))

    every, spread = doubling_steps()
    for to in range(1, 4):
        parts[to] = lax.ppermute(parts[to], "col", [(0, to)])
    block = (blocks[0] + blocks[1]) + (blocks[2] + blocks[3])
    got = lax.ppermute(block, "row", spread)
    block, got, parts = lax.optimization_barrier((block, got, parts))
    load = local_call(merge_kernel, "merge", [(64 + BLOCK + PAD, LEAD)])(*parts, block, got)[0]

    *pieces, plan = local_call(pick_kernel, "pick", [(height, 2 * PW)] * 4, 1, [(4, 8)])(tile_map, front)

    load, lead = lax.optimization_barrier((load, lead))
    near = lax.ppermute(lead, "col", [(0, 1)])
    load = local_call(partial(join_kernel, 64), "join", [(128 + BLOCK, LEAD)])(load, lax.ppermute(load, "row", every[1]))[0]
    load, near, *pieces = lax.optimization_barrier((load, near, *pieces))
    far = lax.ppermute(jnp.where(lax.axis_index("col") == 1, near, lead), "col", [(0, 3), (1, 2)])
    load = local_call(partial(join_kernel, 128), "join", [(256 + BLOCK, LEAD)])(load, lax.ppermute(load, "row", every[2]))[0]
    load, far, *pieces = lax.optimization_barrier((load, far, *pieces))
    gathered, block = local_call(partial(join_kernel, 256), "join", [(512, LEAD), (BLOCK, LEAD)])(
        load, lax.ppermute(load, "row", every[3])
    )
    for hop in (1, 3):
        pieces[hop] = lax.ppermute(pieces[hop], "col", ring[hop])
    block, gathered, *pieces = lax.optimization_barrier((block, gathered, *pieces))
    other = lax.ppermute(block, "row", swap)
    late = lax.ppermute(gathered, "row", every[0])
    pieces[2] = lax.ppermute(pieces[2], "col", ring[2])
    other_gathered = lax.ppermute(gathered, "row", swap)

    inverse = factor(block, other)
    late, other_gathered, inverse, pieces = lax.optimization_barrier((late, other_gathered, inverse, pieces))
    other_late = lax.ppermute(late, "row", swap)
    panel, weight = weigh([lead, near, far], inverse)
    updated = update(plan, weight, pieces, [gathered, late, other_gathered, other_late], ancestor)
    return panel, updated


def solution(mesh):
    return jax.shard_map(
        shards,
        mesh=mesh,
        in_specs=(P("row", "col"), P("row", "col"), P()),
        out_specs=(P("row", None), P("row", "col")),
        check_vma=False,
    )
```

```python
from functools import partial

import jax
import jax.numpy as jnp
from jax import lax
from jax.experimental import pallas as pl
from jax.experimental.pallas import tpu as pltpu
from jax.sharding import PartitionSpec as P

PW = 256
LEAD = 512
HALF = 128
STEP = 8
TURN = 2
BLOCK = 136
PAD = 64
LARGE = pl.CostEstimate(flops=20 << 30, bytes_accessed=1 << 20, transcendentals=0)
SMALL = pl.CostEstimate(flops=1 << 10, bytes_accessed=1 << 10, transcendentals=0)
HIGHEST = lax.Precision.HIGHEST


def dot(a, b, ca, cb):
    return lax.dot_general(
        a, b, (((ca,), (cb,)), ((), ())), precision=HIGHEST, preferred_element_type=jnp.float32
    )


def spread_lane(rows, index):
    return jnp.broadcast_to(rows[:, index : index + 1], rows.shape)


def spread_row(rows, index):
    return jnp.broadcast_to(rows[index : index + 1, :], rows.shape)


def inverse_factor_128(square):
    n = HALF
    lane = lax.broadcasted_iota(jnp.int32, (STEP, n), 1)
    sub = lax.broadcasted_iota(jnp.int32, (STEP, n), 0)
    lane_turn = lax.broadcasted_iota(jnp.int32, (TURN * STEP, n), 1)
    count = n // STEP
    groups = [square[STEP * t : STEP * (t + 1), :] for t in range(count)]
    for turn in range(0, count, TURN):
        for step in range(turn, turn + TURN):
            start = STEP * step
            inside = (lane >= start) & (lane < start + STEP)
            top = groups[step]
            columns = [spread_lane(top, start + i) for i in range(STEP)]
            entry = [[spread_row(columns[i], j) if i <= j else None for i in range(STEP)] for j in range(STEP)]
            top = jnp.where(inside, jnp.where(lane - start == sub, 1.0, 0.0), top)
            rows = [spread_row(top, j) for j in range(STEP)]
            near = range(step + 1, min(turn + 2 * TURN, count))
            beside = {t: [spread_lane(groups[t], start + i) for i in range(STEP)] for t in near}
            for t in near:
                groups[t] = jnp.where(inside, 0.0, groups[t])
            done = [None] * STEP
            for i in range(STEP):
                scale = lax.rsqrt(entry[i][i])
                below = [None] * STEP
                for j in range(i + 1, STEP):
                    below[j] = entry[j][i] * scale
                    for k in range(i + 1, j + 1):
                        entry[j][k] = entry[j][k] - below[j] * below[k]
                done[i] = rows[i] * scale
                for j in range(i + 1, STEP):
                    rows[j] = rows[j] - below[j] * done[i]
                for t in near:
                    column = beside[t][i] * scale
                    for k in range(i + 1, STEP):
                        beside[t][k] = beside[t][k] - column * below[k]
                    groups[t] = groups[t] - column * done[i]
            solved = done[0]
            for i in range(1, STEP):
                solved = jnp.where(sub == i, done[i], solved)
            for t in range(step):
                groups[t] = jnp.where(inside, 0.0, groups[t])
            groups[step] = solved
        far = range(turn + 2 * TURN, count)
        if far:
            start, end = STEP * turn, STEP * (turn + TURN)
            solved = jnp.concatenate(groups[turn : turn + TURN], 0)
            ahead = jnp.where(lane_turn >= end + STEP * TURN, solved, 0.0)
            product = dot(ahead, solved, 0, 0)
            inside = (lane >= start) & (lane < end)
            for t in far:
                groups[t] = jnp.where(inside, 0.0, groups[t]) - product[STEP * t : STEP * (t + 1), :]
    return jnp.concatenate(groups, 0)


def inverse_factor_256(top, left, bottom):
    first = inverse_factor_128(top)
    across = dot(left, first, 1, 1)
    second = inverse_factor_128(bottom - dot(across, across, 1, 1))
    lower = -dot(second, dot(across, first, 1, 0), 1, 0)
    return jnp.concatenate(
        [
            jnp.concatenate([first, jnp.zeros_like(first)], 1),
            jnp.concatenate([lower, second], 1),
        ],
        0,
    )


def local_call(kernel, name, shapes, scalars=0, plan=(), cost=SMALL):
    whole = pl.BlockSpec(memory_space=pltpu.VMEM)
    small = pl.BlockSpec(memory_space=pltpu.SMEM)

    def call(*args):
        return pl.pallas_call(
            kernel,
            out_shape=[jax.ShapeDtypeStruct(shape, jnp.float32) for shape in shapes]
            + [jax.ShapeDtypeStruct(shape, jnp.int32) for shape in plan],
            in_specs=[small] * scalars + [whole] * (len(args) - scalars),
            out_specs=[whole] * len(shapes) + [small] * len(plan),
            compiler_params=pltpu.CompilerParams(vmem_limit_bytes=16 << 20),
            cost_estimate=cost,
            name=name,
        )(*args)

    return call


def position():
    row = lax.axis_index("row")
    return row // 8, (row // 2) % 4, row % 2, lax.axis_index("col")


def factor_kernel(own_ref, other_ref, inv_a_ref, across_ref, inv_b_ref):
    even = lax.axis_index("row") % 2 == 0
    own, other = own_ref[...], other_ref[...]
    zero = jnp.where(even, own, other)
    one = jnp.where(even, other, own)
    down = lax.broadcasted_iota(jnp.int32, (HALF, HALF), 0)
    right = lax.broadcasted_iota(jnp.int32, (HALF, HALF), 1)

    def piece(blocks, index):
        rows = blocks[index * 32 : (index + 1) * 32]
        return jnp.concatenate([rows[:, part * HALF : (part + 1) * HALF] for part in range(4)], 0)

    def diagonal(blocks):
        packed = piece(blocks, 0)
        low = jnp.where(down > right, packed, 0.0)
        high = jnp.where(down < right, packed, 0.0)
        edge = jnp.broadcast_to(blocks[128:129, :HALF], (HALF, HALF))
        first = jnp.where(down >= right, packed, jnp.transpose(low))
        second = jnp.where(down < right, packed, jnp.where(down == right, edge, jnp.transpose(high)))
        return first, second

    top, bottom = diagonal(zero)
    inv_a = inverse_factor_256(top, piece(zero, 1), bottom)
    across = jnp.concatenate(
        [
            dot(jnp.concatenate([piece(zero, 2), piece(zero, 3)], 0), inv_a, 0, 1),
            dot(jnp.concatenate([piece(one, 2), piece(one, 3)], 1), inv_a, 1, 1),
        ],
        0,
    )
    square = dot(across, across, 1, 1)
    top, bottom = diagonal(one)
    inv_b = inverse_factor_256(
        top - square[:HALF, :HALF],
        piece(one, 1) - square[HALF:, :HALF],
        bottom - square[HALF:, HALF:],
    )
    inv_a_ref[...] = inv_a
    across_ref[...] = across
    inv_b_ref[...] = inv_b


def factor(own, other):
    return local_call(factor_kernel, "factor", [(PW, PW)] * 3, cost=LARGE)(own, other)


def share_kernel(lead_ref, mate_ref, *outs):
    _, line, core, _ = position()
    for hop in range(4):
        rows = pl.ds(pl.multiple_of(32 * (2 * ((line + hop) % 4) + core), 32), 32)
        for parity in range(2):

            @pl.when(core == parity)
            def _():
                outs[hop][parity] = lead_ref[rows, :]
                outs[hop][1 - parity] = mate_ref[rows, :]


def owners_and_ranks(map_ref, group):
    owners = [map_ref[8 * group + t] // 8 for t in range(8)]
    ranks = [sum((owners[p] == owners[t]).astype(jnp.int32) for p in range(t)) + jnp.int32(0) for t in range(8)]
    return owners, ranks


def sort_kernel(map_ref, *refs):
    ins, outs = refs[:4], refs[4:]
    plane, line, _, _ = position()
    owners, ranks = owners_and_ranks(map_ref, plane)
    for tile in range(8):
        for hop in range(4):

            @pl.when((line - tile // 2) % 4 == hop)
            def _():
                piece = ins[hop][tile % 2]
                for owner in range(4):

                    @pl.when(owners[tile] == owner)
                    def _():
                        outs[owner][pl.ds(ranks[tile], 1)] = piece[None]


def corner_kernel(lead_ref, out_ref):
    plane, line, core, col = position()
    out_ref[...] = jnp.zeros_like(out_ref)
    down = lax.broadcasted_iota(jnp.int32, (HALF, HALF), 0)
    right = lax.broadcasted_iota(jnp.int32, (HALF, HALF), 1)
    places = [[(0, 0), (1, 1), (1, 0), (0, 2), (1, 2)], [(0, 2), (1, 3), (1, 2), (1, 0), (1, 1)]]
    for holder in range(2):

        @pl.when((col == 0) & (plane == 0) & (line == 0) & (core == holder))
        def _():
            blocks = [lead_ref[i * HALF : i * HALF + HALF, j * HALF : j * HALF + HALF] for i, j in places[holder]]
            first, second = blocks[:2]
            for index, block in enumerate([jnp.where(down >= right, first, second)] + blocks[2:]):
                for part in range(4):
                    out_ref[index * 32 : index * 32 + 32, part * HALF : part * HALF + HALF] = block[part * 32 : part * 32 + 32]
            diagonal = jnp.sum(jnp.where(down == right, second, 0.0), axis=0, keepdims=True)
            out_ref[128:, :HALF] = jnp.broadcast_to(diagonal, (8, HALF))


def merge_kernel(*refs):
    parts, block_ref, got_ref, out_ref = refs[:4], refs[4], refs[5], refs[6]
    for index, ref in enumerate(parts):

        @pl.when(lax.axis_index("col") == index)
        def _():
            out_ref[:32] = ref[0]
            out_ref[32:64] = ref[1]

    out_ref[64 : 64 + BLOCK] = block_ref[...] + got_ref[...]
    out_ref[64 + BLOCK :] = jnp.zeros((PAD, LEAD), jnp.float32)


def join_kernel(rows, own_ref, got_ref, *outs):
    outs[0][:rows] = own_ref[:rows]
    outs[0][rows : 2 * rows] = got_ref[:rows]
    block = own_ref[rows : rows + BLOCK] + got_ref[rows : rows + BLOCK]
    if len(outs) == 1:
        outs[0][2 * rows :] = block
    else:
        outs[1][...] = block


def pick_kernel(map_ref, front_ref, *refs):
    outs, plan_ref = refs[:4], refs[4]
    col = lax.axis_index("col")
    row = lax.axis_index("row")
    for group in range(4):
        owners, ranks = owners_and_ranks(map_ref, group)

        @pl.when(col == group)
        def _():
            for tile in range(8):
                for hop in range(4):

                    @pl.when((owners[tile] - col) % 4 == hop)
                    def _():
                        column = pl.multiple_of(ranks[tile] * PW, PW)
                        outs[hop][:, pl.ds(column, PW)] = front_ref[:, tile * PW : (tile + 1) * PW]

        for tile in range(8):
            slot = map_ref[8 * group + tile] % 8

            @pl.when(owners[tile] == col)
            def _():
                plan_ref[0, slot] = (col - group) % 4
                plan_ref[1, slot] = jnp.int32(group)
                plan_ref[2, slot] = ranks[tile]
                plan_ref[3, slot] = ((row >= 2) & (8 * group + tile >= 2)).astype(jnp.int32)


def weight_kernel(*refs):
    rows, inverse = refs[:4], refs[4:7]
    panel_ref, weight_ref, rows_ref = refs[7:]
    col = lax.axis_index("col")
    for index in range(2):

        @pl.when(col == index)
        def _():
            rows_ref[...] = rows[index][...]

    @pl.when(col >= 2)
    def _():
        rows_ref[:, :PW] = rows[2][...]
        rows_ref[:, PW:] = rows[3][...]

    inv_a, across, inv_b = [ref[...] for ref in inverse]
    panel_a = dot(rows_ref[:, :PW], inv_a, 1, 1)
    panel_b = dot(rows_ref[:, PW:] - dot(panel_a, across, 1, 1), inv_b, 1, 1)
    weight_b = dot(panel_b, inv_b, 1, 0)
    panel_ref[:, :PW] = panel_a
    panel_ref[:, PW:] = jnp.where(lax.axis_index("row") == 0, 0.0, panel_b)
    weight_ref[:, :PW] = dot(panel_a - dot(weight_b, across, 1, 0), inv_a, 1, 0)
    weight_ref[:, PW:] = weight_b


def weigh(rows, inverse):
    whole = pl.BlockSpec(memory_space=pltpu.VMEM)
    shape = (rows[0].shape[0], LEAD)
    return pl.pallas_call(
        weight_kernel,
        out_shape=[jax.ShapeDtypeStruct(shape, jnp.float32)] * 2,
        in_specs=[whole] * 7,
        out_specs=[whole] * 2,
        scratch_shapes=[pltpu.VMEM(shape, jnp.float32)],
        compiler_params=pltpu.CompilerParams(vmem_limit_bytes=16 << 20),
        cost_estimate=SMALL,
        name="weigh",
    )(*rows, *inverse)


def update_kernel(plan, *refs):
    weight_ref, pieces, gathered = refs[0], refs[1:5], refs[5:9]
    base_ref, out_ref, ahead_ref = refs[9:]
    slot = pl.program_id(0)
    plane, line, core, _ = position()
    group, place = plan[1, slot], plan[2, slot]
    for parity in range(2):
        holder = core if parity == 0 else 1 - core
        for x in range(4):
            off_z, off_x = plane ^ group, line ^ x
            first = jnp.where(holder == 0, off_x, off_z)
            second = jnp.where(holder == 0, off_z, off_x)
            index = (first >> 1) + 2 * ((second & 1) ^ (second >> 1)) + 4 * (second >> 1)
            rows = pl.ds(pl.multiple_of(index * 64 + place * 32, 32), 32)
            into = pl.ds(pl.multiple_of((2 * x + holder) * 32, 32), 32)
            late = ((first & 1) ^ (first >> 1)) == 1
            ahead_ref[into, :] = jnp.where(late, gathered[2 * parity + 1][rows, :], gathered[2 * parity][rows, :])

    product = dot(weight_ref[...], ahead_ref[...], 1, 1)
    column = pl.multiple_of(place * PW, PW)
    base = base_ref[...]

    @pl.when(plan[3, slot] == 0)
    def _():
        out_ref[...] = base

    for index, ref in enumerate(pieces):

        @pl.when((plan[0, slot] == index) & (plan[3, slot] == 1))
        def _():
            out_ref[...] = base + (ref[:, pl.ds(column, PW)] - product)


def update(plan, weight, pieces, gathered, base):
    height, width = base.shape
    whole = pl.BlockSpec(memory_space=pltpu.VMEM)
    tile = pl.BlockSpec((height, PW), lambda u, plan: (0, u))
    return pl.pallas_call(
        update_kernel,
        out_shape=jax.ShapeDtypeStruct(base.shape, jnp.float32),
        grid_spec=pltpu.PrefetchScalarGridSpec(
            num_scalar_prefetch=1,
            grid=(width // PW,),
            in_specs=[whole] * 9 + [tile],
            out_specs=tile,
            scratch_shapes=[pltpu.VMEM((PW, LEAD), jnp.float32)],
        ),
        compiler_params=pltpu.CompilerParams(vmem_limit_bytes=16 << 20),
        name="update",
    )(plan, weight, *pieces, *gathered, base)


def doubling_steps():
    every = []
    for step in range(4):
        flip = 1 if step % 2 == 0 else 3
        pairs = []
        for z in range(4):
            for x in range(4):
                for core in range(2):
                    to = (z, x ^ flip) if step // 2 == core else (z ^ flip, x)
                    pairs.append(((z * 4 + x) * 2 + core, (to[0] * 4 + to[1]) * 2 + core))
        every.append(pairs)
    return every, [pair for pair in every[0] if pair[0] < 2]


def shards(front, ancestor, tile_map):
    height = front.shape[0]
    swap = [(i, i ^ 1) for i in range(32)]
    part = (2, 32, LEAD)
    lead = front[:, :LEAD]

    ring = [[(i, (i + hop) % 4) for i in range(4)] for hop in range(4)]

    blocks = [local_call(corner_kernel, "corner", [(BLOCK, LEAD)])(lead)[0]]
    for to in range(1, 4):
        blocks.append(lax.ppermute(blocks[0], ("row", "col"), [(4 * core, 4 * core + to) for core in range(2)]))

    mate = lax.ppermute(lead, "row", swap)
    parts = list(local_call(share_kernel, "share", [part] * 4)(lead, mate))
    for hop in range(1, 4):
        pairs = [(i, i // 8 * 8 + (i + 2 * hop) % 8) for i in range(2, 32)]
        parts[hop] = lax.ppermute(parts[hop], "row", pairs)
    parts = list(local_call(sort_kernel, "sort", [part] * 4, 1)(tile_map, *parts))
    blocks, parts = lax.optimization_barrier((blocks, parts))

    every, spread = doubling_steps()
    for to in range(1, 4):
        parts[to] = lax.ppermute(parts[to], "col", [(0, to)])
    block = (blocks[0] + blocks[1]) + (blocks[2] + blocks[3])
    got = lax.ppermute(block, "row", spread)
    block, got, parts = lax.optimization_barrier((block, got, parts))
    load = local_call(merge_kernel, "merge", [(64 + BLOCK + PAD, LEAD)])(*parts, block, got)[0]

    *pieces, plan = local_call(pick_kernel, "pick", [(height, 2 * PW)] * 4, 1, [(4, 8)])(tile_map, front)

    load, lead = lax.optimization_barrier((load, lead))
    near = lax.ppermute(lead, "col", [(0, 1)])
    load = local_call(partial(join_kernel, 64), "join", [(128 + BLOCK, LEAD)])(load, lax.ppermute(load, "row", every[1]))[0]
    load, near, *pieces = lax.optimization_barrier((load, near, *pieces))
    hold = jnp.where(lax.axis_index("col") == 1, near, lead)
    onward = [(0, 3), (1, 2)]
    far = [lax.ppermute(hold[:, :PW], "col", onward), hold[:, PW:]]
    load = local_call(partial(join_kernel, 128), "join", [(256 + BLOCK, LEAD)])(load, lax.ppermute(load, "row", every[2]))[0]
    load, far, *pieces = lax.optimization_barrier((load, far, *pieces))
    far[1] = lax.ppermute(far[1], "col", onward)
    gathered, block = local_call(partial(join_kernel, 256), "join", [(512, LEAD), (BLOCK, LEAD)])(
        load, lax.ppermute(load, "row", every[3])
    )
    for hop in (1, 3):
        pieces[hop] = lax.ppermute(pieces[hop], "col", ring[hop])
    block, gathered, far, *pieces = lax.optimization_barrier((block, gathered, far, *pieces))
    other = lax.ppermute(block, "row", swap)
    late = lax.ppermute(gathered, "row", every[0])
    pieces[2] = lax.ppermute(pieces[2], "col", ring[2])
    other_gathered = lax.ppermute(gathered, "row", swap)

    inverse = factor(block, other)
    late, other_gathered, inverse, pieces = lax.optimization_barrier((late, other_gathered, inverse, pieces))
    other_late = lax.ppermute(late, "row", swap)
    panel, weight = weigh([lead, near, *far], inverse)
    updated = update(plan, weight, pieces, [gathered, late, other_gathered, other_late], ancestor)
    return panel, updated


def solution(mesh):
    return jax.shard_map(
        shards,
        mesh=mesh,
        in_specs=(P("row", "col"), P("row", "col"), P()),
        out_specs=(P("row", None), P("row", "col")),
        check_vma=False,
    )
```

```python
from functools import partial

import jax
import jax.numpy as jnp
from jax import lax
from jax.experimental import pallas as pl
from jax.experimental.pallas import tpu as pltpu
from jax.sharding import PartitionSpec as P

PW = 256
LEAD = 512
HALF = 128
STEP = 8
TURN = 2
BLOCK = 136
PAD = 64
LARGE = pl.CostEstimate(flops=20 << 30, bytes_accessed=1 << 20, transcendentals=0)
SMALL = pl.CostEstimate(flops=1 << 10, bytes_accessed=1 << 10, transcendentals=0)
HIGHEST = lax.Precision.HIGHEST


def dot(a, b, ca, cb):
    return lax.dot_general(
        a, b, (((ca,), (cb,)), ((), ())), precision=HIGHEST, preferred_element_type=jnp.float32
    )


def spread_lane(rows, index):
    return jnp.broadcast_to(rows[:, index : index + 1], rows.shape)


def spread_row(rows, index):
    return jnp.broadcast_to(rows[index : index + 1, :], rows.shape)


def inverse_factor_128(square):
    n = HALF
    lane = lax.broadcasted_iota(jnp.int32, (STEP, n), 1)
    sub = lax.broadcasted_iota(jnp.int32, (STEP, n), 0)
    lane_turn = lax.broadcasted_iota(jnp.int32, (TURN * STEP, n), 1)
    count = n // STEP
    groups = [square[STEP * t : STEP * (t + 1), :] for t in range(count)]
    for turn in range(0, count, TURN):
        for step in range(turn, turn + TURN):
            start = STEP * step
            inside = (lane >= start) & (lane < start + STEP)
            top = groups[step]
            columns = [spread_lane(top, start + i) for i in range(STEP)]
            entry = [[spread_row(columns[i], j) if i <= j else None for i in range(STEP)] for j in range(STEP)]
            top = jnp.where(inside, jnp.where(lane - start == sub, 1.0, 0.0), top)
            rows = [spread_row(top, j) for j in range(STEP)]
            near = range(step + 1, min(turn + 2 * TURN, count))
            beside = {t: [spread_lane(groups[t], start + i) for i in range(STEP)] for t in near}
            for t in near:
                groups[t] = jnp.where(inside, 0.0, groups[t])
            done = [None] * STEP
            for i in range(STEP):
                scale = lax.rsqrt(entry[i][i])
                below = [None] * STEP
                for j in range(i + 1, STEP):
                    below[j] = entry[j][i] * scale
                    for k in range(i + 1, j + 1):
                        entry[j][k] = entry[j][k] - below[j] * below[k]
                done[i] = rows[i] * scale
                for j in range(i + 1, STEP):
                    rows[j] = rows[j] - below[j] * done[i]
                for t in near:
                    column = beside[t][i] * scale
                    for k in range(i + 1, STEP):
                        beside[t][k] = beside[t][k] - column * below[k]
                    groups[t] = groups[t] - column * done[i]
            solved = done[0]
            for i in range(1, STEP):
                solved = jnp.where(sub == i, done[i], solved)
            for t in range(step):
                groups[t] = jnp.where(inside, 0.0, groups[t])
            groups[step] = solved
        far = range(turn + 2 * TURN, count)
        if far:
            start, end = STEP * turn, STEP * (turn + TURN)
            solved = jnp.concatenate(groups[turn : turn + TURN], 0)
            ahead = jnp.where(lane_turn >= end + STEP * TURN, solved, 0.0)
            product = dot(ahead, solved, 0, 0)
            inside = (lane >= start) & (lane < end)
            for t in far:
                groups[t] = jnp.where(inside, 0.0, groups[t]) - product[STEP * t : STEP * (t + 1), :]
    return jnp.concatenate(groups, 0)


def inverse_factor_256(top, left, bottom):
    first = inverse_factor_128(top)
    across = dot(left, first, 1, 1)
    second = inverse_factor_128(bottom - dot(across, across, 1, 1))
    lower = -dot(second, dot(across, first, 1, 0), 1, 0)
    return jnp.concatenate(
        [
            jnp.concatenate([first, jnp.zeros_like(first)], 1),
            jnp.concatenate([lower, second], 1),
        ],
        0,
    )


def local_call(kernel, name, shapes, scalars=0, plan=(), cost=SMALL):
    whole = pl.BlockSpec(memory_space=pltpu.VMEM)
    small = pl.BlockSpec(memory_space=pltpu.SMEM)

    def call(*args):
        return pl.pallas_call(
            kernel,
            out_shape=[jax.ShapeDtypeStruct(shape, jnp.float32) for shape in shapes]
            + [jax.ShapeDtypeStruct(shape, jnp.int32) for shape in plan],
            in_specs=[small] * scalars + [whole] * (len(args) - scalars),
            out_specs=[whole] * len(shapes) + [small] * len(plan),
            compiler_params=pltpu.CompilerParams(vmem_limit_bytes=16 << 20),
            cost_estimate=cost,
            name=name,
        )(*args)

    return call


def position():
    row = lax.axis_index("row")
    return row // 8, (row // 2) % 4, row % 2, lax.axis_index("col")


def factor_kernel(own_ref, other_ref, inv_a_ref, across_ref, inv_b_ref):
    even = lax.axis_index("row") % 2 == 0
    own, other = own_ref[...], other_ref[...]
    zero = jnp.where(even, own, other)
    one = jnp.where(even, other, own)
    down = lax.broadcasted_iota(jnp.int32, (HALF, HALF), 0)
    right = lax.broadcasted_iota(jnp.int32, (HALF, HALF), 1)

    def piece(blocks, index):
        rows = blocks[index * 32 : (index + 1) * 32]
        return jnp.concatenate([rows[:, part * HALF : (part + 1) * HALF] for part in range(4)], 0)

    def diagonal(blocks):
        packed = piece(blocks, 0)
        low = jnp.where(down > right, packed, 0.0)
        high = jnp.where(down < right, packed, 0.0)
        edge = jnp.broadcast_to(blocks[128:129, :HALF], (HALF, HALF))
        first = jnp.where(down >= right, packed, jnp.transpose(low))
        second = jnp.where(down < right, packed, jnp.where(down == right, edge, jnp.transpose(high)))
        return first, second

    top, bottom = diagonal(zero)
    inv_a = inverse_factor_256(top, piece(zero, 1), bottom)
    across = jnp.concatenate(
        [
            dot(jnp.concatenate([piece(zero, 2), piece(zero, 3)], 0), inv_a, 0, 1),
            dot(jnp.concatenate([piece(one, 2), piece(one, 3)], 1), inv_a, 1, 1),
        ],
        0,
    )
    square = dot(across, across, 1, 1)
    top, bottom = diagonal(one)
    inv_b = inverse_factor_256(
        top - square[:HALF, :HALF],
        piece(one, 1) - square[HALF:, :HALF],
        bottom - square[HALF:, HALF:],
    )
    inv_a_ref[...] = inv_a
    across_ref[...] = across
    inv_b_ref[...] = inv_b


def factor(own, other):
    return local_call(factor_kernel, "factor", [(PW, PW)] * 3, cost=LARGE)(own, other)


def share_kernel(lead_ref, mate_ref, *outs):
    _, line, core, _ = position()
    for hop in range(4):
        rows = pl.ds(pl.multiple_of(32 * (2 * ((line + hop) % 4) + core), 32), 32)
        for parity in range(2):

            @pl.when(core == parity)
            def _():
                outs[hop][parity] = lead_ref[rows, :]
                outs[hop][1 - parity] = mate_ref[rows, :]


def owners_and_ranks(map_ref, group):
    owners = [map_ref[8 * group + t] // 8 for t in range(8)]
    ranks = [sum((owners[p] == owners[t]).astype(jnp.int32) for p in range(t)) + jnp.int32(0) for t in range(8)]
    return owners, ranks


def sort_kernel(map_ref, *refs):
    ins, outs = refs[:4], refs[4:]
    plane, line, _, _ = position()
    owners, ranks = owners_and_ranks(map_ref, plane)
    for tile in range(8):
        for hop in range(4):

            @pl.when((line - tile // 2) % 4 == hop)
            def _():
                piece = ins[hop][tile % 2]
                for owner in range(4):

                    @pl.when(owners[tile] == owner)
                    def _():
                        outs[owner][pl.ds(ranks[tile], 1)] = piece[None]


def corner_kernel(lead_ref, out_ref):
    plane, line, core, col = position()
    out_ref[...] = jnp.zeros_like(out_ref)
    down = lax.broadcasted_iota(jnp.int32, (HALF, HALF), 0)
    right = lax.broadcasted_iota(jnp.int32, (HALF, HALF), 1)
    places = [[(0, 0), (1, 1), (1, 0), (0, 2), (1, 2)], [(0, 2), (1, 3), (1, 2), (1, 0), (1, 1)]]
    for holder in range(2):

        @pl.when((col == 0) & (plane == 0) & (line == 0) & (core == holder))
        def _():
            blocks = [lead_ref[i * HALF : i * HALF + HALF, j * HALF : j * HALF + HALF] for i, j in places[holder]]
            first, second = blocks[:2]
            for index, block in enumerate([jnp.where(down >= right, first, second)] + blocks[2:]):
                for part in range(4):
                    out_ref[index * 32 : index * 32 + 32, part * HALF : part * HALF + HALF] = block[part * 32 : part * 32 + 32]
            diagonal = jnp.sum(jnp.where(down == right, second, 0.0), axis=0, keepdims=True)
            out_ref[128:, :HALF] = jnp.broadcast_to(diagonal, (8, HALF))


def merge_kernel(*refs):
    parts, block_ref, got_ref, out_ref = refs[:4], refs[4], refs[5], refs[6]
    for index, ref in enumerate(parts):

        @pl.when(lax.axis_index("col") == index)
        def _():
            out_ref[:32] = ref[0]
            out_ref[32:64] = ref[1]

    out_ref[64 : 64 + BLOCK] = block_ref[...] + got_ref[...]
    out_ref[64 + BLOCK :] = jnp.zeros((PAD, LEAD), jnp.float32)


def join_kernel(rows, own_ref, got_ref, *outs):
    outs[0][:rows] = own_ref[:rows]
    outs[0][rows : 2 * rows] = got_ref[:rows]
    block = own_ref[rows : rows + BLOCK] + got_ref[rows : rows + BLOCK]
    if len(outs) == 1:
        outs[0][2 * rows :] = block
    else:
        outs[1][...] = block


def pick_kernel(map_ref, front_ref, *refs):
    outs, plan_ref = refs[:4], refs[4]
    col = lax.axis_index("col")
    row = lax.axis_index("row")
    for group in range(4):
        owners, ranks = owners_and_ranks(map_ref, group)

        @pl.when(col == group)
        def _():
            for tile in range(8):
                for hop in range(4):

                    @pl.when((owners[tile] - col) % 4 == hop)
                    def _():
                        column = pl.multiple_of(ranks[tile] * PW, PW)
                        outs[hop][:, pl.ds(column, PW)] = front_ref[:, tile * PW : (tile + 1) * PW]

        for tile in range(8):
            slot = map_ref[8 * group + tile] % 8

            @pl.when(owners[tile] == col)
            def _():
                plan_ref[0, slot] = (col - group) % 4
                plan_ref[1, slot] = jnp.int32(group)
                plan_ref[2, slot] = ranks[tile]
                plan_ref[3, slot] = ((row >= 2) & (8 * group + tile >= 2)).astype(jnp.int32)


def weight_kernel(*refs):
    rows, inverse = refs[:4], refs[4:7]
    panel_ref, weight_ref, rows_ref = refs[7:]
    col = lax.axis_index("col")
    for index in range(2):

        @pl.when(col == index)
        def _():
            rows_ref[...] = rows[index][...]

    @pl.when(col >= 2)
    def _():
        rows_ref[:, :PW] = rows[2][...]
        rows_ref[:, PW:] = rows[3][...]

    inv_a, across, inv_b = [ref[...] for ref in inverse]
    panel_a = dot(rows_ref[:, :PW], inv_a, 1, 1)
    panel_b = dot(rows_ref[:, PW:] - dot(panel_a, across, 1, 1), inv_b, 1, 1)
    weight_b = dot(panel_b, inv_b, 1, 0)
    panel_ref[:, :PW] = panel_a
    panel_ref[:, PW:] = jnp.where(lax.axis_index("row") == 0, 0.0, panel_b)
    weight_ref[:, :PW] = dot(panel_a - dot(weight_b, across, 1, 0), inv_a, 1, 0)
    weight_ref[:, PW:] = weight_b


def weigh(rows, inverse):
    whole = pl.BlockSpec(memory_space=pltpu.VMEM)
    shape = (rows[0].shape[0], LEAD)
    return pl.pallas_call(
        weight_kernel,
        out_shape=[jax.ShapeDtypeStruct(shape, jnp.float32)] * 2,
        in_specs=[whole] * 7,
        out_specs=[whole] * 2,
        scratch_shapes=[pltpu.VMEM(shape, jnp.float32)],
        compiler_params=pltpu.CompilerParams(vmem_limit_bytes=16 << 20),
        cost_estimate=SMALL,
        name="weigh",
    )(*rows, *inverse)


def update_kernel(plan, *refs):
    weight_ref, pieces, gathered = refs[0], refs[1:5], refs[5:9]
    base_ref, out_ref, ahead_ref = refs[9:]
    slot = pl.program_id(0)
    plane, line, core, _ = position()
    group, place = plan[1, slot], plan[2, slot]
    for parity in range(2):
        holder = core if parity == 0 else 1 - core
        for x in range(4):
            off_z, off_x = plane ^ group, line ^ x
            first = jnp.where(holder == 0, off_x, off_z)
            second = jnp.where(holder == 0, off_z, off_x)
            index = (first >> 1) + 2 * ((second & 1) ^ (second >> 1)) + 4 * (second >> 1)
            rows = pl.ds(pl.multiple_of(index * 64 + place * 32, 32), 32)
            into = pl.ds(pl.multiple_of((2 * x + holder) * 32, 32), 32)
            late = ((first & 1) ^ (first >> 1)) == 1
            ahead_ref[into, :] = jnp.where(late, gathered[2 * parity + 1][rows, :], gathered[2 * parity][rows, :])

    product = dot(weight_ref[...], ahead_ref[...], 1, 1)
    column = pl.multiple_of(place * PW, PW)
    base = base_ref[...]

    @pl.when(plan[3, slot] == 0)
    def _():
        out_ref[...] = base

    for index, ref in enumerate(pieces):

        @pl.when((plan[0, slot] == index) & (plan[3, slot] == 1))
        def _():
            out_ref[...] = base + (ref[:, pl.ds(column, PW)] - product)


def update(plan, weight, pieces, gathered, base):
    height, width = base.shape
    whole = pl.BlockSpec(memory_space=pltpu.VMEM)
    tile = pl.BlockSpec((height, PW), lambda u, plan: (0, u))
    return pl.pallas_call(
        update_kernel,
        out_shape=jax.ShapeDtypeStruct(base.shape, jnp.float32),
        grid_spec=pltpu.PrefetchScalarGridSpec(
            num_scalar_prefetch=1,
            grid=(width // PW,),
            in_specs=[whole] * 9 + [tile],
            out_specs=tile,
            scratch_shapes=[pltpu.VMEM((PW, LEAD), jnp.float32)],
        ),
        compiler_params=pltpu.CompilerParams(vmem_limit_bytes=16 << 20),
        name="update",
    )(plan, weight, *pieces, *gathered, base)


def doubling_steps():
    every = []
    for step in range(4):
        flip = 1 if step % 2 == 0 else 3
        pairs = []
        for z in range(4):
            for x in range(4):
                for core in range(2):
                    to = (z, x ^ flip) if step // 2 == core else (z ^ flip, x)
                    pairs.append(((z * 4 + x) * 2 + core, (to[0] * 4 + to[1]) * 2 + core))
        every.append(pairs)
    return every, [pair for pair in every[0] if pair[0] < 2]


def shards(front, ancestor, tile_map):
    height = front.shape[0]
    swap = [(i, i ^ 1) for i in range(32)]
    part = (2, 32, LEAD)
    lead = front[:, :LEAD]

    ring = [[(i, (i + hop) % 4) for i in range(4)] for hop in range(4)]

    blocks = [local_call(corner_kernel, "corner", [(BLOCK, LEAD)])(lead)[0]]
    for to in range(1, 4):
        blocks.append(lax.ppermute(blocks[0], ("row", "col"), [(4 * core, 4 * core + to) for core in range(2)]))

    mate = lax.ppermute(lead, "row", swap)
    parts = list(local_call(share_kernel, "share", [part] * 4)(lead, mate))
    for hop in range(1, 4):
        pairs = [(i, i // 8 * 8 + (i + 2 * hop) % 8) for i in range(2, 32)]
        parts[hop] = lax.ppermute(parts[hop], "row", pairs)
    parts = list(local_call(sort_kernel, "sort", [part] * 4, 1)(tile_map, *parts))
    blocks, parts = lax.optimization_barrier((blocks, parts))

    every, spread = doubling_steps()
    for to in range(1, 4):
        parts[to] = lax.ppermute(parts[to], "col", [(0, to)])
    block = (blocks[0] + blocks[1]) + (blocks[2] + blocks[3])
    got = lax.ppermute(block, "row", spread)
    block, got, parts = lax.optimization_barrier((block, got, parts))
    load = local_call(merge_kernel, "merge", [(64 + BLOCK + PAD, LEAD)])(*parts, block, got)[0]

    *pieces, plan = local_call(pick_kernel, "pick", [(height, 2 * PW)] * 4, 1, [(4, 8)])(tile_map, front)

    load, lead = lax.optimization_barrier((load, lead))
    near = lax.ppermute(lead, "col", [(0, 1)])
    load = local_call(partial(join_kernel, 64), "join", [(128 + BLOCK, LEAD)])(load, lax.ppermute(load, "row", every[1]))[0]
    load, near, *pieces = lax.optimization_barrier((load, near, *pieces))
    hold = jnp.where(lax.axis_index("col") == 1, near, lead)
    onward = [(0, 3), (1, 2)]
    far = [lax.ppermute(hold[:, :PW], "col", onward), hold[:, PW:]]
    load = local_call(partial(join_kernel, 128), "join", [(256 + BLOCK, LEAD)])(load, lax.ppermute(load, "row", every[2]))[0]
    load, far, *pieces = lax.optimization_barrier((load, far, *pieces))
    far[1] = lax.ppermute(far[1], "col", onward)
    gathered, block = local_call(partial(join_kernel, 256), "join", [(512, LEAD), (BLOCK, LEAD)])(
        load, lax.ppermute(load, "row", every[3])
    )
    for hop in (1, 3):
        pieces[hop] = lax.ppermute(pieces[hop], "col", ring[hop])
    block, gathered, *pieces = lax.optimization_barrier((block, gathered, *pieces))
    other = lax.ppermute(block, "row", swap)
    late = lax.ppermute(gathered, "row", every[0])
    pieces[2] = lax.ppermute(pieces[2], "col", ring[2])
    other_gathered = lax.ppermute(gathered, "row", swap)

    inverse = factor(block, other)
    late, other_gathered, inverse, pieces = lax.optimization_barrier((late, other_gathered, inverse, pieces))
    other_late = lax.ppermute(late, "row", swap)
    panel, weight = weigh([lead, near, *far], inverse)
    updated = update(plan, weight, pieces, [gathered, late, other_gathered, other_late], ancestor)
    return panel, updated


def solution(mesh):
    return jax.shard_map(
        shards,
        mesh=mesh,
        in_specs=(P("row", "col"), P("row", "col"), P()),
        out_specs=(P("row", None), P("row", "col")),
        check_vma=False,
    )
```
